32 devices in a mesh: seq: 4 (over y, x), fsdp: 8 (over z, core).
Axes of the slice: x: 2, y: 2, z: 4, core: 2. Of those that a mesh axis runs over, the one named last changes fastest.
Arguments:
- tokens: bfloat16 [16, 1024, 1536], P('fsdp', 'seq'), may hold values from -6 to 6
- joined_input_weight: bfloat16 [1536, 3072], P('fsdp'), may hold values from -0.15625 to 0.15625
- out_projection: bfloat16 [1536, 1536], P('fsdp'), may hold values from -1.25 to 1.25
- gate_weight: bfloat16 [1536, 4096], P('fsdp'), may hold values from -0.15625 to 0.15625
- up_weight: bfloat16 [1536, 4096], P('fsdp'), may hold values from -0.15625 to 0.15625
- down_weight: bfloat16 [4096, 1536], P('fsdp'), may hold values from -0.09375 to 0.09375
- norm_first: float32 [1536], replicated, may hold values from 0.25 to 1.75
- norm_second: float32 [1536], replicated, may hold values from 0.25 to 1.75
- positions: int32 [16, 1024], P('fsdp'), may hold values from 0 to 767, as said below
- cotangent: bfloat16 [16, 1024, 1536], P('fsdp', 'seq'), may hold values from -6 to 6
Outputs:
- block_out: bfloat16 [16, 1024, 1536], P('fsdp', 'seq')
- tokens_grad: bfloat16 [16, 1024, 1536], P('fsdp', 'seq')
- in_projection_grad: float32 [1536, 3072], P('fsdp')
- out_projection_grad: float32 [1536, 1536], P('fsdp')
- gate_grad: float32 [1536, 4096], P('fsdp')
- up_grad: float32 [1536, 4096], P('fsdp')
- down_grad: float32 [4096, 1536], P('fsdp')
- norm_first_grad: float32 [1536], replicated
- norm_second_grad: float32 [1536], replicated
The draws below stay inside these ranges and needn't reach their ends.
Inputs may be any that keep to these rules, and one draw needn't show every extreme that they name: `positions`: in every sequence row 0 has position 0, and each later row has the position of the row before plus one, or 0 where a new document starts; every sequence holds three documents, the middle one of exactly 768 rows, the others shorter than 256 rows.
All inputs are finite; a program needn't handle non-finite values.
Results may differ from the reference program's by a relative error of at most 0.02.
Values may be sent and summed in bfloat16 or wider, within the bound.
No kernel may reach another device: no remote copies, remote signals or barrier semaphores. Data moves between devices by JAX's collectives and lax.ppermute only.
A program may use at most 384 MiB of HBM per device.

```python
import math
import jax
import jax.numpy as jnp
from jax import lax

EMBED_WIDTH = 1536
FF = 4096
QUERY_HEAD_COUNT = 16
KEY_VALUE_HEADS = 8
HEAD_DIMENSION = 96
SEQUENCE_TOKENS = 1024
SEQS = 16
SPAN = 256


def draw_positions(key, part):
    key = jax.random.fold_in(key, 7)
    first_end = jax.random.randint(key, (SEQS, 1), 1, SPAN)
    second_end = first_end + (SEQUENCE_TOKENS - SPAN)
    row_index = jnp.arange(SEQUENCE_TOKENS, dtype=jnp.int32)[None, :]
    doc_first = jnp.where(row_index < first_end, 0, jnp.where(row_index < second_end, first_end, second_end))
    return (row_index - doc_first).astype(jnp.int32)


def shard_levels(rng, extent, cuts, smallest, high):
    level, own = 1.0, jax.random.fold_in(rng, 6)
    for dim, shards_of in cuts:
        draws = jnp.exp(jax.random.uniform(jax.random.fold_in(own, dim), (shards_of,), jnp.float32, smallest / len(cuts), high / len(cuts)))
        level = level * jnp.repeat(draws, extent[dim] // shards_of).reshape([-1 if axis == dim else 1 for axis in range(len(extent))])
    return level


def noise(key, extent, spread, reach, pieces=(), kind=jnp.bfloat16):
    values = spread * jax.random.normal(key, extent, jnp.float32)
    if pieces:
        values = values * shard_levels(key, extent, pieces, -0.22, 0.18)
    return jnp.clip(values, -reach, reach).astype(kind)


def setup_inputs(seed: int = 0) -> dict:
    seeds = jax.random.split(jax.random.key(seed), 11)
    tokens = noise(seeds[0], (SEQS, SEQUENCE_TOKENS, EMBED_WIDTH), 1.0, 6.0, ((0, 8), (1, 4)))
    joined_input_weight = noise(seeds[1], (EMBED_WIDTH, (QUERY_HEAD_COUNT + 2 * KEY_VALUE_HEADS) * HEAD_DIMENSION), EMBED_WIDTH ** -0.5, 0.15625, ((0, 8),))
    out_projection = noise(seeds[2], (QUERY_HEAD_COUNT * HEAD_DIMENSION, EMBED_WIDTH), (QUERY_HEAD_COUNT * HEAD_DIMENSION * 16 // SEQUENCE_TOKENS) ** -0.5, 1.25, ((0, 8),))
    gate_weight = noise(seeds[3], (EMBED_WIDTH, FF), EMBED_WIDTH ** -0.5, 0.15625, ((0, 8),))
    up_weight = noise(seeds[4], (EMBED_WIDTH, FF), EMBED_WIDTH ** -0.5, 0.15625, ((0, 8),))
    down_weight = noise(seeds[5], (FF, EMBED_WIDTH), FF ** -0.5, 0.09375, ((0, 8),))
    norm_first = jnp.clip(1.0 + 0.15 * jax.random.normal(seeds[6], (EMBED_WIDTH,), jnp.float32), 0.25, 1.75)
    norm_second = jnp.clip(1.0 + 0.15 * jax.random.normal(seeds[7], (EMBED_WIDTH,), jnp.float32), 0.25, 1.75)
    positions = draw_positions(jax.random.fold_in(seeds[10], 71), 0)
    cotangent = noise(seeds[9], (SEQS, SEQUENCE_TOKENS, EMBED_WIDTH), 1.0, 6.0, ((0, 8), (1, 4)))
    return dict(tokens=tokens, joined_input_weight=joined_input_weight, out_projection=out_projection, gate_weight=gate_weight, up_weight=up_weight, down_weight=down_weight, norm_first=norm_first, norm_second=norm_second, positions=positions, cotangent=cotangent)


@jax.custom_vjp
def lower_precision(v):
    return lax.optimization_barrier(v.astype(jnp.bfloat16)).astype(jnp.float32)

@jax.custom_vjp
def lower_precision_backward(v):
    return v

def low_keep(v):
    return (lower_precision(v), None)

def low_pass(kept, grad):
    return (grad,)

def back_keep(v):
    return (v, None)

def back_low(kept, grad):
    return (lower_precision(grad),)
lower_precision.defvjp(low_keep, low_pass)
lower_precision_backward.defvjp(back_keep, back_low)
epsilon = 1e-05
rope_base = 100000.0
highest = lax.Precision.HIGHEST

def norm_scale(values, gain_row):
    return values * lax.rsqrt(lax.optimization_barrier(jnp.mean(values * values, axis=-1, keepdims=True)) + epsilon) * gain_row

def apply_rotary(values, cosine_lookup, sine_lookup):
    halves = values.shape[-1] // 2
    first_half = values[..., :halves]
    second_half = values[..., halves:]
    return jnp.concatenate([first_half * cosine_lookup - second_half * sine_lookup, second_half * cosine_lookup + first_half * sine_lookup], axis=-1)

def attention(query_rows, input_keys, input_values, positions):
    heads_per_group = query_rows.shape[0]
    sequence_length = query_rows.shape[1]
    grouped_heads = query_rows.reshape(heads_per_group, sequence_length, KEY_VALUE_HEADS, QUERY_HEAD_COUNT // KEY_VALUE_HEADS, HEAD_DIMENSION)
    scores = lower_precision_backward(jnp.einsum('gqkrd,gtkd->gkrqt', grouped_heads, input_keys, precision=highest)) * (1.0 / math.sqrt(HEAD_DIMENSION))
    row_index = jnp.arange(sequence_length, dtype=jnp.int32)
    doc_first = row_index[None, :] - positions
    allowed = (row_index[None, None, :] <= row_index[None, :, None]) & (row_index[None, None, :] >= doc_first[:, :, None])
    scores = jnp.where(allowed[:, None, None], scores, -1e+30)
    row_max = lax.optimization_barrier(jnp.max(scores, axis=-1, keepdims=True))
    raised = jnp.exp(scores - row_max)
    shares = lower_precision(raised / lax.optimization_barrier(jnp.sum(raised, axis=-1, keepdims=True)))
    mixed_heads = jnp.einsum('gkrqt,gtkd->gqkrd', shares, input_values, precision=highest)
    return mixed_heads.reshape(heads_per_group, sequence_length, QUERY_HEAD_COUNT * HEAD_DIMENSION)

def forward(block_in, joined_input_weight, out_projection, gate_weight, up_weight, down_weight, norm_first, norm_second, positions):
    heads_per_group = block_in.shape[0]
    query_columns = QUERY_HEAD_COUNT * HEAD_DIMENSION
    paired_width = KEY_VALUE_HEADS * HEAD_DIMENSION
    normed_in = lower_precision(norm_scale(block_in, norm_first))
    projected_tokens = lower_precision_backward(jnp.einsum('gld,de->gle', normed_in, joined_input_weight, precision=highest))
    frequency = jnp.exp(jnp.arange(HEAD_DIMENSION // 2, dtype=jnp.float32) * (-2.0 * math.log(rope_base) / HEAD_DIMENSION))
    angles = positions.astype(jnp.float32)[..., None] * frequency
    cosine_lookup = jnp.cos(angles)[:, :, None, :]
    sine_lookup = jnp.sin(angles)[:, :, None, :]
    query_rows = lower_precision_backward(lower_precision(apply_rotary(projected_tokens[..., :query_columns].reshape(heads_per_group, SEQUENCE_TOKENS, QUERY_HEAD_COUNT, HEAD_DIMENSION), cosine_lookup, sine_lookup)))
    input_keys = lower_precision_backward(lower_precision(apply_rotary(projected_tokens[..., query_columns:query_columns + paired_width].reshape(heads_per_group, SEQUENCE_TOKENS, KEY_VALUE_HEADS, HEAD_DIMENSION), cosine_lookup, sine_lookup)))
    input_values = lower_precision_backward(lower_precision(projected_tokens[..., query_columns + paired_width:].reshape(heads_per_group, SEQUENCE_TOKENS, KEY_VALUE_HEADS, HEAD_DIMENSION)))
    mixed_rows = lower_precision_backward(lower_precision(attention(query_rows, input_keys, input_values, positions)))
    residual = block_in + lower_precision_backward(jnp.einsum('gle,ed->gld', mixed_rows, out_projection, precision=highest))
    normed_mid = lower_precision(norm_scale(residual, norm_second))
    gate_pre = lower_precision_backward(jnp.einsum('gld,df->glf', normed_mid, gate_weight, precision=highest))
    up_pre = lower_precision_backward(jnp.einsum('gld,df->glf', normed_mid, up_weight, precision=highest))
    hidden = lower_precision(jax.nn.silu(gate_pre) * up_pre)
    return residual + lower_precision_backward(jnp.einsum('glf,fd->gld', hidden, down_weight, precision=highest))

def reference(tokens, joined_input_weight, out_projection, gate_weight, up_weight, down_weight, norm_first, norm_second, positions, cotangent):
    weights = tuple((weight.astype(jnp.float32) for weight in (joined_input_weight, out_projection, gate_weight, up_weight, down_weight, norm_first, norm_second)))
    heads_per_group = math.gcd(SEQS, max(1, 4096 // SEQUENCE_TOKENS))
    group_count = SEQS // heads_per_group
    token_groups = tokens.reshape(group_count, heads_per_group, SEQUENCE_TOKENS, EMBED_WIDTH)
    position_groups = positions.reshape(group_count, heads_per_group, SEQUENCE_TOKENS)
    cotangent_groups = cotangent.reshape(group_count, heads_per_group, SEQUENCE_TOKENS, EMBED_WIDTH)

    def add_group(totals, block_item):
        block_rows, block_pos, block_grad = block_item

        def apply_block(block_in, *weight_list):
            return forward(block_in, *weight_list, block_pos)
        result, pull_back = jax.vjp(apply_block, block_rows.astype(jnp.float32), *weights)
        grad_list = pull_back(block_grad.astype(jnp.float32))
        totals = tuple((running + update for running, update in zip(totals, grad_list[1:])))
        return (totals, (result.astype(jnp.bfloat16), grad_list[0].astype(jnp.bfloat16)))
    zero_totals = tuple((jnp.zeros(weight.shape, jnp.float32) for weight in weights))
    totals, (out_groups, grad_groups) = lax.scan(add_group, zero_totals, (token_groups, position_groups, cotangent_groups))
    return (out_groups.reshape(SEQS, SEQUENCE_TOKENS, EMBED_WIDTH), grad_groups.reshape(SEQS, SEQUENCE_TOKENS, EMBED_WIDTH), totals[0], totals[1], totals[2], totals[3], totals[4], totals[5], totals[6])
```

```python
import functools
import math

import jax
import jax.numpy as jnp
import numpy as np
from jax import lax
from jax.experimental import pallas as pl
from jax.experimental.pallas import tpu as pltpu
from jax.sharding import PartitionSpec as P

FF = 4096
QUERY_HEAD_COUNT = 16
KEY_VALUE_HEADS = 8
HEAD_DIMENSION = 96
HALF = HEAD_DIMENSION // 2
LANES = 128

epsilon = 1e-05
rope_base = 100000.0
SCALING = 1.0 / math.sqrt(HEAD_DIMENSION)
LOG2E = 1.4426950408889634
BF16 = jnp.bfloat16
F32 = jnp.float32
MIB = 1024 * 1024


def dot(a, b, ca, cb):
    return lax.dot_general(a, b, (((ca,), (cb,)), ((), ())), preferred_element_type=F32)


def params(limit):
    return pltpu.CompilerParams(
        vmem_limit_bytes=limit * MIB,
    )


def cost(flops, moved, trans=0):
    return pl.CostEstimate(flops=int(flops), bytes_accessed=int(moved), transcendentals=int(trans))


def pad_matrix(pairs, repeat):
    unit = repeat + 2
    out = np.zeros((pairs * unit * HEAD_DIMENSION, pairs * unit * LANES), np.float32)
    for g in range(pairs):
        for r in range(unit):
            if r < repeat:
                src = (g * repeat + r) * HEAD_DIMENSION
            else:
                src = (pairs * repeat + (r - repeat) * pairs + g) * HEAD_DIMENSION
            dst = (g * unit + r) * LANES
            for j in range(HEAD_DIMENSION):
                lane = j if (r == unit - 1 or j < HALF) else 64 + j - HALF
                out[src + j, dst + lane] = 1.0
    return out


def place_matrix(pairs, repeat):
    out = np.zeros((pairs, repeat * LANES, pairs * repeat * HEAD_DIMENSION), np.float32)
    for g in range(pairs):
        for r in range(repeat):
            for j in range(HEAD_DIMENSION):
                out[g, r * LANES + j, (g * repeat + r) * HEAD_DIMENSION + j] = 1.0
    return out


def in_kernel(unit, x_ref, w_ref, pad_ref, cos_ref, sin_ref, out_ref, wide):
    @pl.when((pl.program_id(0) == 0) & (pl.program_id(1) == 0))
    def _():
        wide[...] = dot(w_ref[...], pad_ref[...], 1, 0).astype(BF16)

    rows = dot(x_ref[...], wide[...], 1, 0)
    cosine, sine = cos_ref[...], sin_ref[...]
    for part in range(rows.shape[1] // LANES):
        piece = rows[:, part * LANES : (part + 1) * LANES]
        if part % unit != unit - 1:
            piece = piece * cosine + pltpu.roll(piece, 64, 1) * sine
        out_ref[:, part * LANES : (part + 1) * LANES] = piece.astype(BF16)


def project_in(normed, w_slice, pad, cosine, sine, unit):
    spans, seqs, span, width = normed.shape
    narrow, wide = pad.shape
    rows = spans * seqs * span
    return pl.pallas_call(
        functools.partial(in_kernel, unit),
        out_shape=jax.ShapeDtypeStruct((spans, seqs, span, wide), BF16),
        grid=(spans, seqs),
        in_specs=[
            pl.BlockSpec((None, None, span, width), lambda i, j: (i, j, 0, 0)),
            pl.BlockSpec((width, narrow), lambda i, j: (0, 0)),
            pl.BlockSpec((narrow, wide), lambda i, j: (0, 0)),
            pl.BlockSpec((None, None, span, LANES), lambda i, j: (i, j, 0, 0)),
            pl.BlockSpec((None, None, span, LANES), lambda i, j: (i, j, 0, 0)),
        ],
        out_specs=pl.BlockSpec((None, None, span, wide), lambda i, j: (i, j, 0, 0)),
        scratch_shapes=[pltpu.VMEM((width, wide), BF16)],
        compiler_params=params(40),
        cost_estimate=cost(2 * rows * width * wide, 2 * rows * (width + wide) + 2 * width * narrow),
        name="project_in",
    )(normed, w_slice, pad, cosine, sine)


def mask_of(scores, first_key, first_row, starts, repeat, diagonal):
    keys = lax.broadcasted_iota(jnp.int32, scores.shape, 0) + first_key
    allowed = keys >= starts
    if diagonal:
        step = scores.shape[1] // repeat
        rows = lax.broadcasted_iota(jnp.int32, scores.shape, 1) % step + first_row
        allowed = allowed & (keys <= rows)
    return jnp.where(allowed, scores, -1e30)


def forward_kernel(step, repeat, proj_ref, start_ref, place_ref, out_ref, lse_ref):
    spans, span, _ = proj_ref.shape
    full = spans * span
    pair = pl.program_id(1)
    key = proj_ref[:, :, repeat * LANES : (repeat + 1) * LANES].reshape(full, LANES)
    value = proj_ref[:, :, (repeat + 1) * LANES :].reshape(full, LANES)
    value_t = value.T
    starts = start_ref[...]
    for block in range(full // step):
        begin, end = block * step, (block + 1) * step
        rows = slice(begin, end)
        query = jnp.concatenate(
            [
                proj_ref[:, :, r * LANES : (r + 1) * LANES].reshape(full, LANES)[rows]
                for r in range(repeat)
            ],
            axis=0,
        )
        starts_now = jnp.concatenate([starts[:, rows]] * repeat, axis=1)
        pieces = []
        for key_block in range(block + 1):
            first = key_block * step
            scores = dot(key[first : first + step], query, 1, 1) * (SCALING * LOG2E)
            pieces.append(
                mask_of(scores, first, begin, starts_now, repeat, key_block == block)
            )
        top = functools.reduce(
            jnp.maximum, [jnp.max(p, axis=0, keepdims=True) for p in pieces]
        )
        total = None
        summed = None
        for key_block in range(block + 1):
            first = key_block * step
            raised = jnp.exp2(pieces[key_block] - top)
            part = jnp.sum(raised, axis=0, keepdims=True)
            mixed = dot(value_t[:, first : first + step], raised.astype(BF16), 1, 0)
            total = part if total is None else total + part
            summed = mixed if summed is None else summed + mixed
        mixed_t = (summed * (1.0 / total)).astype(BF16)
        lse_ref[block : block + 1, :] = top + jnp.log2(total)
        wide = None
        for r in range(repeat):
            term = dot(
                mixed_t[:, r * step : (r + 1) * step],
                place_ref[r * LANES : (r + 1) * LANES, :],
                0,
                0,
            )
            wide = term if wide is None else wide + term
        wide = wide.astype(BF16)
        for piece in range(step // span):
            at = block * (step // span) + piece
            rows_now = wide[piece * span : (piece + 1) * span]

            @pl.when(pair == 0)
            def _():
                out_ref[at] = rows_now

            @pl.when(pair != 0)
            def _():
                out_ref[at] = out_ref[at] + rows_now


def attention_forward(proj, starts, place, repeat, step):
    spans, seqs, span, wide = proj.shape
    pairs, _, narrow = place.shape
    full = spans * span
    group = wide // pairs
    work = seqs * pairs * repeat * full * full
    return pl.pallas_call(
        functools.partial(forward_kernel, step, repeat),
        out_shape=(
            jax.ShapeDtypeStruct((spans, seqs, span, narrow), BF16),
            jax.ShapeDtypeStruct((seqs, pairs, full // step, repeat * step), F32),
        ),
        grid=(seqs, pairs),
        in_specs=[
            pl.BlockSpec((spans, None, span, group), lambda i, j: (0, i, 0, j)),
            pl.BlockSpec((None, 1, full), lambda i, j: (i, 0, 0)),
            pl.BlockSpec((None, repeat * LANES, narrow), lambda i, j: (j, 0, 0)),
        ],
        out_specs=(
            pl.BlockSpec((spans, None, span, narrow), lambda i, j: (0, i, 0, 0)),
            pl.BlockSpec((None, None, full // step, repeat * step), lambda i, j: (i, j, 0, 0)),
        ),
        compiler_params=params(48),
        cost_estimate=cost(2 * work * 256, 2 * proj.size * 2, work),
        name="attention_forward",
    )(proj, starts, place)


def backward_kernel(
    step,
    repeat,
    proj_ref,
    start_ref,
    place_ref,
    grad_ref,
    lse_ref,
    cos_ref,
    sin_ref,
    pad_ref,
    out_ref,
    key_acc,
    value_acc,
):
    spans, span, _ = proj_ref.shape
    full = spans * span
    pair = pl.program_id(1)
    key = proj_ref[:, :, repeat * LANES : (repeat + 1) * LANES].reshape(full, LANES)
    value = proj_ref[:, :, (repeat + 1) * LANES :].reshape(full, LANES)
    key_t = key.T
    starts = start_ref[...]
    cosine = cos_ref[...].reshape(full, LANES)
    sine = sin_ref[...].reshape(full, LANES)
    key_acc[...] = jnp.zeros_like(key_acc)
    value_acc[...] = jnp.zeros_like(value_acc)

    def turn_back(grad, rows):
        grad = grad.astype(BF16).astype(F32)
        return (grad * cosine[rows] - pltpu.roll(grad, 64, 1) * sine[rows]).astype(BF16)

    def put(at, rows_now):
        @pl.when(pair == 0)
        def _():
            out_ref[at] = rows_now

        @pl.when(pair != 0)
        def _():
            out_ref[at] = out_ref[at] + rows_now

    for block in range(full // step):
        begin, end = block * step, (block + 1) * step
        rows = slice(begin, end)
        query = jnp.concatenate(
            [
                proj_ref[:, :, r * LANES : (r + 1) * LANES].reshape(full, LANES)[rows]
                for r in range(repeat)
            ],
            axis=0,
        )
        grad_rows = grad_ref[...].reshape(full, grad_ref.shape[2])[rows]
        grad = jnp.concatenate(
            [
                dot(grad_rows, place_ref[r * LANES : (r + 1) * LANES, :], 1, 1).astype(BF16)
                for r in range(repeat)
            ],
            axis=0,
        )
        starts_now = jnp.concatenate([starts[:, rows]] * repeat, axis=1)
        lse = lse_ref[block : block + 1, :]
        kept = []
        mean_dot = None
        for key_block in range(block + 1):
            first = key_block * step
            keys = slice(first, first + step)
            scores = dot(key[keys], query, 1, 1) * (SCALING * LOG2E)
            scores = mask_of(scores, first, begin, starts_now, repeat, key_block == block)
            shares = jnp.exp2(scores - lse)
            value_acc[keys, :] += dot(shares.astype(BF16), grad, 1, 0)
            prob_grad = dot(value[keys], grad, 1, 1)
            product = shares * prob_grad
            part = jnp.sum(product, axis=0, keepdims=True)
            mean_dot = part if mean_dot is None else mean_dot + part
            kept.append((shares, product))
        query_grad_t = None
        for key_block in range(block + 1):
            first = key_block * step
            keys = slice(first, first + step)
            shares, product = kept[key_block]
            score_grad = (SCALING * (product - shares * mean_dot)).astype(BF16)
            key_acc[keys, :] += dot(score_grad, query, 1, 0)
            term = dot(key_t[:, keys], score_grad, 1, 0)
            query_grad_t = term if query_grad_t is None else query_grad_t + term
        query_grad = query_grad_t.T
        wide = None
        for r in range(repeat):
            turned = turn_back(query_grad[r * step : (r + 1) * step], rows)
            term = dot(turned, pad_ref[:, r * LANES : (r + 1) * LANES], 1, 1)
            wide = term if wide is None else wide + term
        wide = wide.astype(BF16)
        for piece in range(step // span):
            put(block * (step // span) + piece, wide[piece * span : (piece + 1) * span])
    for at in range(spans):
        rows = slice(at * span, (at + 1) * span)
        turned = turn_back(key_acc[rows, :], rows)
        wide = dot(turned, pad_ref[:, repeat * LANES : (repeat + 1) * LANES], 1, 1)
        wide += dot(value_acc[rows, :].astype(BF16), pad_ref[:, (repeat + 1) * LANES :], 1, 1)
        out_ref[at] = out_ref[at] + wide.astype(BF16)


def attention_backward(proj, starts, place, grad, lse, cosine, sine, pad, repeat, step):
    spans, seqs, span, wide = proj.shape
    pairs, _, narrow = place.shape
    full = spans * span
    group = wide // pairs
    work = seqs * pairs * repeat * full * full
    return pl.pallas_call(
        functools.partial(backward_kernel, step, repeat),
        out_shape=jax.ShapeDtypeStruct((spans, seqs, span, pad.shape[0]), BF16),
        grid=(seqs, pairs),
        in_specs=[
            pl.BlockSpec((spans, None, span, group), lambda i, j: (0, i, 0, j)),
            pl.BlockSpec((None, 1, full), lambda i, j: (i, 0, 0)),
            pl.BlockSpec((None, repeat * LANES, narrow), lambda i, j: (j, 0, 0)),
            pl.BlockSpec((spans, None, span, narrow), lambda i, j: (0, i, 0, 0)),
            pl.BlockSpec((None, None, full // step, repeat * step), lambda i, j: (i, j, 0, 0)),
            pl.BlockSpec((spans, None, span, LANES), lambda i, j: (0, i, 0, 0)),
            pl.BlockSpec((spans, None, span, LANES), lambda i, j: (0, i, 0, 0)),
            pl.BlockSpec((pad.shape[0], group), lambda i, j: (0, j)),
        ],
        out_specs=pl.BlockSpec((spans, None, span, pad.shape[0]), lambda i, j: (0, i, 0, 0)),
        scratch_shapes=[pltpu.VMEM((full, LANES), F32), pltpu.VMEM((full, LANES), F32)],
        compiler_params=params(56),
        cost_estimate=cost(2 * work * 640, 2 * proj.size * 4, work),
        name="attention_backward",
    )(proj, starts, place, grad, lse, cosine, sine, pad)


def out_kernel(mixed_ref, w_ref, tokens_ref, gain_ref, resid_ref, normed_ref):
    summed = tokens_ref[...].astype(F32)
    depth = mixed_ref.shape[2]
    for at in range(mixed_ref.shape[0]):
        summed += dot(mixed_ref[at], w_ref[at * depth : (at + 1) * depth, :], 1, 0)
    resid_ref[...] = summed
    factor = lax.rsqrt(jnp.mean(summed * summed, axis=-1, keepdims=True) + epsilon)
    normed_ref[...] = (summed * factor * gain_ref[...]).astype(BF16)


def project_out(mixed, w_out, tokens, gain, block):
    spans, rows, depth = mixed.shape
    width = w_out.shape[1]
    return pl.pallas_call(
        out_kernel,
        out_shape=(
            jax.ShapeDtypeStruct((rows, width), F32),
            jax.ShapeDtypeStruct((rows, width), BF16),
        ),
        grid=(rows // block,),
        in_specs=[
            pl.BlockSpec((spans, block, depth), lambda i: (0, i, 0)),
            pl.BlockSpec(w_out.shape, lambda i: (0, 0)),
            pl.BlockSpec((block, width), lambda i: (i, 0)),
            pl.BlockSpec((1, width), lambda i: (0, 0)),
        ],
        out_specs=(
            pl.BlockSpec((block, width), lambda i: (i, 0)),
            pl.BlockSpec((block, width), lambda i: (i, 0)),
        ),
        compiler_params=params(40),
        cost_estimate=cost(2 * rows * width * width, rows * width * 10 + width * width * 2),
        name="project_out",
    )(mixed, w_out, tokens, gain)


def feed_kernel(
    x_ref, c_ref, gate_ref, up_ref, down_ref, out_ref, dx_ref, hid_ref, dgate_ref, dup_ref
):
    x = x_ref[...]
    gate = dot(x, gate_ref[...], 1, 0)
    up = dot(x, up_ref[...], 1, 0)
    sig = jax.nn.sigmoid(gate)
    act = gate * sig
    hidden = (act * up).astype(BF16)
    hid_ref[...] = hidden
    out_ref[...] = dot(hidden, down_ref[...], 1, 0).astype(BF16)
    grad_hidden = dot(c_ref[...], down_ref[...], 1, 1)
    grad_gate = (grad_hidden * up * (sig * (1.0 + gate * (1.0 - sig)))).astype(BF16)
    grad_up = (grad_hidden * act).astype(BF16)
    dgate_ref[...] = grad_gate
    dup_ref[...] = grad_up
    dx_ref[...] = (dot(grad_gate, gate_ref[...], 1, 1) + dot(grad_up, up_ref[...], 1, 1)).astype(
        BF16
    )


def feed_forward(x, c, gate_w, up_w, down_w, block):
    rows, width = x.shape
    inner = gate_w.shape[1]
    one = pl.Buffered(1)
    row_spec = pl.BlockSpec((block, width), lambda i: (i, 0))
    hid_spec = pl.BlockSpec((block, inner), lambda i: (i, 0))
    return pl.pallas_call(
        feed_kernel,
        out_shape=(
            jax.ShapeDtypeStruct((rows, width), BF16),
            jax.ShapeDtypeStruct((rows, width), BF16),
            jax.ShapeDtypeStruct((rows, inner), BF16),
            jax.ShapeDtypeStruct((rows, inner), BF16),
            jax.ShapeDtypeStruct((rows, inner), BF16),
        ),
        grid=(rows // block,),
        in_specs=[
            row_spec,
            row_spec,
            pl.BlockSpec(gate_w.shape, lambda i: (0, 0), pipeline_mode=one),
            pl.BlockSpec(up_w.shape, lambda i: (0, 0), pipeline_mode=one),
            pl.BlockSpec(down_w.shape, lambda i: (0, 0), pipeline_mode=one),
        ],
        out_specs=(row_spec, row_spec, hid_spec, hid_spec, hid_spec),
        compiler_params=params(56),
        cost_estimate=cost(
            12 * rows * width * inner, rows * (8 * width + 6 * inner) + 6 * width * inner
        ),
        name="feed_forward",
    )(x, c, gate_w, up_w, down_w)


def back_kernel(grad_ref, resid_ref, cot_ref, gain_ref, w_ref, resid_grad_ref, branch_ref, mixed_ref):
    rows = resid_ref[...]
    factor = lax.rsqrt(jnp.mean(rows * rows, axis=-1, keepdims=True) + epsilon)
    unit_rows = rows * factor
    scaled = grad_ref[...].astype(F32) * gain_ref[...]
    mean_dot = jnp.mean(scaled * unit_rows, axis=-1, keepdims=True)
    grad = cot_ref[...].astype(F32) + factor * (scaled - unit_rows * mean_dot)
    resid_grad_ref[...] = grad
    branch = grad.astype(BF16)
    branch_ref[...] = branch
    depth = mixed_ref.shape[2]
    for at in range(mixed_ref.shape[0]):
        mixed_ref[at] = dot(branch, w_ref[at * depth : (at + 1) * depth, :], 1, 1).astype(BF16)


def norm_out_back(grad_mid, resid, cot, gain, w_out, spans, block):
    rows, width = resid.shape
    depth = w_out.shape[0] // spans
    row_spec = pl.BlockSpec((block, width), lambda i: (i, 0))
    return pl.pallas_call(
        back_kernel,
        out_shape=(
            jax.ShapeDtypeStruct((rows, width), F32),
            jax.ShapeDtypeStruct((rows, width), BF16),
            jax.ShapeDtypeStruct((spans, rows, depth), BF16),
        ),
        grid=(rows // block,),
        in_specs=[
            row_spec,
            row_spec,
            row_spec,
            pl.BlockSpec((1, width), lambda i: (0, 0)),
            pl.BlockSpec(w_out.shape, lambda i: (0, 0)),
        ],
        out_specs=(row_spec, row_spec, pl.BlockSpec((spans, block, depth), lambda i: (0, i, 0))),
        compiler_params=params(40),
        cost_estimate=cost(2 * rows * width * width, rows * width * 16 + width * width * 2),
        name="norm_out_back",
    )(grad_mid, resid, cot, gain, w_out)


def turning_tables(positions, spans):
    seqs, full = positions.shape
    frequency = jnp.exp(
        jnp.arange(HALF, dtype=F32) * (-2.0 * math.log(rope_base) / HEAD_DIMENSION)
    )
    angles = positions.astype(F32)[:, :, None] * frequency
    cosine, sine = jnp.cos(angles), jnp.sin(angles)
    empty = jnp.zeros((seqs, full, 64 - HALF), F32)

    def spread(first, second):
        table = jnp.concatenate([first, empty, second, empty], axis=-1)
        return table.reshape(seqs, spans, full // spans, LANES).transpose(1, 0, 2, 3)

    return spread(cosine, cosine), spread(-sine, sine)


def after(value, *others):
    return lax.optimization_barrier((value, *others))[0]


def body(
    tokens,
    joined_input_weight,
    out_projection,
    gate_weight,
    up_weight,
    down_weight,
    norm_first,
    norm_second,
    positions,
    cotangent,
):
    seqs, span, width = tokens.shape
    spans = lax.axis_size("seq")
    shards = lax.axis_size("fsdp")
    me = lax.axis_index("seq")
    rows = seqs * span
    full = positions.shape[1]
    pairs = KEY_VALUE_HEADS // spans
    repeat = QUERY_HEAD_COUNT // KEY_VALUE_HEADS
    unit = repeat + 2
    query_columns = QUERY_HEAD_COUNT * HEAD_DIMENSION
    pair_columns = KEY_VALUE_HEADS * HEAD_DIMENSION
    query_slab = query_columns // spans
    pair_slab = pair_columns // spans
    own_rows = joined_input_weight.shape[0]
    piece = FF // (shards * spans)
    step = span
    pad = jnp.asarray(pad_matrix(pairs, repeat), BF16)
    place = jnp.asarray(place_matrix(pairs, repeat), BF16)

    def columns(begin, size):
        return lax.dynamic_slice_in_dim(joined_input_weight, begin + me * size, size, 1)

    in_shard = jnp.concatenate(
        [
            columns(0, query_slab),
            columns(query_columns, pair_slab),
            columns(query_columns + pair_columns, pair_slab),
        ],
        axis=1,
    )

    def inner_columns(weight):
        cut = weight.reshape(own_rows, shards, spans, piece)
        return lax.dynamic_index_in_dim(cut, me, 2, keepdims=False).reshape(
            own_rows, shards * piece
        )

    def gather(shard):
        return lax.all_gather(shard, "fsdp", axis=0, tiled=True)

    w_in = gather(in_shard)
    w_out = gather(out_projection)
    w_gate = gather(inner_columns(gate_weight))
    w_up = gather(inner_columns(up_weight))
    w_down = gather(lax.dynamic_slice_in_dim(down_weight, me * piece, piece, 0))

    inputs = tokens.reshape(rows, width).astype(F32)
    factor_in = lax.rsqrt(jnp.mean(inputs * inputs, axis=-1, keepdims=True) + epsilon)
    unit_in = inputs * factor_in
    normed_in = (unit_in * norm_first).astype(BF16)
    x_in = lax.all_gather(normed_in.reshape(seqs, span, width), "seq", axis=0)
    cosine, sine = turning_tables(positions, spans)
    starts = (jnp.arange(full, dtype=jnp.int32)[None, :] - positions)[:, None, :]

    proj = project_in(x_in, w_in, pad, cosine, sine, unit)
    grad_all = lax.all_gather(after(cotangent, proj), "seq", axis=0).reshape(spans * rows, width)
    mixed, lse = attention_forward(proj, starts, place, repeat, step)
    mixed_rows = lax.all_to_all(
        mixed, "seq", split_axis=0, concat_axis=0, tiled=True
    ).reshape(spans, rows, query_slab)
    resid, normed_mid = project_out(
        mixed_rows, w_out, tokens.reshape(rows, width), norm_second[None, :], min(256, rows)
    )
    x_mid = lax.all_gather(normed_mid, "seq", axis=0).reshape(spans * rows, width)
    down_part, grad_mid_part, hidden, grad_gate, grad_up = feed_forward(
        x_mid, grad_all, w_gate, w_up, w_down, 256
    )

    def scatter(value):
        return lax.psum_scatter(
            value.reshape(spans, rows, width), "seq", scatter_dimension=0, tiled=False
        )

    grad_mid = scatter(grad_mid_part)
    down_sum = scatter(after(down_part, grad_mid))
    block_out = (resid + down_sum.astype(F32)).astype(BF16).reshape(seqs, span, width)

    def product_of(left, right):
        return jnp.einsum("rd,re->de", left, right, preferred_element_type=F32)

    gate_part = product_of(x_mid, grad_gate)
    up_part = product_of(x_mid, grad_up)
    down_grad_part = product_of(hidden, grad_all)
    gain_second = (
        jnp.sum(gate_part * w_gate.astype(F32), axis=1) + jnp.sum(up_part * w_up.astype(F32), axis=1)
    ) / norm_second

    def owned(value):
        return lax.psum_scatter(value.astype(BF16), "fsdp", scatter_dimension=0, tiled=True)

    def inner_whole(value):
        every = lax.all_gather(value, "seq", axis=0).astype(F32)
        return (
            every.reshape(spans, own_rows, shards, piece)
            .transpose(1, 2, 0, 3)
            .reshape(own_rows, FF)
        )

    gate_grad = inner_whole(owned(gate_part))
    up_grad = inner_whole(owned(up_part))
    down_grad = lax.all_gather(owned(down_grad_part), "seq", axis=0, tiled=True).astype(F32)

    grad_resid, grad_branch, grad_mixed = norm_out_back(
        grad_mid,
        resid,
        cotangent.reshape(rows, width),
        norm_second[None, :],
        w_out,
        spans,
        min(256, rows),
    )
    head_grad = lax.all_to_all(
        grad_mixed.reshape(spans, seqs, span, query_slab),
        "seq",
        split_axis=0,
        concat_axis=0,
        tiled=True,
    )
    out_part = jnp.einsum(
        "srd,re->sde", mixed_rows, grad_branch, preferred_element_type=F32
    ).reshape(query_columns, width)
    out_own = lax.psum_scatter(
        out_part.astype(BF16), ("fsdp", "seq"), scatter_dimension=0, tiled=True
    )
    out_grad = lax.all_gather(out_own, "seq", axis=0, tiled=True).astype(F32)

    grad_proj = attention_backward(
        proj, starts, place, head_grad, lse, cosine, sine, pad, repeat, step
    ).reshape(spans * rows, pad.shape[0])
    grad_in_part = jnp.einsum(
        "re,de->rd", grad_proj, w_in, preferred_element_type=F32
    ).astype(BF16)
    grad_in = scatter(grad_in_part).astype(F32)
    in_part = product_of(x_in.reshape(spans * rows, width), grad_proj)
    gain_first = jnp.sum(in_part * w_in.astype(F32), axis=1) / norm_first
    in_every = lax.all_gather(owned(in_part), "seq", axis=0).astype(F32)
    in_grad = jnp.concatenate(
        [
            part.transpose(1, 0, 2).reshape(own_rows, -1)
            for part in (
                in_every[:, :, :query_slab],
                in_every[:, :, query_slab : query_slab + pair_slab],
                in_every[:, :, query_slab + pair_slab :],
            )
        ],
        axis=1,
    )
    scaled = grad_in * norm_first
    mean_dot = jnp.mean(scaled * unit_in, axis=-1, keepdims=True)
    tokens_grad = (
        (grad_resid + factor_in * (scaled - unit_in * mean_dot))
        .astype(BF16)
        .reshape(seqs, span, width)
    )
    gain_totals = lax.psum((gain_first, gain_second), ("seq", "fsdp"))
    return (
        block_out,
        tokens_grad,
        in_grad,
        out_grad,
        gate_grad,
        up_grad,
        down_grad,
        gain_totals[0],
        gain_totals[1],
    )


def solution(mesh):
    return jax.shard_map(
        body,
        mesh=mesh,
        in_specs=(
            P("fsdp", "seq", None),
            P("fsdp", None),
            P("fsdp", None),
            P("fsdp", None),
            P("fsdp", None),
            P("fsdp", None),
            P(),
            P(),
            P("fsdp", None),
            P("fsdp", "seq", None),
        ),
        out_specs=(
            P("fsdp", "seq", None),
            P("fsdp", "seq", None),
            P("fsdp", None),
            P("fsdp", None),
            P("fsdp", None),
            P("fsdp", None),
            P("fsdp", None),
            P(),
            P(),
        ),
        check_vma=False,
    )
```

```python
import functools
import math

import jax
import jax.numpy as jnp
import numpy as np
from jax import lax
from jax.experimental import pallas as pl
from jax.experimental.pallas import tpu as pltpu
from jax.sharding import PartitionSpec as P

FF = 4096
QUERY_HEAD_COUNT = 16
KEY_VALUE_HEADS = 8
HEAD_DIMENSION = 96
HALF = HEAD_DIMENSION // 2
LANES = 128

epsilon = 1e-05
rope_base = 100000.0
SCALING = 1.0 / math.sqrt(HEAD_DIMENSION)
LOG2E = 1.4426950408889634
BF16 = jnp.bfloat16
F32 = jnp.float32
MIB = 1024 * 1024
VMEM_LIMIT = 60
COST_SCALE = 20


def dot(a, b, ca, cb):
    return lax.dot_general(a, b, (((ca,), (cb,)), ((), ())), preferred_element_type=F32)


def params(limit):
    return pltpu.CompilerParams(vmem_limit_bytes=limit * MIB)


def cost(flops, moved, trans=0):
    return pl.CostEstimate(
        flops=int(flops) * COST_SCALE, bytes_accessed=int(moved) * COST_SCALE, transcendentals=0
    )


CHAIN = []


def call(kernel, *, out_shape, in_specs, out_specs, prefetch=0, grid=(1,), scratch=(), cost_estimate=None, name=None, waits=()):
    count = prefetch + len(in_specs)
    waits = (*waits, *CHAIN[-1:])

    def run(*refs):
        kernel(*refs[:count], *refs[count + len(waits) :])

    inner = pl.pallas_call(
        run,
        out_shape=out_shape,
        grid_spec=pltpu.PrefetchScalarGridSpec(
            num_scalar_prefetch=prefetch,
            grid=grid,
            in_specs=[*in_specs, *[pl.BlockSpec(memory_space=pltpu.HBM)] * len(waits)],
            out_specs=out_specs,
            scratch_shapes=list(scratch),
        ),
        compiler_params=params(VMEM_LIMIT),
        cost_estimate=cost_estimate,
        name=name,
    )

    def made(*args):
        out = inner(*args, *waits)
        CHAIN.append(out[-1] if isinstance(out, (list, tuple)) else out)
        return out

    return made


def pin(*values):
    waits = tuple(CHAIN[-1:])
    count = len(values)
    hbm = pl.BlockSpec(memory_space=pltpu.HBM)
    out = pl.pallas_call(
        lambda *refs: None,
        out_shape=[shape(*x.shape, dtype=x.dtype) for x in values],
        in_specs=[hbm] * (count + len(waits)),
        out_specs=[hbm] * count,
        input_output_aliases={at: at for at in range(count)},
        cost_estimate=cost(0, 0),
        name="pin",
    )(*values, *waits)
    CHAIN.append(out[-1])
    return out


def whole(array, **extra):
    return pl.BlockSpec(array.shape, lambda *_: (0,) * len(array.shape), **extra)


def shape(*sizes, dtype=BF16):
    return jax.ShapeDtypeStruct(sizes, dtype)


def pad_matrix(pairs, repeat):
    unit = repeat + 2
    out = np.zeros((pairs * unit * HEAD_DIMENSION, pairs * unit * LANES), np.float32)
    for g in range(pairs):
        for r in range(unit):
            if r < repeat:
                src = (g * repeat + r) * HEAD_DIMENSION
            else:
                src = (pairs * repeat + (r - repeat) * pairs + g) * HEAD_DIMENSION
            dst = (g * unit + r) * LANES
            for j in range(HEAD_DIMENSION):
                lane = j if (r == unit - 1 or j < HALF) else 64 + j - HALF
                out[src + j, dst + lane] = 1.0
    return out


def place_matrix(pairs, repeat):
    out = np.zeros((pairs, repeat * LANES, pairs * repeat * HEAD_DIMENSION), np.float32)
    for g in range(pairs):
        for r in range(repeat):
            for j in range(HEAD_DIMENSION):
                out[g, r * LANES + j, (g * repeat + r) * HEAD_DIMENSION + j] = 1.0
    return out


def order_of(bits):
    owners = [0]
    for bit in bits:
        owners = owners + [at ^ (1 << bit) for at in owners]
    return owners


def swap(value, bit):
    size = lax.axis_size("seq")
    return lax.ppermute(value, "seq", [(i, i ^ (1 << bit)) for i in range(size)])


def exchange(value, other):
    size = lax.axis_size("seq")
    return lax.ppermute(value, "seq", [(i, i ^ other) for i in range(size)])


def shared(heads):
    return [heads[0]] + [exchange(heads[at], at) for at in range(1, len(heads))]


def around(value):
    size = lax.axis_size("fsdp")
    return lax.ppermute(value, "fsdp", [(i, (i + 2) % size) for i in range(size)])


def beside(value):
    size = lax.axis_size("fsdp")
    return lax.ppermute(value, "fsdp", [(i, i ^ 1) for i in range(size)])


def copy_kernel(source_ref, *outs):
    for at, ref in enumerate(outs):
        ref[...] = source_ref[at]


def split_rows(value, waits=()):
    seqs, span, width = value.shape
    out_shape = [shape(span, width)] * seqs
    return call(
        copy_kernel,
        out_shape=out_shape,
        in_specs=[whole(value)],
        out_specs=[whole(x) for x in out_shape],
        cost_estimate=cost(0, 4 * value.size),
        name="split_rows",
        waits=waits,
    )(value)


def stack_kernel(*refs):
    count = len(refs) // 3
    for at in range(count):
        first, second, out = refs[2 * at], refs[2 * at + 1], refs[2 * count + at]
        rows = first.shape[0]
        out[:rows] = first[...]
        out[rows:] = second[...]


def stack_rows(pairs, name, waits=()):
    out_shape = [shape(2 * a.shape[0], a.shape[1]) for a, _ in pairs]
    flat = [x for pair in pairs for x in pair]
    return call(
        stack_kernel,
        out_shape=out_shape,
        in_specs=[whole(x) for x in flat],
        out_specs=[whole(x) for x in out_shape],
        cost_estimate=cost(0, 4 * sum(x.size for x in flat)),
        name=name,
        waits=waits,
    )(*flat)


def gather_start(blocks, orders):
    return [swap(x, bits[0]) for x, bits in zip(blocks, orders)]


def gather_end(blocks, got, orders, name, waits=()):
    held = list(zip(blocks, got))
    for level in range(1, len(orders[0])):
        joined = stack_rows(held, name, waits if level == 1 else ())
        held = [(x, swap(x, bits[level])) for x, bits in zip(joined, orders)]
    return held


def fold_kernel(*refs):
    count = len(refs) // 4
    for at in range(count):
        near, got, keep, send = refs[at], refs[count + at], refs[2 * count + at], refs[3 * count + at]
        total = near[...].astype(F32) + got[...].astype(F32)
        cut = total.shape[0] // 2
        keep[...] = total[:cut]
        send[...] = total[cut:].astype(BF16)


def fold(near, got, waits=()):
    out_shape = [shape(x.shape[0] // 2, x.shape[1], dtype=F32) for x in near]
    out_shape += [shape(x.shape[0] // 2, x.shape[1]) for x in near]
    out = call(
        fold_kernel,
        out_shape=out_shape,
        in_specs=[whole(x) for x in (*near, *got)],
        out_specs=[whole(x) for x in out_shape],
        cost_estimate=cost(0, 5 * sum(x.size for x in near)),
        name="fold",
        waits=waits,
    )(*near, *got)
    return out[: len(near)], out[len(near) :]


def scatter_start(parts, orders):
    return [near for near, _ in parts], [swap(far, bits[-1]) for (_, far), bits in zip(parts, orders)]


def scatter_end(near, got, orders, waits=()):
    for level in range(len(orders[0]) - 2, -1, -1):
        near, sent = fold(near, got, waits)
        got = [swap(x, bits[level]) for x, bits in zip(sent, orders)]
    return list(zip(near, got))


def norm_kernel(tokens_ref, gain_ref, *outs):
    for seq, out in enumerate(outs):
        rows = tokens_ref[seq].astype(F32)
        factor = lax.rsqrt(jnp.mean(rows * rows, axis=-1, keepdims=True) + epsilon)
        out[...] = (rows * factor * gain_ref[...]).astype(BF16)


def norm_rows(tokens, gain):
    seqs, span, width = tokens.shape
    out_shape = [shape(span, width)] * seqs
    return call(
        norm_kernel,
        out_shape=out_shape,
        in_specs=[whole(tokens), whole(gain)],
        out_specs=[whole(x) for x in out_shape],
        cost_estimate=cost(8 * tokens.size, 4 * tokens.size),
        name="norm_rows",
    )(tokens, gain)


def cut_in_kernel(spans, sizes, me_ref, w_ref, out_ref):
    for own in range(spans):

        @pl.when(me_ref[0] == own)
        def _():
            begin, put = 0, 0
            for size in sizes:
                out_ref[:, put : put + size] = w_ref[:, begin + own * size : begin + (own + 1) * size]
                begin, put = begin + spans * size, put + size


def cut_in(me, weight, spans, sizes):
    out_shape = shape(weight.shape[0], sum(sizes))
    return call(
        functools.partial(cut_in_kernel, spans, sizes),
        out_shape=out_shape,
        prefetch=1,
        in_specs=[whole(weight)],
        out_specs=whole(out_shape),
        cost_estimate=cost(0, 4 * weight.size),
        name="cut_in",
    )(me, weight)


def cut_feed_kernel(spans, shards, piece, me_ref, gate_ref, up_ref, down_ref, both_ref, out_ref):
    inner = shards * piece
    for own in range(spans):

        @pl.when(me_ref[0] == own)
        def _():
            for shard in range(shards):
                begin = (shard * spans + own) * piece
                put = shard * piece
                both_ref[:, put : put + piece] = gate_ref[:, begin : begin + piece]
                both_ref[:, inner + put : inner + put + piece] = up_ref[:, begin : begin + piece]
            out_ref[...] = down_ref[own * piece : (own + 1) * piece, :]


def cut_feed(me, gate, up, down, spans, shards, piece, waits):
    out_shape = (shape(gate.shape[0], 2 * shards * piece), shape(piece, down.shape[1]))
    return call(
        functools.partial(cut_feed_kernel, spans, shards, piece),
        out_shape=out_shape,
        prefetch=1,
        in_specs=[whole(x) for x in (gate, up, down)],
        out_specs=[whole(x) for x in out_shape],
        cost_estimate=cost(0, 4 * gate.size),
        name="cut_feed",
        waits=waits,
    )(me, gate, up, down)


def widen_kernel(w_ref, pad_ref, out_ref):
    out_ref[...] = dot(w_ref[...], pad_ref[...], 1, 0).astype(BF16)


def widen(w_slice, pad, waits=()):
    rows, narrow = w_slice.shape
    wide = pad.shape[1]
    out_shape = shape(rows, wide)
    return call(
        widen_kernel,
        out_shape=out_shape,
        in_specs=[whole(w_slice), whole(pad)],
        out_specs=whole(out_shape),
        cost_estimate=cost(2 * rows * narrow * wide, 2 * rows * (narrow + wide)),
        name="widen",
        waits=waits,
    )(w_slice, pad)


class Walk:
    def __init__(self, spans, span, near_first):
        self.cut, self.span, self.near_first = spans // 2, span, near_first

    def first(self, step):
        return jnp.minimum(step, self.cut - 1)

    def second(self, step):
        return jnp.maximum(step - self.cut, 0)

    def near(self, step, *_):
        return (self.first(step) if self.near_first else self.second(step), 0)

    def far(self, step, *_):
        return (self.second(step) if self.near_first else self.first(step), 0)

    def both(self, step, *_):
        return (step if self.near_first else lax.rem(step + self.cut, 2 * self.cut), 0)

    def specs(self, width):
        return [
            pl.BlockSpec((self.span, width), self.near),
            pl.BlockSpec((self.span, width), self.far),
        ]

    def is_near(self):
        early = pl.program_id(0) < self.cut
        return early if self.near_first else jnp.logical_not(early)

    def load(self, near_ref, far_ref):
        return jnp.where(self.is_near(), near_ref[...], far_ref[...])

    def store(self, near_ref, far_ref, value):
        near = self.is_near()

        @pl.when(near)
        def _():
            near_ref[...] = value

        @pl.when(jnp.logical_not(near))
        def _():
            far_ref[...] = value


def owner_at(order, index):
    owner = 0
    for at, value in enumerate(order):
        owner = jnp.where(index == at, value, owner)
    return owner


class Visits:
    def __init__(self, spans, span):
        self.spans, self.span = spans, span
        self.order = sorted(range(spans), key=lambda at: -bin(at).count("1"))

    def index(self, blocks):
        held = [blocks.get(owner) for owner in self.order]
        known = next(x for x in held if x is not None)
        for at, value in enumerate(held):
            known = held[at] = known if value is None else value
        return lambda step, *_: (owner_at(held, step), 0)

    def parts(self, bits):
        order = order_of(bits)
        cut = self.spans // 2
        near = {owner: at for at, owner in enumerate(order[:cut])}
        far = {owner: at for at, owner in enumerate(order[cut:])}
        return near, far

    def specs(self, bits, width):
        return [pl.BlockSpec((self.span, width), self.index(blocks)) for blocks in self.parts(bits)]

    def rows(self, bits, width):
        order = order_of(bits)
        return pl.BlockSpec(
            (self.span, width), self.index({owner: at for at, owner in enumerate(order)})
        )

    def is_near(self, bits):
        near, _ = self.parts(bits)
        flag = jnp.bool_(False)
        for at, owner in enumerate(self.order):
            if owner in near:
                flag = jnp.logical_or(flag, pl.program_id(0) == at)
        return flag

    def load(self, bits, near_ref, far_ref):
        return jnp.where(self.is_near(bits), near_ref[...], far_ref[...])

    def store(self, bits, near_ref, far_ref, value):
        near = self.is_near(bits)

        @pl.when(near)
        def _():
            near_ref[...] = value

        @pl.when(jnp.logical_not(near))
        def _():
            far_ref[...] = value

    def store_halves(self, ways, refs, value):
        columns = value.shape[1] // len(ways)
        for at, bits in enumerate(ways):
            part = value[:, at * columns : (at + 1) * columns]
            self.store(bits, refs[2 * at], refs[2 * at + 1], part)


def in_kernel(walk, unit, me_ref, w_ref, cos_ref, sin_ref, near_ref, far_ref, out_ref):
    rows = dot(walk.load(near_ref, far_ref), w_ref[...], 1, 0)
    cosine, sine = cos_ref[...], sin_ref[...]
    for part in range(rows.shape[1] // LANES):
        lanes = slice(part * LANES, (part + 1) * LANES)
        piece = rows[:, lanes]
        if part % unit != unit - 1:
            piece = piece * cosine + pltpu.roll(piece, 64, 1) * sine
        out_ref[:, lanes] = piece.astype(BF16)


def project_in(me, rows, bits, w_wide, cosine, sine, unit, waits=()):
    width, wide = w_wide.shape
    order = order_of(bits)
    spans = len(order)
    full = cosine.shape[0]
    span = full // spans
    walk = Walk(spans, span, True)

    def ordered(step, me_ref):
        return (jnp.bitwise_xor(me_ref[0], owner_at(order, step)), 0)

    return call(
        functools.partial(in_kernel, walk, unit),
        out_shape=shape(full, wide),
        prefetch=1,
        grid=(spans,),
        in_specs=[
            whole(w_wide, pipeline_mode=pl.Buffered(1)),
            pl.BlockSpec((span, LANES), ordered),
            pl.BlockSpec((span, LANES), ordered),
            *walk.specs(width),
        ],
        out_specs=pl.BlockSpec((span, wide), ordered),
        cost_estimate=cost(2 * full * width * wide, 2 * full * (width + wide) + 2 * width * wide),
        name="project_in",
        waits=waits,
    )(me, w_wide, cosine, sine, *rows)


def mask_of(scores, first_key, first_row, starts, repeat, diagonal):
    keys = lax.broadcasted_iota(jnp.int32, scores.shape, 0) + first_key
    allowed = keys >= starts
    if diagonal:
        step = scores.shape[1] // repeat
        rows = lax.broadcasted_iota(jnp.int32, scores.shape, 1) % step + first_row
        allowed = allowed & (keys <= rows)
    return jnp.where(allowed, scores, -1e30)


def query_of(proj_ref, rows, repeat):
    return jnp.concatenate(
        [proj_ref[rows, r * LANES : (r + 1) * LANES] for r in range(repeat)], axis=0
    )


def forward_kernel(spans, step, repeat, me_ref, proj_ref, start_ref, place_ref, *rest):
    outs, lse_ref, held = rest[:spans], rest[spans], rest[spans + 1]
    full = proj_ref.shape[0]
    span = full // spans
    pair = pl.program_id(0)
    me = me_ref[0]
    value_t = proj_ref[:, (repeat + 1) * LANES :].T
    starts = start_ref[...]

    @pl.when(pair == 0)
    def _():
        held[...] = jnp.zeros_like(held)

    for block in range(full // step):
        begin, end = block * step, (block + 1) * step
        rows = slice(begin, end)
        query = query_of(proj_ref, rows, repeat)
        starts_now = jnp.concatenate([starts[:, rows]] * repeat, axis=1)
        pieces = []
        for key_block in range(block + 1):
            first = key_block * step
            key = proj_ref[first : first + step, repeat * LANES : (repeat + 1) * LANES]
            scores = dot(key, query, 1, 1) * (SCALING * LOG2E)
            pieces.append(mask_of(scores, first, begin, starts_now, repeat, key_block == block))
        top = functools.reduce(jnp.maximum, [jnp.max(p, axis=0, keepdims=True) for p in pieces])
        total = None
        summed = None
        for key_block in range(block + 1):
            first = key_block * step
            raised = jnp.exp2(pieces[key_block] - top)
            part = jnp.sum(raised, axis=0, keepdims=True)
            mixed = dot(value_t[:, first : first + step], raised.astype(BF16), 1, 0)
            total = part if total is None else total + part
            summed = mixed if summed is None else summed + mixed
        mixed_t = (summed * (1.0 / total)).astype(BF16)
        lse_ref[block : block + 1, :] = top + jnp.log2(total)
        wide = None
        for r in range(repeat):
            term = dot(
                mixed_t[:, r * step : (r + 1) * step],
                place_ref[r * LANES : (r + 1) * LANES, :],
                0,
                0,
            )
            wide = term if wide is None else wide + term
        wide = wide.astype(BF16)
        for piece in range(step // span):
            at = jnp.bitwise_xor(me, block * (step // span) + piece)
            held[at] = held[at] + wide[piece * span : (piece + 1) * span]

    @pl.when(pair == pl.num_programs(0) - 1)
    def _():
        for at in range(spans):
            outs[at][...] = held[at]


def attention_forward(me, proj, starts, place, spans, repeat, step, waits=()):
    full, wide = proj.shape
    pairs, _, narrow = place.shape
    group = wide // pairs
    span = full // spans
    work = pairs * repeat * full * full
    out_shape = [jax.ShapeDtypeStruct((span, narrow), BF16)] * spans
    out_shape.append(jax.ShapeDtypeStruct((pairs, full // step, repeat * step), F32))
    *mixed, lse = call(
        functools.partial(forward_kernel, spans, step, repeat),
        out_shape=out_shape,
        prefetch=1,
        grid=(pairs,),
        in_specs=[
            pl.BlockSpec((full, group), lambda j, _: (0, j)),
            pl.BlockSpec((1, full), lambda j, _: (0, 0)),
            pl.BlockSpec((None, repeat * LANES, narrow), lambda j, _: (j, 0, 0)),
        ],
        out_specs=[whole(x) for x in out_shape[:-1]]
        + [pl.BlockSpec((None, full // step, repeat * step), lambda j, _: (j, 0, 0))],
        scratch=[pltpu.VMEM((spans, span, narrow), BF16)],
        cost_estimate=cost(2 * work * 256, 2 * proj.size * 2, work),
        name="attention_forward",
        waits=waits,
    )(me, proj, starts, place)
    return mixed, lse


def backward_kernel(
    order, step, repeat, me_ref, proj_ref, start_ref, place_ref, lse_ref, cos_ref, sin_ref, pad_ref, *rest
):
    spans = len(order)
    grads, (out_ref, key_acc, value_acc, held) = rest[:spans], rest[spans:]
    full = proj_ref.shape[0]
    span = full // spans
    pair = pl.program_id(0)
    me = me_ref[0]
    key_t = proj_ref[:, repeat * LANES : (repeat + 1) * LANES].T
    starts = start_ref[...]
    key_acc[...] = jnp.zeros_like(key_acc)
    value_acc[...] = jnp.zeros_like(value_acc)

    @pl.when(pair == 0)
    def _():
        for at in range(spans):
            held[jnp.bitwise_xor(me, at)] = grads[at][...]
        out_ref[...] = jnp.zeros_like(out_ref)

    def turn_back(grad, rows):
        grad = grad.astype(BF16).astype(F32)
        return (grad * cos_ref[rows, :] - pltpu.roll(grad, 64, 1) * sin_ref[rows, :]).astype(BF16)

    def put(begin, wide):
        for at in range(0, wide.shape[0], span):
            owner = jnp.bitwise_xor(me, (begin + at) // span)
            where = 0
            for index, value in enumerate(order):
                where = jnp.where(owner == value, index, where)
            here = pl.ds(pl.multiple_of(where * span, span), span)
            out_ref[here, :] = out_ref[here, :] + wide[at : at + span]

    for block in range(full // step):
        begin, end = block * step, (block + 1) * step
        rows = slice(begin, end)
        query = query_of(proj_ref, rows, repeat)
        grad_rows = jnp.concatenate(
            [held[at] for at in range(begin // span, end // span)], axis=0
        )
        grad = jnp.concatenate(
            [
                dot(grad_rows, place_ref[r * LANES : (r + 1) * LANES, :], 1, 1).astype(BF16)
                for r in range(repeat)
            ],
            axis=0,
        )
        starts_now = jnp.concatenate([starts[:, rows]] * repeat, axis=1)
        lse = lse_ref[block : block + 1, :]
        kept = []
        mean_dot = None
        for key_block in range(block + 1):
            first = key_block * step
            keys = slice(first, first + step)
            key = proj_ref[keys, repeat * LANES : (repeat + 1) * LANES]
            value = proj_ref[keys, (repeat + 1) * LANES :]
            scores = dot(key, query, 1, 1) * (SCALING * LOG2E)
            scores = mask_of(scores, first, begin, starts_now, repeat, key_block == block)
            shares = jnp.exp2(scores - lse)
            value_acc[keys, :] += dot(shares.astype(BF16), grad, 1, 0)
            product = shares * dot(value, grad, 1, 1)
            part = jnp.sum(product, axis=0, keepdims=True)
            mean_dot = part if mean_dot is None else mean_dot + part
            kept.append((shares, product))
        query_grad_t = None
        for key_block in range(block + 1):
            first = key_block * step
            keys = slice(first, first + step)
            shares, product = kept[key_block]
            score_grad = (SCALING * (product - shares * mean_dot)).astype(BF16)
            key_acc[keys, :] += dot(score_grad, query, 1, 0)
            term = dot(key_t[:, keys], score_grad, 1, 0)
            query_grad_t = term if query_grad_t is None else query_grad_t + term
        query_grad = query_grad_t.T
        wide = None
        for r in range(repeat):
            turned = turn_back(query_grad[r * step : (r + 1) * step], rows)
            term = dot(turned, pad_ref[:, r * LANES : (r + 1) * LANES], 1, 1)
            wide = term if wide is None else wide + term
        put(begin, wide.astype(BF16))
    for block in range(full // step):
        rows = slice(block * step, (block + 1) * step)
        turned = turn_back(key_acc[rows, :], rows)
        wide = dot(turned, pad_ref[:, repeat * LANES : (repeat + 1) * LANES], 1, 1)
        wide += dot(value_acc[rows, :].astype(BF16), pad_ref[:, (repeat + 1) * LANES :], 1, 1)
        put(block * step, wide.astype(BF16))


def attention_backward(
    me, proj, starts, place, grads, bits, lse, cosine, sine, pad, repeat, step, waits=()):
    full, wide = proj.shape
    pairs, _, narrow = place.shape
    group = wide // pairs
    work = pairs * repeat * full * full
    out_shape = shape(full, pad.shape[0])
    return call(
        functools.partial(backward_kernel, order_of(bits), step, repeat),
        out_shape=out_shape,
        prefetch=1,
        grid=(pairs,),
        in_specs=[
            pl.BlockSpec((full, group), lambda j, _: (0, j)),
            pl.BlockSpec((1, full), lambda j, _: (0, 0)),
            pl.BlockSpec((None, repeat * LANES, narrow), lambda j, _: (j, 0, 0)),
            pl.BlockSpec((None, full // step, repeat * step), lambda j, _: (j, 0, 0)),
            whole(cosine),
            whole(sine),
            pl.BlockSpec((pad.shape[0], group), lambda j, _: (0, j)),
            *[whole(x) for x in grads],
        ],
        out_specs=whole(out_shape),
        scratch=[
            pltpu.VMEM((full, LANES), F32),
            pltpu.VMEM((full, LANES), F32),
            pltpu.VMEM((len(grads), full // len(grads), narrow), BF16),
        ],
        cost_estimate=cost(2 * work * 640, 2 * proj.size * 4, work),
        name="attention_backward",
        waits=waits,
    )(me, proj, starts, place, lse, cosine, sine, pad, *grads)


def out_kernel(spans, me_ref, w_ref, tokens_ref, gain_ref, *rest):
    mixed, (resid_ref, *parts) = rest[:spans], rest[spans:]
    summed = tokens_ref[...].astype(F32)
    for at in range(spans):
        summed += dot(mixed[at][...], w_ref[jnp.bitwise_xor(me_ref[0], at)], 1, 0)
    resid_ref[...] = summed
    factor = lax.rsqrt(jnp.mean(summed * summed, axis=-1, keepdims=True) + epsilon)
    normed = (summed * factor * gain_ref[...]).astype(BF16)
    columns = parts[0].shape[1]
    for at, part in enumerate(parts):
        part[...] = normed[:, at * columns : (at + 1) * columns]


def project_out(seq, me, mixed, w_out, tokens, gain, ways, waits=()):
    _, span, width = tokens.shape
    out_shape = [shape(span, width, dtype=F32)] + [shape(span, width // len(ways))] * len(ways)
    return call(
        functools.partial(out_kernel, len(mixed)),
        out_shape=out_shape,
        prefetch=1,
        in_specs=[
            whole(w_out),
            pl.BlockSpec((None, span, width), lambda *_: (seq, 0, 0)),
            whole(gain),
            *[whole(x) for x in mixed],
        ],
        out_specs=[whole(x) for x in out_shape],
        cost_estimate=cost(2 * span * width * width, span * width * 10 + width * width * 2),
        name="project_out",
        waits=waits,
    )(me, w_out, tokens, gain, *mixed)


def assemble(held, core, near_ref, far_ref):
    for chip in range(near_ref.shape[0]):
        held[2 * chip + core] = near_ref[chip]
        held[2 * chip + 1 - core] = far_ref[chip]


def feed_kernel(
    visits, bits, ways, shard_ref, both_ref, near_ref, far_ref, cn_ref, cf_ref, *rest
):
    count = 2 * len(ways)
    rows, (hid_ref, dboth_ref, x_ref, *outs), held = rest[:count], rest[count:-1], rest[-1]
    inner = both_ref.shape[1] // 2

    @pl.when(pl.program_id(0) == 0)
    def _():
        assemble(held, shard_ref[0] % 2, near_ref, far_ref)

    down = held[...].reshape(inner, held.shape[2])
    columns = rows[0].shape[1]
    for at, way in enumerate(ways):
        x_ref[:, at * columns : (at + 1) * columns] = visits.load(way, rows[2 * at], rows[2 * at + 1])
    x = x_ref[...]
    gate = dot(x, both_ref[:, :inner], 1, 0)
    up = dot(x, both_ref[:, inner:], 1, 0)
    sig = jax.nn.sigmoid(gate)
    act = gate * sig
    hid_ref[...] = (act * up).astype(BF16)
    grad_hidden = dot(visits.load(bits, cn_ref, cf_ref), down, 1, 1)
    dboth_ref[:, :inner] = (grad_hidden * up * (sig * (1.0 + gate * (1.0 - sig)))).astype(BF16)
    dboth_ref[:, inner:] = (grad_hidden * act).astype(BF16)
    visits.store_halves(ways, outs, dot(dboth_ref[...], both_ref[...], 1, 1).astype(BF16))


def pairs_of(values):
    return list(zip(values[::2], values[1::2]))


def feed_forward(spans, me_shard, rows, cots, bits, ways, both_w, near, far, waits=()):
    width, inner = both_w.shape[0], both_w.shape[1] // 2
    half = cots[0].shape[0]
    span = 2 * half // spans
    visits = Visits(spans, span)
    one = pl.Buffered(1)
    total = 2 * half
    part = width // len(ways)
    flat = [x for pair in rows for x in pair]
    hidden, grads, x_all, *parts = call(
        functools.partial(feed_kernel, visits, bits, ways),
        out_shape=[shape(total, inner), shape(total, 2 * inner), shape(total, width)]
        + [shape(half, part)] * 2 * len(ways),
        prefetch=1,
        grid=(spans,),
        in_specs=[
            whole(both_w, pipeline_mode=one),
            whole(near, pipeline_mode=one),
            whole(far, pipeline_mode=one),
            *visits.specs(bits, width),
            *[spec for way in ways for spec in visits.specs(way, part)],
        ],
        out_specs=[
            visits.rows(bits, inner),
            visits.rows(bits, 2 * inner),
            visits.rows(bits, width),
            *[spec for way in ways for spec in visits.specs(way, part)],
        ],
        scratch=[pltpu.VMEM((2 * near.shape[0], *near.shape[1:]), BF16)],
        cost_estimate=cost(
            10 * total * width * inner, total * (6 * width + 6 * inner) + 6 * width * inner
        ),
        name="feed_forward",
        waits=waits,
    )(me_shard, both_w, near, far, *cots, *flat)
    return pairs_of(parts), hidden, grads, x_all


def feed_out_kernel(count, walk, shard_ref, near_ref, far_ref, *rest):
    hidden, outs, held = rest[:count], rest[count:-1], rest[-1]

    @pl.when(pl.program_id(0) == 0)
    def _():
        assemble(held, shard_ref[0] % 2, near_ref, far_ref)

    down = held[...].reshape(-1, held.shape[2])
    for at in range(count):
        walk.store(outs[2 * at], outs[2 * at + 1], dot(hidden[at][...], down, 1, 0).astype(BF16))


def feed_out(spans, me_shard, hidden, near, far, waits=()):
    total, inner = hidden[0].shape
    width = near.shape[2]
    walk = Walk(spans, total // spans, False)
    count = len(hidden)
    return pairs_of(
        call(
            functools.partial(feed_out_kernel, count, walk),
            out_shape=[shape(total // 2, width)] * 2 * count,
            prefetch=1,
            grid=(spans,),
            in_specs=[
                whole(near, pipeline_mode=pl.Buffered(1)),
                whole(far, pipeline_mode=pl.Buffered(1)),
                *[pl.BlockSpec((total // spans, inner), walk.both)] * count,
            ],
            out_specs=walk.specs(width) * count,
            scratch=[pltpu.VMEM((2 * near.shape[0], *near.shape[1:]), BF16)],
            cost_estimate=cost(
                2 * count * total * inner * width,
                2 * count * total * (inner + width) + 2 * inner * width,
            ),
            name="feed_out",
            waits=waits,
        )(me_shard, near, far, *hidden)
    )


def terms_of(*refs):
    sums = [a[...].astype(F32) + b[...].astype(F32) for a, b in zip(refs[::2], refs[1::2])]
    return sums[0] if len(sums) == 1 else jnp.concatenate(sums, axis=1)


def back_kernel(count, me_ref, resid_ref, cot_ref, gain_ref, w_ref, *rest):
    terms, (resid_grad_ref, branch_ref, *mixed) = rest[:count], rest[count:]
    rows = resid_ref[...]
    factor = lax.rsqrt(jnp.mean(rows * rows, axis=-1, keepdims=True) + epsilon)
    unit_rows = rows * factor
    scaled = terms_of(*terms) * gain_ref[...]
    mean_dot = jnp.mean(scaled * unit_rows, axis=-1, keepdims=True)
    grad = cot_ref[...].astype(F32) + factor * (scaled - unit_rows * mean_dot)
    resid_grad_ref[...] = grad
    branch = grad.astype(BF16)
    branch_ref[...] = branch
    for at, out in enumerate(mixed):
        out[...] = dot(branch, w_ref[jnp.bitwise_xor(me_ref[0], at)], 1, 1).astype(BF16)


def norm_out_back(seq, me, spans, parts, resid, cot, gain, w_out, waits=()):
    rows, width = resid.shape
    terms = [x for pair in parts for x in pair]
    out_shape = [shape(rows, width, dtype=F32), shape(rows, width)]
    out_shape += [shape(rows, w_out.shape[1])] * spans
    out = call(
        functools.partial(back_kernel, len(terms)),
        out_shape=out_shape,
        prefetch=1,
        in_specs=[whole(resid), pl.BlockSpec((None, rows, width), lambda *_: (seq, 0, 0))]
        + [whole(x) for x in (gain, w_out, *terms)],
        out_specs=[whole(x) for x in out_shape],
        cost_estimate=cost(2 * rows * width * width, rows * width * 16 + width * width * 2),
        name="norm_out_back",
        waits=waits,
    )(me, resid, cot, gain, w_out, *terms)
    return out[0], out[1], out[2:]


def grad_in_kernel(visits, ways, proj_ref, w_ref, *outs):
    visits.store_halves(ways, outs, dot(proj_ref[...], w_ref[...], 1, 1).astype(BF16))


def grad_into_rows(spans, proj_grad, bits, ways, w_in, waits=()):
    full, narrow = proj_grad.shape
    width = w_in.shape[0]
    visits = Visits(spans, full // spans)
    part = width // len(ways)
    parts = call(
        functools.partial(grad_in_kernel, visits, ways),
        out_shape=[shape(full // 2, part)] * 2 * len(ways),
        grid=(spans,),
        in_specs=[visits.rows(bits, narrow), whole(w_in, pipeline_mode=pl.Buffered(1))],
        out_specs=[spec for way in ways for spec in visits.specs(way, part)],
        cost_estimate=cost(2 * full * narrow * width, 2 * full * (narrow + width) + 2 * narrow * width),
        name="grad_into_rows",
        waits=waits,
    )(proj_grad, w_in)
    return pairs_of(parts)


def product_of(lefts, rights):
    total = None
    i = j = a = b = 0
    while i < len(lefts):
        size = min(lefts[i].shape[0] - a, rights[j].shape[0] - b)
        term = dot(lefts[i][a : a + size, :], rights[j][b : b + size, :], 0, 0)
        total = term if total is None else total + term
        a, b = a + size, b + size
        if a == lefts[i].shape[0]:
            i, a = i + 1, 0
        if b == rights[j].shape[0]:
            j, b = j + 1, 0
    return total


def weight_kernel(left_count, right_count, gain, *refs):
    lefts, rights = refs[:left_count], refs[left_count : left_count + right_count]
    rest = refs[left_count + right_count :]
    total = product_of(lefts, rights)
    if gain:
        w_ref, out_ref, gain_ref = rest
        gain_ref[...] = jnp.sum(total * w_ref[...].astype(F32), axis=1, keepdims=True)
    else:
        (out_ref,) = rest
    out_ref[...] = total.astype(BF16)


def weight_grad(lefts, rights, weight, name, waits=()):
    rows = lefts[0].shape[1]
    tile = 256
    columns = rights[0].shape[1]
    depth = sum(x.shape[0] for x in lefts)
    out_shape = [shape(rows, columns)]
    out_specs = [pl.BlockSpec((tile, columns), lambda i: (i, 0))]
    weights = () if weight is None else (weight,)
    if weights:
        out_shape.append(shape(rows, 1, dtype=F32))
        out_specs.append(pl.BlockSpec((tile, 1), lambda i: (i, 0)))
    return call(
        functools.partial(weight_kernel, len(lefts), len(rights), bool(weights)),
        out_shape=out_shape,
        grid=(rows // tile,),
        in_specs=[pl.BlockSpec((x.shape[0], tile), lambda i: (0, i)) for x in lefts]
        + [whole(x, pipeline_mode=pl.Buffered(1)) for x in rights]
        + [pl.BlockSpec((tile, x.shape[1]), lambda i: (i, 0)) for x in weights],
        out_specs=out_specs,
        cost_estimate=cost(
            2 * depth * rows * columns, 2 * depth * (rows + columns) + 2 * rows * columns
        ),
        name=name,
        waits=waits,
    )(*lefts, *rights, *weights)


def in_weight_kernel(own, shards, left_count, me_ref, *refs):
    lefts, (*rights, w_ref, near_ref, far_ref, gain_ref) = refs[:left_count], refs[left_count:]
    total = product_of(lefts, rights)
    gain_ref[...] = jnp.sum(total * w_ref[...].astype(F32), axis=1, keepdims=True)
    total = total.astype(BF16)
    steps = shards.bit_length() - 1
    count = total.shape[0] // own
    for at in range(count):
        apart = jnp.bitwise_xor(me_ref[0], pl.program_id(0) * count + at)
        where = 0
        for bit in range(steps):
            where = where * 2 + (apart >> bit) % 2
        piece = total[at * own : (at + 1) * own]

        @pl.when(where < shards // 2)
        def _():
            near_ref[where] = piece

        @pl.when(where >= shards // 2)
        def _():
            far_ref[where - shards // 2] = piece


def in_weight_grad(me, lefts, rights, weight, own, shards, waits=()):
    rows, columns = weight.shape
    tile = math.lcm(own, LANES)
    depth = sum(x.shape[0] for x in lefts)
    half = shape(shards // 2, own, columns)
    out_shape = (half, half, shape(rows, 1, dtype=F32))
    return call(
        functools.partial(in_weight_kernel, own, shards, len(lefts)),
        out_shape=out_shape,
        prefetch=1,
        grid=(rows // tile,),
        in_specs=[pl.BlockSpec((x.shape[0], tile), lambda i, _: (0, i)) for x in lefts]
        + [whole(x) for x in rights]
        + [pl.BlockSpec((tile, columns), lambda i, _: (i, 0))],
        out_specs=[whole(half), whole(half), pl.BlockSpec((tile, 1), lambda i, _: (i, 0))],
        cost_estimate=cost(
            2 * depth * rows * columns, 2 * depth * (rows + columns) + 2 * rows * columns
        ),
        name="in_weight_grad",
        waits=waits,
    )(me, *lefts, *rights, weight)


def add_pairs(left, right):
    return (left.astype(F32) + right.astype(F32)).astype(BF16)


def halve_kernel(near_ref, got_ref, *outs):
    total = (near_ref[...].astype(F32) + got_ref[...].astype(F32)).astype(BF16)
    cut = total.shape[0] // len(outs)
    for at, out in enumerate(outs):
        out[...] = total[at * cut : (at + 1) * cut]


def halve(near, got):
    parts = 2 if near.shape[0] > 1 else 1
    out_shape = [shape(near.shape[0] // parts, *near.shape[1:])] * parts
    return call(
        halve_kernel,
        out_shape=out_shape,
        in_specs=[whole(near), whole(got)],
        out_specs=[whole(x) for x in out_shape],
        cost_estimate=cost(0, 6 * near.size),
        name="halve",
    )(near, got)


def across(value, bit):
    size = lax.axis_size("fsdp")
    return lax.ppermute(value, "fsdp", [(i, i ^ bit) for i in range(size)])


def arrange_kernel(order, copies, outs_count, me_ref, *rest):
    blocks, outs, held = rest[: len(order)], rest[len(order) : -1], rest[-1]
    for at, owner in enumerate(order):
        held[jnp.bitwise_xor(me_ref[0], owner)] = blocks[at][...]
    for own in range(len(order)):
        for source, out, target, size in copies:
            begin = target(own)
            outs[out][:, begin : begin + size] = held[own, :, source : source + size].astype(F32)


def arrange(me, blocks, bits, copies, widths, name):
    rows, columns = blocks[0].shape
    tile = rows // 2
    order = order_of(bits)
    out_shape = [shape(rows, width, dtype=F32) for width in widths]
    return call(
        functools.partial(arrange_kernel, order, copies, len(widths)),
        out_shape=out_shape,
        prefetch=1,
        grid=(2,),
        in_specs=[pl.BlockSpec((tile, columns), lambda i, _: (i, 0))] * len(blocks),
        out_specs=[pl.BlockSpec((tile, width), lambda i, _: (i, 0)) for width in widths],
        scratch=[pltpu.VMEM((len(blocks), tile, columns), BF16)],
        cost_estimate=cost(0, 6 * rows * sum(widths)),
        name=name,
    )(me, *blocks)


def arrange_rows_kernel(order, me_ref, *rest):
    blocks, out_ref = rest[:-1], rest[-1]
    rows = blocks[0].shape[0]
    for at, owner in enumerate(order):
        begin = pl.multiple_of(jnp.bitwise_xor(me_ref[0], owner) * rows, rows)
        out_ref[pl.ds(begin, rows), :] = blocks[at][...].astype(F32)


def arrange_rows(me, blocks, bits):
    rows, width = blocks[0].shape
    out_shape = shape(len(blocks) * rows, width, dtype=F32)
    return call(
        functools.partial(arrange_rows_kernel, order_of(bits)),
        out_shape=out_shape,
        prefetch=1,
        in_specs=[whole(x) for x in blocks],
        out_specs=whole(out_shape),
        cost_estimate=cost(0, 6 * len(blocks) * rows * width),
        name="arrange_rows",
    )(me, *blocks)


def block_out_kernel(count, seqs, *refs):
    out_ref = refs[-1]
    for seq in range(seqs):
        resid_ref, *terms = refs[count * seq : count * (seq + 1)]
        out_ref[seq] = (resid_ref[...] + terms_of(*terms)).astype(BF16)


def finish_block_out(resid, terms, waits=()):
    rows, width = resid[0].shape
    out_shape = shape(len(resid), rows, width)
    flat = [y for q in range(len(resid)) for y in (resid[q], *[x for pair in terms[q] for x in pair])]
    count = len(flat) // len(resid)
    return call(
        functools.partial(block_out_kernel, count, len(resid)),
        out_shape=out_shape,
        in_specs=[whole(x) for x in flat],
        out_specs=whole(out_shape),
        cost_estimate=cost(0, 12 * out_shape.size),
        name="finish_block_out",
        waits=waits,
    )(*flat)


def tokens_grad_kernel(count, seqs, tokens_ref, gain_ref, *refs):
    out_ref = refs[-1]
    for seq in range(seqs):
        resid_ref, *terms = refs[count * seq : count * (seq + 1)]
        rows = tokens_ref[seq].astype(F32)
        factor = lax.rsqrt(jnp.mean(rows * rows, axis=-1, keepdims=True) + epsilon)
        unit_rows = rows * factor
        scaled = terms_of(*terms) * gain_ref[...]
        mean_dot = jnp.mean(scaled * unit_rows, axis=-1, keepdims=True)
        out_ref[seq] = (resid_ref[...] + factor * (scaled - unit_rows * mean_dot)).astype(BF16)


def finish_tokens_grad(tokens, gain, grad_resid, terms, waits=()):
    out_shape = shape(*tokens.shape)
    flat = [
        y for q in range(len(grad_resid)) for y in (grad_resid[q], *[x for pair in terms[q] for x in pair])
    ]
    count = len(flat) // len(grad_resid)
    return call(
        functools.partial(tokens_grad_kernel, count, len(grad_resid)),
        out_shape=out_shape,
        in_specs=[whole(x) for x in (tokens, gain, *flat)],
        out_specs=whole(out_shape),
        cost_estimate=cost(0, 12 * out_shape.size),
        name="finish_tokens_grad",
        waits=waits,
    )(tokens, gain, *flat)


def join_kernel(chips, me_ref, *refs):
    blocks, out_ref = refs[:-1], refs[-1]
    chip = me_ref[0] // 2
    for back in range(chips):
        out_ref[lax.rem(chip - back + chips, chips)] = blocks[back][...]


def join(me, blocks, waits=()):
    rows, width = blocks[0].shape
    out_shape = shape(len(blocks), rows, width)
    return call(
        functools.partial(join_kernel, len(blocks)),
        out_shape=out_shape,
        prefetch=1,
        in_specs=[whole(x) for x in blocks],
        out_specs=whole(out_shape),
        cost_estimate=cost(0, 4 * out_shape.size),
        name="join",
        waits=waits,
    )(me, *blocks)


def out_weight_kernel(spans, seqs, chips, own, me_ref, shard_ref, *refs):
    mixed, (*branches, near_ref, far_ref) = refs[: spans * seqs], refs[spans * seqs :]
    chip, core = shard_ref[0] // 2, shard_ref[0] % 2
    for at in range(spans):
        total = None
        for seq in range(seqs):
            term = dot(mixed[seq * spans + at][...], branches[seq][...], 0, 0)
            total = term if total is None else total + term
        total = total.astype(BF16)
        count = total.shape[0] // own
        for part in range(count):
            owner = jnp.bitwise_xor(me_ref[0], at) * count + part
            back = lax.rem(chip - owner // 2 + chips, chips)

            @pl.when(owner % 2 == core)
            def _():
                near_ref[back] = total[part * own : (part + 1) * own]

            @pl.when(owner % 2 != core)
            def _():
                far_ref[back] = total[part * own : (part + 1) * own]


def out_weight_grad(me, me_shard, mixed, branches, own, shards, waits=()):
    flat = [x for group in mixed for x in group]
    narrow, width = flat[0].shape[1], branches[0].shape[1]
    out_shape = [shape(shards // 2, own, width)] * 2
    return call(
        functools.partial(out_weight_kernel, len(mixed[0]), len(branches), shards // 2, own),
        out_shape=out_shape,
        prefetch=2,
        in_specs=[whole(x) for x in (*flat, *branches)],
        out_specs=[whole(x) for x in out_shape],
        cost_estimate=cost(
            2 * len(flat) * flat[0].size * width,
            2 * len(mixed[0]) * narrow * width,
        ),
        name="out_weight_grad",
        waits=waits,
    )(me, me_shard, *flat, *branches)


def turning_tables(positions):
    frequency = jnp.exp(
        jnp.arange(HALF, dtype=F32) * (-2.0 * math.log(rope_base) / HEAD_DIMENSION)
    )
    angles = positions.astype(F32)[:, :, None] * frequency
    cosine, sine = jnp.cos(angles), jnp.sin(angles)
    empty = jnp.zeros((*positions.shape, 64 - HALF), F32)
    return (
        jnp.concatenate([cosine, empty, cosine, empty], axis=-1),
        jnp.concatenate([-sine, empty, sine, empty], axis=-1),
    )


def sum_all(value):
    for axis in ("seq", "fsdp"):
        size = lax.axis_size(axis)
        bit = 1
        while bit < size:
            value = value + lax.ppermute(value, axis, [(i, i ^ bit) for i in range(size)])
            bit *= 2
    return value


def body(
    tokens,
    joined_input_weight,
    out_projection,
    gate_weight,
    up_weight,
    down_weight,
    norm_first,
    norm_second,
    positions,
    cotangent,
):
    seqs, span, width = tokens.shape
    spans = lax.axis_size("seq")
    shards = lax.axis_size("fsdp")
    chips = shards // 2
    me = jnp.full((1,), lax.axis_index("seq"), jnp.int32)
    me_shard = jnp.full((1,), lax.axis_index("fsdp"), jnp.int32)
    full = positions.shape[1]
    pairs = KEY_VALUE_HEADS // spans
    repeat = QUERY_HEAD_COUNT // KEY_VALUE_HEADS
    unit = repeat + 2
    query_columns = QUERY_HEAD_COUNT * HEAD_DIMENSION
    pair_columns = KEY_VALUE_HEADS * HEAD_DIMENSION
    query_slab = query_columns // spans
    pair_slab = pair_columns // spans
    own_rows = joined_input_weight.shape[0]
    piece = FF // (shards * spans)
    inner = shards * piece
    step = min(256, full)
    pad = jnp.asarray(pad_matrix(pairs, repeat), BF16)
    place = jnp.asarray(place_matrix(pairs, repeat), BF16)
    gain_in, gain_mid = norm_first[None, :], norm_second[None, :]
    upward = tuple(range(spans.bit_length() - 1))
    orders = [(upward[::-1], upward)[q % 2] for q in range(seqs)]
    both = range(seqs)
    del CHAIN[:]

    def gather(shard):
        return lax.all_gather(shard, "fsdp", axis=0, tiled=True)

    def owned(value):
        return lax.psum_scatter(value, "fsdp", scatter_dimension=0, tiled=True)

    ways = (upward[::-1], upward)

    def flat(pairs):
        return tuple(x for pair in pairs for x in pair)

    def copied(value, bits):
        held = [value]
        for bit in bits:
            held = held + [swap(x, bit) for x in held]
        return held

    in_shard = cut_in(me, joined_input_weight, spans, (query_slab, pair_slab, pair_slab))
    w_in = gather(in_shard)
    w_out = gather(out_projection).reshape(spans, query_slab, width)
    normed = norm_rows(tokens, gain_in)
    x_got = gather_start(normed, orders)
    both_shard, down_shard = cut_feed(
        me, gate_weight, up_weight, down_weight, spans, shards, piece, ()
    )
    w_both = gather(both_shard)
    down_blocks = [down_shard, around(down_shard)]

    def arrived():
        down_blocks[-1:] = pin(down_blocks[-1])

    def pass_on():
        if len(down_blocks) < chips:
            arrived()
            down_blocks.append(around(down_blocks[-1]))

    cosine, sine = turning_tables(positions)
    starts = (jnp.arange(full, dtype=jnp.int32)[None, :] - positions)[:, None, :]
    x_in = gather_end(normed, x_got, orders, "stack_in")
    arrived()
    w_wide = widen(w_in, pad)
    cot_rows = split_rows(cotangent)
    cot_got = gather_start(cot_rows, orders)

    projected, mixed, lse, resid, x_mid = [], [], [], [], []

    def project_rows(q):
        rows, *normed_mid = project_out(q, me, mixed[q], w_out, tokens, gain_mid, ways)
        resid.append(rows)
        return normed_mid, gather_start(normed_mid, ways)

    for q in both:
        projected.append(
            project_in(
                me, x_in[q], orders[q], w_wide, cosine[q], sine[q], unit, x_in[-1] if q == 0 else ()
            )
        )
        if q == 0:
            cots = gather_end(cot_rows, cot_got, orders, "stack_cot")
        if q == 1:
            pass_on()
            started = project_rows(0)
        heads, sums = attention_forward(me, projected[q], starts[q], place, spans, repeat, step)
        lse.append(sums)
        mixed.append(shared(heads))
        if q == 1:
            x_mid.append(gather_end(*started, ways, "stack_mid", flat(cots)))
    while len(down_blocks) < chips:
        pass_on()
    down_near = join(me_shard, down_blocks)
    down_far = beside(down_near)
    for q in both[1:]:
        x_mid.append(gather_end(*project_rows(q), ways, "stack_mid"))

    hidden, grad_both, grad_mid, x_all = [], [], [], []
    for q in both:
        parts, kept, grads, rows = feed_forward(
            spans, me_shard, x_mid[q], cots[q], orders[q], ways, w_both, down_near, down_far
        )
        hidden.append(kept)
        grad_both.append(grads)
        x_all.append(rows)
        grad_mid.append(scatter_start(parts, ways))

    grad_resid, branches, head_grads = [], [], []

    def norm_back(q, waits=()):
        rows, branch, heads = norm_out_back(
            q, me, spans, grad_mid[q], resid[q], cotangent, gain_mid, w_out, waits
        )
        grad_resid.append(rows)
        branches.append(branch)
        head_grads.append(shared(heads))

    grad_mid[0] = scatter_end(*grad_mid[0], ways)
    both_part, gain_second = weight_grad(x_all, grad_both, w_both, "gate_up_grad")
    both_own = owned(both_part)
    norm_back(0)
    for q in both[1:]:
        grad_mid[q] = scatter_end(*grad_mid[q], ways)
    outs = scatter_start(
        feed_out(spans, me_shard, hidden, down_near, down_far, tuple(head_grads[0][1:])), orders
    )
    for q in both[1:]:
        norm_back(q)
    (down_part,) = weight_grad(hidden, flat(cots), None, "down_grad")
    down_own = owned(down_part)
    out_near, out_far = out_weight_grad(me, me_shard, mixed, branches, own_rows, shards)
    out_got = beside(out_far)

    both_every = copied(both_own, ways[0])
    down_every = copied(down_own, ways[1])
    proj_grads, grad_in = [], []
    for q in both:
        proj_grads.append(
            attention_backward(
                me,
                projected[q],
                starts[q],
                place,
                head_grads[q],
                orders[q],
                lse[q],
                cosine[q],
                sine[q],
                pad,
                repeat,
                step,
                () if q == 0 else (both_own,),
            )
        )
        if q == 0:
            (out_got,) = pin(out_got)
            out_near = add_pairs(out_near, out_got)
            out_passing = around(out_near[1])
        if q == seqs - 1:
            for p in both[:-1]:
                grad_in[p] = scatter_end(*grad_in[p], ways)
            (out_passing,) = pin(out_passing)
            out_passing = around(add_pairs(out_near[2], out_passing))
            in_near, in_far, gain_first = in_weight_grad(
                me_shard,
                flat(x_in),
                proj_grads,
                w_in,
                own_rows,
                shards,
                both_every[1:2],
            )
            in_got = across(in_far, 1)
        waits = tuple(x for group in head_grads[1:] for x in group[1:]) if q == 0 else ()
        parts = grad_into_rows(spans, proj_grads[q], orders[q], ways, w_in, tuple(waits))
        grad_in.append(scatter_start(parts, ways))
        if q == 0:
            outs = scatter_end(*outs, orders)
    in_near, in_sent = halve(in_near, in_got)
    in_got = across(in_sent, 2)
    for back in range(3, chips):
        (out_passing,) = pin(out_passing)
        out_passing = around(add_pairs(out_near[back], out_passing))
    gains = sum_all(
        jnp.stack([gain_first.reshape(width) / norm_first, gain_second.reshape(width) / norm_second])
    )
    block_out = finish_block_out(resid, [[pair] for pair in outs])
    bit = 4
    while in_near.shape[0] > 1:
        in_near, in_sent = halve(in_near, in_got)
        in_got = across(in_sent, bit)
        bit *= 2
    out_total = add_pairs(out_near[0], out_passing)
    grad_in[-1] = scatter_end(*grad_in[-1], ways)
    copies = [
        (part * inner + shard * piece, part, lambda own, shard=shard: (shard * spans + own) * piece, piece)
        for part in range(2)
        for shard in range(shards)
    ]
    gate_grad, up_grad = arrange(me, both_every, ways[0], copies, (FF, FF), "arrange_gate_up")
    (in_own,) = halve(in_near, in_got)
    in_own = in_own[0]
    down_grad = arrange_rows(me, down_every, ways[1])
    tokens_grad = finish_tokens_grad(tokens, gain_in, grad_resid, grad_in)
    copies = [
        (0, 0, lambda own: own * query_slab, query_slab),
        (query_slab, 0, lambda own: query_columns + own * pair_slab, pair_slab),
        (
            query_slab + pair_slab,
            0,
            lambda own: query_columns + pair_columns + own * pair_slab,
            pair_slab,
        ),
    ]
    (in_grad,) = arrange(
        me,
        copied(in_own, upward),
        upward,
        copies,
        (query_columns + 2 * pair_columns,),
        "arrange_in",
    )
    for bit in upward:
        out_total = add_pairs(out_total, swap(out_total, bit))
    out_grad = out_total.astype(F32)
    return (
        block_out,
        tokens_grad,
        in_grad,
        out_grad,
        gate_grad,
        up_grad,
        down_grad,
        gains[0],
        gains[1],
    )


def solution(mesh):
    return jax.shard_map(
        body,
        mesh=mesh,
        in_specs=(
            P("fsdp", "seq", None),
            P("fsdp", None),
            P("fsdp", None),
            P("fsdp", None),
            P("fsdp", None),
            P("fsdp", None),
            P(),
            P(),
            P("fsdp", None),
            P("fsdp", "seq", None),
        ),
        out_specs=(
            P("fsdp", "seq", None),
            P("fsdp", "seq", None),
            P("fsdp", None),
            P("fsdp", None),
            P("fsdp", None),
            P("fsdp", None),
            P("fsdp", None),
            P(),
            P(),
        ),
        check_vma=False,
    )
```

```python
import functools
import math

import jax
import jax.numpy as jnp
import numpy as np
from jax import lax
from jax.experimental import pallas as pl
from jax.experimental.pallas import tpu as pltpu
from jax.sharding import PartitionSpec as P

FF = 4096
QUERY_HEAD_COUNT = 16
KEY_VALUE_HEADS = 8
HEAD_DIMENSION = 96
HALF = HEAD_DIMENSION // 2
LANES = 128

epsilon = 1e-05
rope_base = 100000.0
SCALING = 1.0 / math.sqrt(HEAD_DIMENSION)
LOG2E = 1.4426950408889634
BF16 = jnp.bfloat16
F32 = jnp.float32
MIB = 1024 * 1024
VMEM_LIMIT = 64
COST_SCALE = 20
WEIGHTS = {"norm_out_back": 2.5, "feed_out": 2.5}
OPTIONS = (1, 0, 0, 0, 0, 0, 1, 0)


def dot(a, b, ca, cb):
    return lax.dot_general(a, b, (((ca,), (cb,)), ((), ())), preferred_element_type=F32)


def params(limit):
    return pltpu.CompilerParams(vmem_limit_bytes=limit * MIB)


def cost(flops, moved, trans=0):
    return int(flops), int(moved)


def weighted(estimate, name):
    scale = WEIGHTS.get(name, COST_SCALE)
    return pl.CostEstimate(
        flops=int(estimate[0] * scale), bytes_accessed=int(estimate[1] * scale), transcendentals=0
    )


CHAIN = []


def call(kernel, *, out_shape, in_specs, out_specs, prefetch=0, grid=(1,), scratch=(), cost_estimate=None, name=None, waits=()):
    count = prefetch + len(in_specs)
    waits = (*waits, *CHAIN[-1:])

    def run(*refs):
        kernel(*refs[:count], *refs[count + len(waits) :])

    inner = pl.pallas_call(
        run,
        out_shape=out_shape,
        grid_spec=pltpu.PrefetchScalarGridSpec(
            num_scalar_prefetch=prefetch,
            grid=grid,
            in_specs=[*in_specs, *[pl.BlockSpec(memory_space=pltpu.HBM)] * len(waits)],
            out_specs=out_specs,
            scratch_shapes=list(scratch),
        ),
        compiler_params=params(VMEM_LIMIT),
        cost_estimate=weighted(cost_estimate, name),
        name=name,
    )

    def made(*args):
        out = inner(*args, *waits)
        CHAIN.append(out[-1] if isinstance(out, (list, tuple)) else out)
        return out

    return made


def pin(*values):
    waits = tuple(CHAIN[-1:])
    count = len(values)
    hbm = pl.BlockSpec(memory_space=pltpu.HBM)
    out = pl.pallas_call(
        lambda *refs: None,
        out_shape=[shape(*x.shape, dtype=x.dtype) for x in values],
        in_specs=[hbm] * (count + len(waits)),
        out_specs=[hbm] * count,
        input_output_aliases={at: at for at in range(count)},
        cost_estimate=weighted(cost(0, 0), "pin"),
        name="pin",
    )(*values, *waits)
    CHAIN.append(out[-1])
    return out


def whole(array, **extra):
    return pl.BlockSpec(array.shape, lambda *_: (0,) * len(array.shape), **extra)


def shape(*sizes, dtype=BF16):
    return jax.ShapeDtypeStruct(sizes, dtype)


def pad_matrix(pairs, repeat):
    unit = repeat + 2
    out = np.zeros((pairs * unit * HEAD_DIMENSION, pairs * unit * LANES), np.float32)
    for g in range(pairs):
        for r in range(unit):
            if r < repeat:
                src = (g * repeat + r) * HEAD_DIMENSION
            else:
                src = (pairs * repeat + (r - repeat) * pairs + g) * HEAD_DIMENSION
            dst = (g * unit + r) * LANES
            for j in range(HEAD_DIMENSION):
                lane = j if (r == unit - 1 or j < HALF) else 64 + j - HALF
                out[src + j, dst + lane] = 1.0
    return out


def place_matrix(pairs, repeat):
    out = np.zeros((pairs, repeat * LANES, pairs * repeat * HEAD_DIMENSION), np.float32)
    for g in range(pairs):
        for r in range(repeat):
            for j in range(HEAD_DIMENSION):
                out[g, r * LANES + j, (g * repeat + r) * HEAD_DIMENSION + j] = 1.0
    return out


def order_of(bits):
    owners = [0]
    for bit in bits:
        owners = owners + [at ^ (1 << bit) for at in owners]
    return owners


def swap(value, bit):
    size = lax.axis_size("seq")
    return lax.ppermute(value, "seq", [(i, i ^ (1 << bit)) for i in range(size)])


def exchange(value, other):
    size = lax.axis_size("seq")
    return lax.ppermute(value, "seq", [(i, i ^ other) for i in range(size)])


def shared(heads):
    return [heads[0]] + [exchange(heads[at], at) for at in range(1, len(heads))]


def around(value):
    size = lax.axis_size("fsdp")
    return lax.ppermute(value, "fsdp", [(i, (i + 2) % size) for i in range(size)])


def beside(value):
    size = lax.axis_size("fsdp")
    return lax.ppermute(value, "fsdp", [(i, i ^ 1) for i in range(size)])


def copy_kernel(source_ref, *outs):
    for at, ref in enumerate(outs):
        ref[...] = source_ref[at]


def split_rows(value, waits=()):
    seqs, span, width = value.shape
    out_shape = [shape(span, width)] * seqs
    return call(
        copy_kernel,
        out_shape=out_shape,
        in_specs=[whole(value)],
        out_specs=[whole(x) for x in out_shape],
        cost_estimate=cost(0, 4 * value.size),
        name="split_rows",
        waits=waits,
    )(value)


def stack_kernel(*refs):
    count = len(refs) // 3
    for at in range(count):
        first, second, out = refs[2 * at], refs[2 * at + 1], refs[2 * count + at]
        rows = first.shape[0]
        out[:rows] = first[...]
        out[rows:] = second[...]


def stack_rows(pairs, name, waits=()):
    out_shape = [shape(2 * a.shape[0], a.shape[1]) for a, _ in pairs]
    flat = [x for pair in pairs for x in pair]
    return call(
        stack_kernel,
        out_shape=out_shape,
        in_specs=[whole(x) for x in flat],
        out_specs=[whole(x) for x in out_shape],
        cost_estimate=cost(0, 4 * sum(x.size for x in flat)),
        name=name,
        waits=waits,
    )(*flat)


def gather_start(blocks, orders):
    return [swap(x, bits[0]) for x, bits in zip(blocks, orders)]


def gather_end(blocks, got, orders, name, waits=()):
    held = list(zip(blocks, got))
    for level in range(1, len(orders[0])):
        joined = stack_rows(held, name, waits if level == 1 else ())
        held = [(x, swap(x, bits[level])) for x, bits in zip(joined, orders)]
    return held


def fold_kernel(*refs):
    count = len(refs) // 4
    for at in range(count):
        near, got, keep, send = refs[at], refs[count + at], refs[2 * count + at], refs[3 * count + at]
        total = near[...].astype(F32) + got[...].astype(F32)
        cut = total.shape[0] // 2
        keep[...] = total[:cut]
        send[...] = total[cut:].astype(BF16)


def fold(near, got, waits=()):
    out_shape = [shape(x.shape[0] // 2, x.shape[1], dtype=F32) for x in near]
    out_shape += [shape(x.shape[0] // 2, x.shape[1]) for x in near]
    out = call(
        fold_kernel,
        out_shape=out_shape,
        in_specs=[whole(x) for x in (*near, *got)],
        out_specs=[whole(x) for x in out_shape],
        cost_estimate=cost(0, 5 * sum(x.size for x in near)),
        name="fold",
        waits=waits,
    )(*near, *got)
    return out[: len(near)], out[len(near) :]


def scatter_start(parts, orders):
    return [near for near, _ in parts], [swap(far, bits[-1]) for (_, far), bits in zip(parts, orders)]


def scatter_end(near, got, orders, waits=()):
    for level in range(len(orders[0]) - 2, -1, -1):
        near, sent = fold(near, got, waits)
        got = [swap(x, bits[level]) for x, bits in zip(sent, orders)]
    return list(zip(near, got))


def norm_kernel(tokens_ref, gain_ref, *outs):
    for seq, out in enumerate(outs):
        rows = tokens_ref[seq].astype(F32)
        factor = lax.rsqrt(jnp.mean(rows * rows, axis=-1, keepdims=True) + epsilon)
        out[...] = (rows * factor * gain_ref[...]).astype(BF16)


def norm_rows(tokens, gain):
    seqs, span, width = tokens.shape
    out_shape = [shape(span, width)] * seqs
    return call(
        norm_kernel,
        out_shape=out_shape,
        in_specs=[whole(tokens), whole(gain)],
        out_specs=[whole(x) for x in out_shape],
        cost_estimate=cost(8 * tokens.size, 4 * tokens.size),
        name="norm_rows",
    )(tokens, gain)


def cut_in_kernel(spans, sizes, me_ref, w_ref, out_ref):
    for own in range(spans):

        @pl.when(me_ref[0] == own)
        def _():
            begin, put = 0, 0
            for size in sizes:
                out_ref[:, put : put + size] = w_ref[:, begin + own * size : begin + (own + 1) * size]
                begin, put = begin + spans * size, put + size


def cut_in(me, weight, spans, sizes):
    out_shape = shape(weight.shape[0], sum(sizes))
    return call(
        functools.partial(cut_in_kernel, spans, sizes),
        out_shape=out_shape,
        prefetch=1,
        in_specs=[whole(weight)],
        out_specs=whole(out_shape),
        cost_estimate=cost(0, 4 * weight.size),
        name="cut_in",
    )(me, weight)


def cut_feed_kernel(spans, shards, piece, me_ref, gate_ref, up_ref, down_ref, both_ref, out_ref):
    inner = shards * piece
    for own in range(spans):

        @pl.when(me_ref[0] == own)
        def _():
            for shard in range(shards):
                begin = (shard * spans + own) * piece
                put = shard * piece
                both_ref[:, put : put + piece] = gate_ref[:, begin : begin + piece]
                both_ref[:, inner + put : inner + put + piece] = up_ref[:, begin : begin + piece]
            out_ref[...] = down_ref[own * piece : (own + 1) * piece, :]


def cut_feed(me, gate, up, down, spans, shards, piece, waits):
    out_shape = (shape(gate.shape[0], 2 * shards * piece), shape(piece, down.shape[1]))
    return call(
        functools.partial(cut_feed_kernel, spans, shards, piece),
        out_shape=out_shape,
        prefetch=1,
        in_specs=[whole(x) for x in (gate, up, down)],
        out_specs=[whole(x) for x in out_shape],
        cost_estimate=cost(0, 4 * gate.size),
        name="cut_feed",
        waits=waits,
    )(me, gate, up, down)


def widen_kernel(w_ref, pad_ref, out_ref):
    out_ref[...] = dot(w_ref[...], pad_ref[...], 1, 0).astype(BF16)


def widen(w_slice, pad, waits=()):
    rows, narrow = w_slice.shape
    wide = pad.shape[1]
    out_shape = shape(rows, wide)
    return call(
        widen_kernel,
        out_shape=out_shape,
        in_specs=[whole(w_slice), whole(pad)],
        out_specs=whole(out_shape),
        cost_estimate=cost(2 * rows * narrow * wide, 2 * rows * (narrow + wide)),
        name="widen",
        waits=waits,
    )(w_slice, pad)


class Walk:
    def __init__(self, spans, span, near_first):
        self.cut, self.span, self.near_first = spans // 2, span, near_first

    def first(self, step):
        return jnp.minimum(step, self.cut - 1)

    def second(self, step):
        return jnp.maximum(step - self.cut, 0)

    def near(self, step, *_):
        return (self.first(step) if self.near_first else self.second(step), 0)

    def far(self, step, *_):
        return (self.second(step) if self.near_first else self.first(step), 0)

    def both(self, step, *_):
        return (step if self.near_first else lax.rem(step + self.cut, 2 * self.cut), 0)

    def specs(self, width):
        return [
            pl.BlockSpec((self.span, width), self.near),
            pl.BlockSpec((self.span, width), self.far),
        ]

    def is_near(self):
        early = pl.program_id(0) < self.cut
        return early if self.near_first else jnp.logical_not(early)

    def load(self, near_ref, far_ref):
        return jnp.where(self.is_near(), near_ref[...], far_ref[...])

    def store(self, near_ref, far_ref, value):
        near = self.is_near()

        @pl.when(near)
        def _():
            near_ref[...] = value

        @pl.when(jnp.logical_not(near))
        def _():
            far_ref[...] = value


def owner_at(order, index):
    owner = 0
    for at, value in enumerate(order):
        owner = jnp.where(index == at, value, owner)
    return owner


class Visits:
    def __init__(self, spans, span):
        self.spans, self.span = spans, span
        self.order = sorted(range(spans), key=lambda at: -bin(at).count("1"))

    def index(self, blocks):
        held = [blocks.get(owner) for owner in self.order]
        known = next(x for x in held if x is not None)
        for at, value in enumerate(held):
            known = held[at] = known if value is None else value
        return lambda step, *_: (owner_at(held, step), 0)

    def parts(self, bits):
        order = order_of(bits)
        cut = self.spans // 2
        near = {owner: at for at, owner in enumerate(order[:cut])}
        far = {owner: at for at, owner in enumerate(order[cut:])}
        return near, far

    def specs(self, bits, width):
        return [pl.BlockSpec((self.span, width), self.index(blocks)) for blocks in self.parts(bits)]

    def rows(self, bits, width):
        order = order_of(bits)
        return pl.BlockSpec(
            (self.span, width), self.index({owner: at for at, owner in enumerate(order)})
        )

    def is_near(self, bits):
        near, _ = self.parts(bits)
        flag = jnp.bool_(False)
        for at, owner in enumerate(self.order):
            if owner in near:
                flag = jnp.logical_or(flag, pl.program_id(0) == at)
        return flag

    def load(self, bits, near_ref, far_ref):
        return jnp.where(self.is_near(bits), near_ref[...], far_ref[...])

    def store(self, bits, near_ref, far_ref, value):
        near = self.is_near(bits)

        @pl.when(near)
        def _():
            near_ref[...] = value

        @pl.when(jnp.logical_not(near))
        def _():
            far_ref[...] = value

    def store_halves(self, ways, refs, value):
        columns = value.shape[1] // len(ways)
        for at, bits in enumerate(ways):
            part = value[:, at * columns : (at + 1) * columns]
            self.store(bits, refs[2 * at], refs[2 * at + 1], part)


def in_kernel(walk, unit, me_ref, w_ref, cos_ref, sin_ref, near_ref, far_ref, out_ref):
    rows = dot(walk.load(near_ref, far_ref), w_ref[...], 1, 0)
    cosine, sine = cos_ref[...], sin_ref[...]
    for part in range(rows.shape[1] // LANES):
        lanes = slice(part * LANES, (part + 1) * LANES)
        piece = rows[:, lanes]
        if part % unit != unit - 1:
            piece = piece * cosine + pltpu.roll(piece, 64, 1) * sine
        out_ref[:, lanes] = piece.astype(BF16)


def project_in(me, rows, bits, w_wide, cosine, sine, unit, waits=()):
    width, wide = w_wide.shape
    order = order_of(bits)
    spans = len(order)
    full = cosine.shape[0]
    span = full // spans
    walk = Walk(spans, span, True)

    def ordered(step, me_ref):
        return (jnp.bitwise_xor(me_ref[0], owner_at(order, step)), 0)

    return call(
        functools.partial(in_kernel, walk, unit),
        out_shape=shape(full, wide),
        prefetch=1,
        grid=(spans,),
        in_specs=[
            whole(w_wide, pipeline_mode=pl.Buffered(1)),
            pl.BlockSpec((span, LANES), ordered),
            pl.BlockSpec((span, LANES), ordered),
            *walk.specs(width),
        ],
        out_specs=pl.BlockSpec((span, wide), ordered),
        cost_estimate=cost(2 * full * width * wide, 2 * full * (width + wide) + 2 * width * wide),
        name="project_in",
        waits=waits,
    )(me, w_wide, cosine, sine, *rows)


def mask_of(scores, first_key, first_row, starts, repeat, diagonal):
    keys = lax.broadcasted_iota(jnp.int32, scores.shape, 0) + first_key
    allowed = keys >= starts
    if diagonal:
        step = scores.shape[1] // repeat
        rows = lax.broadcasted_iota(jnp.int32, scores.shape, 1) % step + first_row
        allowed = allowed & (keys <= rows)
    return jnp.where(allowed, scores, -1e30)


def query_of(proj_ref, rows, repeat):
    return jnp.concatenate(
        [proj_ref[rows, r * LANES : (r + 1) * LANES] for r in range(repeat)], axis=0
    )


def forward_kernel(spans, step, repeat, me_ref, proj_ref, start_ref, place_ref, *rest):
    outs, lse_ref, held = rest[:spans], rest[spans], rest[spans + 1]
    full = proj_ref.shape[0]
    span = full // spans
    pair = pl.program_id(0)
    me = me_ref[0]
    value_t = proj_ref[:, (repeat + 1) * LANES :].T
    starts = start_ref[...]

    @pl.when(pair == 0)
    def _():
        held[...] = jnp.zeros_like(held)

    for block in range(full // step):
        begin, end = block * step, (block + 1) * step
        rows = slice(begin, end)
        query = query_of(proj_ref, rows, repeat)
        starts_now = jnp.concatenate([starts[:, rows]] * repeat, axis=1)
        pieces = []
        for key_block in range(block + 1):
            first = key_block * step
            key = proj_ref[first : first + step, repeat * LANES : (repeat + 1) * LANES]
            scores = dot(key, query, 1, 1) * (SCALING * LOG2E)
            pieces.append(mask_of(scores, first, begin, starts_now, repeat, key_block == block))
        top = functools.reduce(jnp.maximum, [jnp.max(p, axis=0, keepdims=True) for p in pieces])
        total = None
        summed = None
        for key_block in range(block + 1):
            first = key_block * step
            raised = jnp.exp2(pieces[key_block] - top)
            part = jnp.sum(raised, axis=0, keepdims=True)
            mixed = dot(value_t[:, first : first + step], raised.astype(BF16), 1, 0)
            total = part if total is None else total + part
            summed = mixed if summed is None else summed + mixed
        mixed_t = (summed * (1.0 / total)).astype(BF16)
        lse_ref[block : block + 1, :] = top + jnp.log2(total)
        wide = None
        for r in range(repeat):
            term = dot(
                mixed_t[:, r * step : (r + 1) * step],
                place_ref[r * LANES : (r + 1) * LANES, :],
                0,
                0,
            )
            wide = term if wide is None else wide + term
        wide = wide.astype(BF16)
        for piece in range(step // span):
            at = jnp.bitwise_xor(me, block * (step // span) + piece)
            held[at] = held[at] + wide[piece * span : (piece + 1) * span]

    @pl.when(pair == pl.num_programs(0) - 1)
    def _():
        for at in range(spans):
            outs[at][...] = held[at]


def attention_forward(me, proj, starts, place, spans, repeat, step, waits=()):
    full, wide = proj.shape
    pairs, _, narrow = place.shape
    group = wide // pairs
    span = full // spans
    work = pairs * repeat * full * full
    out_shape = [jax.ShapeDtypeStruct((span, narrow), BF16)] * spans
    out_shape.append(jax.ShapeDtypeStruct((pairs, full // step, repeat * step), F32))
    *mixed, lse = call(
        functools.partial(forward_kernel, spans, step, repeat),
        out_shape=out_shape,
        prefetch=1,
        grid=(pairs,),
        in_specs=[
            pl.BlockSpec((full, group), lambda j, _: (0, j)),
            pl.BlockSpec((1, full), lambda j, _: (0, 0)),
            pl.BlockSpec((None, repeat * LANES, narrow), lambda j, _: (j, 0, 0)),
        ],
        out_specs=[whole(x) for x in out_shape[:-1]]
        + [pl.BlockSpec((None, full // step, repeat * step), lambda j, _: (j, 0, 0))],
        scratch=[pltpu.VMEM((spans, span, narrow), BF16)],
        cost_estimate=cost(2 * work * 256, 2 * proj.size * 2, work),
        name="attention_forward",
        waits=waits,
    )(me, proj, starts, place)
    return mixed, lse


def backward_kernel(
    order, step, repeat, me_ref, proj_ref, start_ref, place_ref, lse_ref, cos_ref, sin_ref, pad_ref, *rest
):
    spans = len(order)
    grads, (out_ref, key_acc, value_acc, held) = rest[:spans], rest[spans:]
    full = proj_ref.shape[0]
    span = full // spans
    pair = pl.program_id(0)
    me = me_ref[0]
    key_t = proj_ref[:, repeat * LANES : (repeat + 1) * LANES].T
    starts = start_ref[...]
    key_acc[...] = jnp.zeros_like(key_acc)
    value_acc[...] = jnp.zeros_like(value_acc)

    @pl.when(pair == 0)
    def _():
        for at in range(spans):
            held[jnp.bitwise_xor(me, at)] = grads[at][...]
        out_ref[...] = jnp.zeros_like(out_ref)

    def turn_back(grad, rows):
        grad = grad.astype(BF16).astype(F32)
        return (grad * cos_ref[rows, :] - pltpu.roll(grad, 64, 1) * sin_ref[rows, :]).astype(BF16)

    def put(begin, wide):
        for at in range(0, wide.shape[0], span):
            owner = jnp.bitwise_xor(me, (begin + at) // span)
            where = 0
            for index, value in enumerate(order):
                where = jnp.where(owner == value, index, where)
            here = pl.ds(pl.multiple_of(where * span, span), span)
            out_ref[here, :] = out_ref[here, :] + wide[at : at + span]

    for block in range(full // step):
        begin, end = block * step, (block + 1) * step
        rows = slice(begin, end)
        query = query_of(proj_ref, rows, repeat)
        grad_rows = jnp.concatenate(
            [held[at] for at in range(begin // span, end // span)], axis=0
        )
        grad = jnp.concatenate(
            [
                dot(grad_rows, place_ref[r * LANES : (r + 1) * LANES, :], 1, 1).astype(BF16)
                for r in range(repeat)
            ],
            axis=0,
        )
        starts_now = jnp.concatenate([starts[:, rows]] * repeat, axis=1)
        lse = lse_ref[block : block + 1, :]
        kept = []
        mean_dot = None
        for key_block in range(block + 1):
            first = key_block * step
            keys = slice(first, first + step)
            key = proj_ref[keys, repeat * LANES : (repeat + 1) * LANES]
            value = proj_ref[keys, (repeat + 1) * LANES :]
            scores = dot(key, query, 1, 1) * (SCALING * LOG2E)
            scores = mask_of(scores, first, begin, starts_now, repeat, key_block == block)
            shares = jnp.exp2(scores - lse)
            value_acc[keys, :] += dot(shares.astype(BF16), grad, 1, 0)
            product = shares * dot(value, grad, 1, 1)
            part = jnp.sum(product, axis=0, keepdims=True)
            mean_dot = part if mean_dot is None else mean_dot + part
            kept.append((shares, product))
        query_grad_t = None
        for key_block in range(block + 1):
            first = key_block * step
            keys = slice(first, first + step)
            shares, product = kept[key_block]
            score_grad = (SCALING * (product - shares * mean_dot)).astype(BF16)
            key_acc[keys, :] += dot(score_grad, query, 1, 0)
            term = dot(key_t[:, keys], score_grad, 1, 0)
            query_grad_t = term if query_grad_t is None else query_grad_t + term
        query_grad = query_grad_t.T
        wide = None
        for r in range(repeat):
            turned = turn_back(query_grad[r * step : (r + 1) * step], rows)
            term = dot(turned, pad_ref[:, r * LANES : (r + 1) * LANES], 1, 1)
            wide = term if wide is None else wide + term
        put(begin, wide.astype(BF16))
    for block in range(full // step):
        rows = slice(block * step, (block + 1) * step)
        turned = turn_back(key_acc[rows, :], rows)
        wide = dot(turned, pad_ref[:, repeat * LANES : (repeat + 1) * LANES], 1, 1)
        wide += dot(value_acc[rows, :].astype(BF16), pad_ref[:, (repeat + 1) * LANES :], 1, 1)
        put(block * step, wide.astype(BF16))


def attention_backward(
    me, proj, starts, place, grads, bits, lse, cosine, sine, pad, repeat, step, waits=()):
    full, wide = proj.shape
    pairs, _, narrow = place.shape
    group = wide // pairs
    work = pairs * repeat * full * full
    out_shape = shape(full, pad.shape[0])
    return call(
        functools.partial(backward_kernel, order_of(bits), step, repeat),
        out_shape=out_shape,
        prefetch=1,
        grid=(pairs,),
        in_specs=[
            pl.BlockSpec((full, group), lambda j, _: (0, j)),
            pl.BlockSpec((1, full), lambda j, _: (0, 0)),
            pl.BlockSpec((None, repeat * LANES, narrow), lambda j, _: (j, 0, 0)),
            pl.BlockSpec((None, full // step, repeat * step), lambda j, _: (j, 0, 0)),
            whole(cosine),
            whole(sine),
            pl.BlockSpec((pad.shape[0], group), lambda j, _: (0, j)),
            *[whole(x) for x in grads],
        ],
        out_specs=whole(out_shape),
        scratch=[
            pltpu.VMEM((full, LANES), F32),
            pltpu.VMEM((full, LANES), F32),
            pltpu.VMEM((len(grads), full // len(grads), narrow), BF16),
        ],
        cost_estimate=cost(2 * work * 640, 2 * proj.size * 4, work),
        name="attention_backward",
        waits=waits,
    )(me, proj, starts, place, lse, cosine, sine, pad, *grads)


def out_kernel(spans, me_ref, w_ref, tokens_ref, gain_ref, *rest):
    mixed, (resid_ref, *parts) = rest[:spans], rest[spans:]
    summed = tokens_ref[...].astype(F32)
    for at in range(spans):
        summed += dot(mixed[at][...], w_ref[jnp.bitwise_xor(me_ref[0], at)], 1, 0)
    resid_ref[...] = summed
    factor = lax.rsqrt(jnp.mean(summed * summed, axis=-1, keepdims=True) + epsilon)
    normed = (summed * factor * gain_ref[...]).astype(BF16)
    columns = parts[0].shape[1]
    for at, part in enumerate(parts):
        part[...] = normed[:, at * columns : (at + 1) * columns]


def project_out(seq, me, mixed, w_out, tokens, gain, ways, waits=()):
    _, span, width = tokens.shape
    out_shape = [shape(span, width, dtype=F32)] + [shape(span, width // len(ways))] * len(ways)
    return call(
        functools.partial(out_kernel, len(mixed)),
        out_shape=out_shape,
        prefetch=1,
        in_specs=[
            whole(w_out),
            pl.BlockSpec((None, span, width), lambda *_: (seq, 0, 0)),
            whole(gain),
            *[whole(x) for x in mixed],
        ],
        out_specs=[whole(x) for x in out_shape],
        cost_estimate=cost(2 * span * width * width, span * width * 10 + width * width * 2),
        name="project_out",
        waits=waits,
    )(me, w_out, tokens, gain, *mixed)


def assemble(held, core, near_ref, far_ref):
    for chip in range(near_ref.shape[0]):
        held[2 * chip + core] = near_ref[chip]
        held[2 * chip + 1 - core] = far_ref[chip]


def feed_kernel(
    visits, bits, ways, shard_ref, both_ref, near_ref, far_ref, cn_ref, cf_ref, *rest
):
    count = 2 * len(ways)
    rows, (hid_ref, dboth_ref, x_ref, *outs), held = rest[:count], rest[count:-1], rest[-1]
    inner = both_ref.shape[1] // 2

    @pl.when(pl.program_id(0) == 0)
    def _():
        assemble(held, shard_ref[0] % 2, near_ref, far_ref)

    down = held[...].reshape(inner, held.shape[2])
    columns = rows[0].shape[1]
    for at, way in enumerate(ways):
        x_ref[:, at * columns : (at + 1) * columns] = visits.load(way, rows[2 * at], rows[2 * at + 1])
    x = x_ref[...]
    gate = dot(x, both_ref[:, :inner], 1, 0)
    up = dot(x, both_ref[:, inner:], 1, 0)
    sig = jax.nn.sigmoid(gate)
    act = gate * sig
    hid_ref[...] = (act * up).astype(BF16)
    grad_hidden = dot(visits.load(bits, cn_ref, cf_ref), down, 1, 1)
    dboth_ref[:, :inner] = (grad_hidden * up * (sig * (1.0 + gate * (1.0 - sig)))).astype(BF16)
    dboth_ref[:, inner:] = (grad_hidden * act).astype(BF16)
    visits.store_halves(ways, outs, dot(dboth_ref[...], both_ref[...], 1, 1).astype(BF16))


def pairs_of(values):
    return list(zip(values[::2], values[1::2]))


def feed_forward(spans, me_shard, rows, cots, bits, ways, both_w, near, far, waits=()):
    width, inner = both_w.shape[0], both_w.shape[1] // 2
    half = cots[0].shape[0]
    span = 2 * half // spans
    visits = Visits(spans, span)
    one = pl.Buffered(1)
    total = 2 * half
    part = width // len(ways)
    flat = [x for pair in rows for x in pair]
    hidden, grads, x_all, *parts = call(
        functools.partial(feed_kernel, visits, bits, ways),
        out_shape=[shape(total, inner), shape(total, 2 * inner), shape(total, width)]
        + [shape(half, part)] * 2 * len(ways),
        prefetch=1,
        grid=(spans,),
        in_specs=[
            whole(both_w, pipeline_mode=one),
            whole(near, pipeline_mode=one),
            whole(far, pipeline_mode=one),
            *visits.specs(bits, width),
            *[spec for way in ways for spec in visits.specs(way, part)],
        ],
        out_specs=[
            visits.rows(bits, inner),
            visits.rows(bits, 2 * inner),
            visits.rows(bits, width),
            *[spec for way in ways for spec in visits.specs(way, part)],
        ],
        scratch=[pltpu.VMEM((2 * near.shape[0], *near.shape[1:]), BF16)],
        cost_estimate=cost(
            10 * total * width * inner, total * (6 * width + 6 * inner) + 6 * width * inner
        ),
        name="feed_forward",
        waits=waits,
    )(me_shard, both_w, near, far, *cots, *flat)
    return pairs_of(parts), hidden, grads, x_all


def feed_out_kernel(count, walk, shard_ref, near_ref, far_ref, *rest):
    hidden, outs, held = rest[:count], rest[count:-1], rest[-1]

    @pl.when(pl.program_id(0) == 0)
    def _():
        assemble(held, shard_ref[0] % 2, near_ref, far_ref)

    down = held[...].reshape(-1, held.shape[2])
    for at in range(count):
        walk.store(outs[2 * at], outs[2 * at + 1], dot(hidden[at][...], down, 1, 0).astype(BF16))


def feed_out(spans, me_shard, hidden, near, far, waits=()):
    total, inner = hidden[0].shape
    width = near.shape[2]
    walk = Walk(spans, total // spans, False)
    count = len(hidden)
    return pairs_of(
        call(
            functools.partial(feed_out_kernel, count, walk),
            out_shape=[shape(total // 2, width)] * 2 * count,
            prefetch=1,
            grid=(spans,),
            in_specs=[
                whole(near, pipeline_mode=pl.Buffered(1)),
                whole(far, pipeline_mode=pl.Buffered(1)),
                *[pl.BlockSpec((total // spans, inner), walk.both)] * count,
            ],
            out_specs=walk.specs(width) * count,
            scratch=[pltpu.VMEM((2 * near.shape[0], *near.shape[1:]), BF16)],
            cost_estimate=cost(
                2 * count * total * inner * width,
                2 * count * total * (inner + width) + 2 * inner * width,
            ),
            name="feed_out",
            waits=waits,
        )(me_shard, near, far, *hidden)
    )


def terms_of(*refs):
    sums = [a[...].astype(F32) + b[...].astype(F32) for a, b in zip(refs[::2], refs[1::2])]
    return sums[0] if len(sums) == 1 else jnp.concatenate(sums, axis=1)


def back_kernel(count, me_ref, resid_ref, cot_ref, gain_ref, w_ref, *rest):
    terms, (resid_grad_ref, branch_ref, *mixed) = rest[:count], rest[count:]
    rows = resid_ref[...]
    factor = lax.rsqrt(jnp.mean(rows * rows, axis=-1, keepdims=True) + epsilon)
    unit_rows = rows * factor
    scaled = terms_of(*terms) * gain_ref[...]
    mean_dot = jnp.mean(scaled * unit_rows, axis=-1, keepdims=True)
    grad = cot_ref[...].astype(F32) + factor * (scaled - unit_rows * mean_dot)
    resid_grad_ref[...] = grad
    branch = grad.astype(BF16)
    branch_ref[...] = branch
    for at, out in enumerate(mixed):
        out[...] = dot(branch, w_ref[jnp.bitwise_xor(me_ref[0], at)], 1, 1).astype(BF16)


def norm_out_back(seq, me, spans, parts, resid, cot, gain, w_out, waits=()):
    rows, width = resid.shape
    terms = [x for pair in parts for x in pair]
    out_shape = [shape(rows, width, dtype=F32), shape(rows, width)]
    out_shape += [shape(rows, w_out.shape[1])] * spans
    out = call(
        functools.partial(back_kernel, len(terms)),
        out_shape=out_shape,
        prefetch=1,
        in_specs=[whole(resid), pl.BlockSpec((None, rows, width), lambda *_: (seq, 0, 0))]
        + [whole(x) for x in (gain, w_out, *terms)],
        out_specs=[whole(x) for x in out_shape],
        cost_estimate=cost(2 * rows * width * width, rows * width * 16 + width * width * 2),
        name="norm_out_back",
        waits=waits,
    )(me, resid, cot, gain, w_out, *terms)
    return out[0], out[1], out[2:]


def grad_in_kernel(visits, ways, proj_ref, w_ref, *outs):
    visits.store_halves(ways, outs, dot(proj_ref[...], w_ref[...], 1, 1).astype(BF16))


def grad_into_rows(spans, proj_grad, bits, ways, w_in, waits=()):
    full, narrow = proj_grad.shape
    width = w_in.shape[0]
    visits = Visits(spans, full // spans)
    part = width // len(ways)
    parts = call(
        functools.partial(grad_in_kernel, visits, ways),
        out_shape=[shape(full // 2, part)] * 2 * len(ways),
        grid=(spans,),
        in_specs=[visits.rows(bits, narrow), whole(w_in, pipeline_mode=pl.Buffered(1))],
        out_specs=[spec for way in ways for spec in visits.specs(way, part)],
        cost_estimate=cost(2 * full * narrow * width, 2 * full * (narrow + width) + 2 * narrow * width),
        name="grad_into_rows",
        waits=waits,
    )(proj_grad, w_in)
    return pairs_of(parts)


def product_of(lefts, rights):
    total = None
    i = j = a = b = 0
    while i < len(lefts):
        size = min(lefts[i].shape[0] - a, rights[j].shape[0] - b)
        term = dot(lefts[i][a : a + size, :], rights[j][b : b + size, :], 0, 0)
        total = term if total is None else total + term
        a, b = a + size, b + size
        if a == lefts[i].shape[0]:
            i, a = i + 1, 0
        if b == rights[j].shape[0]:
            j, b = j + 1, 0
    return total


def row_sums(product):
    sums = jnp.sum(product, axis=1, keepdims=True)
    return jnp.broadcast_to(sums, (product.shape[0], LANES)).T[:8]


def weight_kernel(left_count, right_count, gain, *refs):
    lefts, rights = refs[:left_count], refs[left_count : left_count + right_count]
    rest = refs[left_count + right_count :]
    total = product_of(lefts, rights)
    if gain:
        w_ref, out_ref, gain_ref = rest
        gain_ref[...] = row_sums(total * w_ref[...].astype(F32))
    else:
        (out_ref,) = rest
    out_ref[...] = total.astype(BF16)


def weight_grad(lefts, rights, weight, name, waits=()):
    rows = lefts[0].shape[1]
    tile = 256
    columns = rights[0].shape[1]
    depth = sum(x.shape[0] for x in lefts)
    out_shape = [shape(rows, columns)]
    out_specs = [pl.BlockSpec((tile, columns), lambda i: (i, 0))]
    weights = () if weight is None else (weight,)
    if weights:
        out_shape.append(shape(8, rows, dtype=F32))
        out_specs.append(pl.BlockSpec((8, tile), lambda i: (0, i)))
    return call(
        functools.partial(weight_kernel, len(lefts), len(rights), bool(weights)),
        out_shape=out_shape,
        grid=(rows // tile,),
        in_specs=[pl.BlockSpec((x.shape[0], tile), lambda i: (0, i)) for x in lefts]
        + [whole(x, pipeline_mode=pl.Buffered(1)) for x in rights]
        + [pl.BlockSpec((tile, x.shape[1]), lambda i: (i, 0)) for x in weights],
        out_specs=out_specs,
        cost_estimate=cost(
            2 * depth * rows * columns, 2 * depth * (rows + columns) + 2 * rows * columns
        ),
        name=name,
        waits=waits,
    )(*lefts, *rights, *weights)


def in_weight_kernel(own, shards, left_count, me_ref, *refs):
    lefts, (*rights, w_ref, other_ref, near_ref, far_ref, gain_ref) = refs[:left_count], refs[left_count:]
    total = product_of(lefts, rights)
    gain = row_sums(total * w_ref[...].astype(F32))
    first = lax.broadcasted_iota(jnp.int32, gain.shape, 0) < 4
    gain_ref[...] = jnp.where(first, gain, other_ref[...])
    total = total.astype(BF16)
    steps = shards.bit_length() - 1
    count = total.shape[0] // own
    for at in range(count):
        apart = jnp.bitwise_xor(me_ref[0], pl.program_id(0) * count + at)
        where = 0
        for bit in range(steps):
            where = where * 2 + (apart >> bit) % 2
        piece = total[at * own : (at + 1) * own]

        @pl.when(where < shards // 2)
        def _():
            near_ref[where] = piece

        @pl.when(where >= shards // 2)
        def _():
            far_ref[where - shards // 2] = piece


def in_weight_grad(me, lefts, rights, weight, other_gain, own, shards, waits=()):
    rows, columns = weight.shape
    tile = math.lcm(own, LANES)
    depth = sum(x.shape[0] for x in lefts)
    half = shape(shards // 2, own, columns)
    out_shape = (half, half, shape(8, rows, dtype=F32))
    return call(
        functools.partial(in_weight_kernel, own, shards, len(lefts)),
        out_shape=out_shape,
        prefetch=1,
        grid=(rows // tile,),
        in_specs=[pl.BlockSpec((x.shape[0], tile), lambda i, _: (0, i)) for x in lefts]
        + [whole(x) for x in rights]
        + [pl.BlockSpec((tile, columns), lambda i, _: (i, 0)), pl.BlockSpec((8, tile), lambda i, _: (0, i))],
        out_specs=[whole(half), whole(half), pl.BlockSpec((8, tile), lambda i, _: (0, i))],
        cost_estimate=cost(
            2 * depth * rows * columns, 2 * depth * (rows + columns) + 2 * rows * columns
        ),
        name="in_weight_grad",
        waits=waits,
    )(me, *lefts, *rights, weight, other_gain)


def add_pairs(left, right):
    return (left.astype(F32) + right.astype(F32)).astype(BF16)


def halve_kernel(near_ref, got_ref, gain_ref, gain_got_ref, *rest):
    outs, gain_out = rest[:-1], rest[-1]
    total = (near_ref[...].astype(F32) + got_ref[...].astype(F32)).astype(BF16)
    cut = total.shape[0] // len(outs)
    for at, out in enumerate(outs):
        out[...] = total[at * cut : (at + 1) * cut]
    gain_out[...] = gain_ref[...] + gain_got_ref[...]


def halve(near, got, gain, gain_got, waits=()):
    parts = 2 if near.shape[0] > 1 else 1
    out_shape = [shape(near.shape[0] // parts, *near.shape[1:])] * parts + [gain]
    return call(
        halve_kernel,
        out_shape=[shape(*x.shape, dtype=x.dtype) for x in out_shape],
        in_specs=[whole(x) for x in (near, got, gain, gain_got)],
        out_specs=[whole(x) for x in out_shape],
        cost_estimate=cost(0, 6 * near.size),
        name="halve",
        waits=waits,
    )(near, got, gain, gain_got)


def across(value, bit):
    size = lax.axis_size("fsdp")
    return lax.ppermute(value, "fsdp", [(i, i ^ bit) for i in range(size)])


def arrange_kernel(copies, every_ref, *outs):
    for own in range(every_ref.shape[0]):
        for source, out, target, size in copies:
            begin = target(own)
            outs[out][:, begin : begin + size] = every_ref[own, :, source : source + size].astype(F32)


def arrange_halves_kernel(order, copies, me_ref, *rest):
    blocks, (out_ref, held) = rest[:-2], rest[-2:]
    for at, owner in enumerate(order):
        held[jnp.bitwise_xor(me_ref[0], owner)] = blocks[at][...]
    arrange_kernel(copies, held, out_ref)


def arrange_halves(me, near, far, bits, copies, width, name):
    order = order_of(bits)
    count = len(order) // 2
    rows, columns = near.shape[0] // count, near.shape[1]
    tile = rows // 2
    out_shape = shape(rows, width, dtype=F32)

    def block(at):
        return pl.BlockSpec((tile, columns), lambda i, _: (2 * at + i, 0))

    return call(
        functools.partial(arrange_halves_kernel, order, copies),
        out_shape=out_shape,
        prefetch=1,
        grid=(2,),
        in_specs=[block(at) for _ in range(2) for at in range(count)],
        out_specs=pl.BlockSpec((tile, width), lambda i, _: (i, 0)),
        scratch=[pltpu.VMEM((len(order), tile, columns), BF16)],
        cost_estimate=cost(0, 6 * rows * width),
        name=name,
    )(me, *[near] * count, *[far] * count)


def arrange_blocks_kernel(order, copies, me_ref, *rest):
    blocks, outs, held = rest[: len(order)], rest[len(order) : -1], rest[-1]
    for at, owner in enumerate(order):
        held[jnp.bitwise_xor(me_ref[0], owner)] = blocks[at][...]
    arrange_kernel(copies, held, *outs)


def arrange_blocks(me, blocks, bits, copies, widths, name):
    rows, columns = blocks[0].shape
    tile = rows // 2
    order = order_of(bits)
    out_shape = [shape(rows, width, dtype=F32) for width in widths]
    return call(
        functools.partial(arrange_blocks_kernel, order, copies),
        out_shape=out_shape,
        prefetch=1,
        grid=(2,),
        in_specs=[pl.BlockSpec((tile, columns), lambda i, _: (i, 0))] * len(blocks),
        out_specs=[pl.BlockSpec((tile, width), lambda i, _: (i, 0)) for width in widths],
        scratch=[pltpu.VMEM((len(blocks), tile, columns), BF16)],
        cost_estimate=cost(0, 6 * rows * sum(widths)),
        name=name,
    )(me, *blocks)


def widen_rows_kernel(every_ref, out_ref):
    out_ref[...] = every_ref[...].astype(F32)


def to_float(value, name, waits=()):
    rows, width = value.shape
    tile = rows // 4 if rows % 64 == 0 else rows
    spec = pl.BlockSpec((tile, width), lambda i: (i, 0))
    return call(
        widen_rows_kernel,
        out_shape=shape(rows, width, dtype=F32),
        grid=(rows // tile,),
        in_specs=[spec],
        out_specs=spec,
        cost_estimate=cost(0, 6 * value.size),
        name=name,
        waits=waits,
    )(value)


def add_kernel(left_ref, right_ref, out_ref):
    out_ref[...] = left_ref[...].astype(F32) + right_ref[...].astype(F32)


def add_float(left, right):
    rows, width = left.shape
    tile = rows // 2
    spec = pl.BlockSpec((tile, width), lambda i: (i, 0))
    return call(
        add_kernel,
        out_shape=shape(rows, width, dtype=F32),
        grid=(2,),
        in_specs=[spec, spec],
        out_specs=spec,
        cost_estimate=cost(0, 8 * left.size),
        name="add_float",
    )(left, right)


def gains_kernel(left_ref, right_ref, first_norm, second_norm, first_ref, second_ref):
    total = left_ref[...] + right_ref[...]
    first_ref[...] = total[0:1] / first_norm[...]
    second_ref[...] = total[4:5] / second_norm[...]


def finish_gains(left, right, first_norm, second_norm):
    out_shape = [shape(1, left.shape[1], dtype=F32)] * 2
    return call(
        gains_kernel,
        out_shape=out_shape,
        in_specs=[whole(x) for x in (left, right, first_norm, second_norm)],
        out_specs=[whole(x) for x in out_shape],
        cost_estimate=cost(0, 8 * left.size),
        name="finish_gains",
    )(left, right, first_norm, second_norm)


def block_out_kernel(count, seqs, *refs):
    out_ref = refs[-1]
    for seq in range(seqs):
        resid_ref, *terms = refs[count * seq : count * (seq + 1)]
        out_ref[seq] = (resid_ref[...] + terms_of(*terms)).astype(BF16)


def finish_block_out(resid, terms, waits=()):
    rows, width = resid[0].shape
    out_shape = shape(len(resid), rows, width)
    flat = [y for q in range(len(resid)) for y in (resid[q], *[x for pair in terms[q] for x in pair])]
    count = len(flat) // len(resid)
    return call(
        functools.partial(block_out_kernel, count, len(resid)),
        out_shape=out_shape,
        in_specs=[whole(x) for x in flat],
        out_specs=whole(out_shape),
        cost_estimate=cost(0, 12 * out_shape.size),
        name="finish_block_out",
        waits=waits,
    )(*flat)


def tokens_grad_kernel(count, seqs, tokens_ref, gain_ref, *refs):
    out_ref = refs[-1]
    for seq in range(seqs):
        resid_ref, *terms = refs[count * seq : count * (seq + 1)]
        rows = tokens_ref[seq].astype(F32)
        factor = lax.rsqrt(jnp.mean(rows * rows, axis=-1, keepdims=True) + epsilon)
        unit_rows = rows * factor
        scaled = terms_of(*terms) * gain_ref[...]
        mean_dot = jnp.mean(scaled * unit_rows, axis=-1, keepdims=True)
        out_ref[seq] = (resid_ref[...] + factor * (scaled - unit_rows * mean_dot)).astype(BF16)


def finish_tokens_grad(tokens, gain, grad_resid, terms, waits=()):
    out_shape = shape(*tokens.shape)
    flat = [
        y for q in range(len(grad_resid)) for y in (grad_resid[q], *[x for pair in terms[q] for x in pair])
    ]
    count = len(flat) // len(grad_resid)
    return call(
        functools.partial(tokens_grad_kernel, count, len(grad_resid)),
        out_shape=out_shape,
        in_specs=[whole(x) for x in (tokens, gain, *flat)],
        out_specs=whole(out_shape),
        cost_estimate=cost(0, 12 * out_shape.size),
        name="finish_tokens_grad",
        waits=waits,
    )(tokens, gain, *flat)


def join_kernel(chips, me_ref, *refs):
    blocks, out_ref = refs[:-1], refs[-1]
    chip = me_ref[0] // 2
    for back in range(chips):
        out_ref[lax.rem(chip - back + chips, chips)] = blocks[back][...]


def join(me, blocks, waits=()):
    rows, width = blocks[0].shape
    out_shape = shape(len(blocks), rows, width)
    return call(
        functools.partial(join_kernel, len(blocks)),
        out_shape=out_shape,
        prefetch=1,
        in_specs=[whole(x) for x in blocks],
        out_specs=whole(out_shape),
        cost_estimate=cost(0, 4 * out_shape.size),
        name="join",
        waits=waits,
    )(me, *blocks)


def out_weight_kernel(spans, seqs, me_ref, *refs):
    mixed, branches, out_ref = refs[: spans * seqs], refs[spans * seqs : -1], refs[-1]
    for at in range(spans):
        total = None
        for seq in range(seqs):
            term = dot(mixed[seq * spans + at][...], branches[seq][...], 0, 0)
            total = term if total is None else total + term
        out_ref[jnp.bitwise_xor(me_ref[0], at)] = total.astype(BF16)


def out_weight_grad(me, mixed, branches, waits=()):
    flat = [x for group in mixed for x in group]
    narrow, width = flat[0].shape[1], branches[0].shape[1]
    out_shape = shape(len(mixed[0]), narrow, width)
    return call(
        functools.partial(out_weight_kernel, len(mixed[0]), len(branches)),
        out_shape=out_shape,
        prefetch=1,
        in_specs=[whole(x) for x in (*flat, *branches)],
        out_specs=whole(out_shape),
        cost_estimate=cost(2 * len(flat) * flat[0].size * width, 2 * len(mixed[0]) * narrow * width),
        name="out_weight_grad",
        waits=waits,
    )(me, *flat, *branches)


def turning_tables(positions):
    frequency = jnp.exp(
        jnp.arange(HALF, dtype=F32) * (-2.0 * math.log(rope_base) / HEAD_DIMENSION)
    )
    angles = positions.astype(F32)[:, :, None] * frequency
    cosine, sine = jnp.cos(angles), jnp.sin(angles)
    empty = jnp.zeros((*positions.shape, 64 - HALF), F32)
    return (
        jnp.concatenate([cosine, empty, cosine, empty], axis=-1),
        jnp.concatenate([-sine, empty, sine, empty], axis=-1),
    )


def body(
    tokens,
    joined_input_weight,
    out_projection,
    gate_weight,
    up_weight,
    down_weight,
    norm_first,
    norm_second,
    positions,
    cotangent,
):
    seqs, span, width = tokens.shape
    spans = lax.axis_size("seq")
    shards = lax.axis_size("fsdp")
    chips = shards // 2
    me = jnp.full((1,), lax.axis_index("seq"), jnp.int32)
    me_shard = jnp.full((1,), lax.axis_index("fsdp"), jnp.int32)
    full = positions.shape[1]
    pairs = KEY_VALUE_HEADS // spans
    repeat = QUERY_HEAD_COUNT // KEY_VALUE_HEADS
    unit = repeat + 2
    query_columns = QUERY_HEAD_COUNT * HEAD_DIMENSION
    pair_columns = KEY_VALUE_HEADS * HEAD_DIMENSION
    query_slab = query_columns // spans
    pair_slab = pair_columns // spans
    own_rows = joined_input_weight.shape[0]
    piece = FF // (shards * spans)
    inner = shards * piece
    step = min(256, full)
    pad = jnp.asarray(pad_matrix(pairs, repeat), BF16)
    place = jnp.asarray(place_matrix(pairs, repeat), BF16)
    gain_in, gain_mid = norm_first[None, :], norm_second[None, :]
    upward = tuple(range(spans.bit_length() - 1))
    orders = [(upward[::-1], upward)[q % 2] for q in range(seqs)]
    both = range(seqs)
    del CHAIN[:]

    def gather(shard):
        return lax.all_gather(shard, "fsdp", axis=0, tiled=True)

    def owned(value):
        return lax.psum_scatter(value, "fsdp", scatter_dimension=0, tiled=True)

    ways = (upward[::-1], upward)

    def flat(pairs):
        return tuple(x for pair in pairs for x in pair)

    def copied(value, bits):
        held = [value]
        for bit in bits:
            held = held + [swap(x, bit) for x in held]
        return held

    in_shard = cut_in(me, joined_input_weight, spans, (query_slab, pair_slab, pair_slab))
    w_in = gather(in_shard)
    w_out = gather(out_projection).reshape(spans, query_slab, width)
    cot_rows = split_rows(cotangent)
    cot_got = gather_start(cot_rows, orders)
    normed = norm_rows(tokens, gain_in)
    x_got = gather_start(normed, orders)
    both_shard, down_shard = cut_feed(
        me, gate_weight, up_weight, down_weight, spans, shards, piece, ()
    )
    w_both = gather(both_shard)
    down_blocks = [down_shard, around(down_shard)]

    def pass_on():
        if len(down_blocks) < chips:
            down_blocks[-1:] = pin(down_blocks[-1])
            down_blocks.append(around(down_blocks[-1]))

    cosine, sine = turning_tables(positions)
    starts = (jnp.arange(full, dtype=jnp.int32)[None, :] - positions)[:, None, :]
    x_in = gather_end(normed, x_got, orders, "stack_in")
    pass_on()
    w_wide = widen(w_in, pad)
    pass_on()

    projected, mixed, lse, resid, x_mid = [], [], [], [], []

    def project_rows(q, waits=()):
        rows, *normed_mid = project_out(q, me, mixed[q], w_out, tokens, gain_mid, ways, waits)
        resid.append(rows)
        return normed_mid, gather_start(normed_mid, ways)

    for q in both:
        projected.append(
            project_in(
                me, x_in[q], orders[q], w_wide, cosine[q], sine[q], unit, x_in[-1] if q == 0 else ()
            )
        )
        if q == 0:
            cots = gather_end(cot_rows, cot_got, orders, "stack_cot")
            pass_on()
        if q == 1:
            started = [project_rows(0, flat(cots) if OPTIONS[0] == 0 else ())]
        heads, sums = attention_forward(me, projected[q], starts[q], place, spans, repeat, step)
        lse.append(sums)
        mixed.append(shared(heads))
        if q == 0:
            while len(down_blocks) < chips:
                pass_on()
            down_near = join(me_shard, down_blocks)
            down_far = beside(down_near)
    x_mid.append(gather_end(*started[0], ways, "stack_mid"))
    for q in both[1:]:
        started.append(project_rows(q, (down_far,) if OPTIONS[0] != 1 else (down_far, *flat(cots))))
    for q in both[1:]:
        x_mid.append(gather_end(*started[q], ways, "stack_mid"))

    hidden, grad_both, grad_mid, x_all = [], [], [], []
    for q in both:
        parts, kept, grads, rows = feed_forward(
            spans, me_shard, x_mid[q], cots[q], orders[q], ways, w_both, down_near, down_far
        )
        hidden.append(kept)
        grad_both.append(grads)
        x_all.append(rows)
        grad_mid.append(scatter_start(parts, ways))

    grad_resid, branches, head_grads = [], [], []

    def norm_back(q, waits=()):
        rows, branch, heads = norm_out_back(
            q, me, spans, grad_mid[q], resid[q], cotangent, gain_mid, w_out, waits
        )
        grad_resid.append(rows)
        branches.append(branch)
        head_grads.append(shared(heads))

    grad_mid[0] = scatter_end(*grad_mid[0], ways)
    both_part, gain_second = weight_grad(x_all, grad_both, w_both, "gate_up_grad")
    both_own = owned(both_part)
    norm_back(0)
    for q in both[1:]:
        grad_mid[q] = scatter_end(*grad_mid[q], ways)
    outs = scatter_start(
        feed_out(spans, me_shard, hidden, down_near, down_far, tuple(head_grads[0][1:])), orders
    )
    for q in both[1:]:
        norm_back(q)
    for at in (0, 1) if OPTIONS[5] == 0 else (1, 0):
        if at == 0:
            out_part = out_weight_grad(me, mixed, branches).reshape(query_columns, width)
            out_own = owned(out_part)
        else:
            (down_part,) = weight_grad(hidden, flat(cots), None, "down_grad")
            down_own = owned(down_part)

    proj_grads, grad_in = [], []
    for q in both:
        proj_grads.append(
            attention_backward(
                me,
                projected[q],
                starts[q],
                place,
                head_grads[q],
                orders[q],
                lse[q],
                cosine[q],
                sine[q],
                pad,
                repeat,
                step,
            )
        )
        if q == 0:
            if OPTIONS[4] == 0:
                outs = scatter_end(*outs, orders)
            both_every = copied(both_own, ways[0])
        if q == seqs - 1:
            for p in both[:-1]:
                grad_in[p] = scatter_end(*grad_in[p], ways)
            in_near, in_far, in_gain = in_weight_grad(
                me_shard,
                flat(x_in),
                proj_grads,
                w_in,
                gain_second,
                own_rows,
                shards,
                ((*flat(outs), both_every[1]), flat(outs), (both_every[1],), ())[OPTIONS[3]],
            )
            in_got, gain_got = across(in_far, 1), across(in_gain, 1)
        waits = tuple(x for group in head_grads[1:] for x in group[1:]) if q == 0 else (flat(grad_in[0]) if OPTIONS[2] == 0 else ())
        parts = grad_into_rows(spans, proj_grads[q], orders[q], ways, w_in, waits)
        grad_in.append(scatter_start(parts, ways))
        if q == 0 and OPTIONS[4] == 1:
            outs = scatter_end(*outs, orders)
    (down_own,) = pin(down_own)
    down_every = lax.all_gather(down_own, "seq", axis=0, tiled=True)
    in_near, in_sent, in_gain = halve(in_near, in_got, in_gain, gain_got, tuple(both_every) if OPTIONS[1] == 0 else ())
    in_got, gain_got = across(in_sent, 2), across(in_gain, 2)
    copies = [
        (part * inner + shard * piece, part, lambda own, shard=shard: (shard * spans + own) * piece, piece)
        for part in range(2)
        for shard in range(shards)
    ]
    sums = [out_own]

    def out_start(bit):
        sums[:] = pin(*sums)
        total = sums[0] if len(sums) == 1 else add_pairs(*sums)
        sums[:] = [total, swap(total, bit)]

    if OPTIONS[7] == 0:
        out_start(0)
    block_out = finish_block_out(resid, [[pair] for pair in outs])
    if OPTIONS[6] == 1:
        grad_in[-1] = scatter_end(*grad_in[-1], ways)
    bit = 4
    while in_near.shape[0] > 1:
        in_near, in_sent, in_gain = halve(in_near, in_got, in_gain, gain_got)
        in_got, gain_got = across(in_sent, bit), across(in_gain, bit)
        bit *= 2
    if OPTIONS[6] == 0:
        grad_in[-1] = scatter_end(*grad_in[-1], ways)
    in_own, in_gain = halve(in_near, in_got, in_gain, gain_got)
    in_every = [in_own[0]]
    out_start(0 if OPTIONS[7] else 1)
    for bit in upward:
        got = [swap(x, bit) for x in in_every]
        gain_got = swap(in_gain, bit)
        if bit == 0:
            tokens_grad = finish_tokens_grad(tokens, gain_in, grad_resid, grad_in)
        if bit + 1 < len(upward):
            *got, gain_got = pin(*got, gain_got)
        in_every = in_every + got
        if bit + 1 < len(upward):
            in_gain = in_gain + gain_got
    for bit in upward[1 if OPTIONS[7] else 2 :]:
        out_start(bit)
    if OPTIONS[7] == 0:
        out_grad = add_float(*sums)
    gate_grad, up_grad = arrange_blocks(me, both_every, ways[0], copies, (FF, FF), "arrange_gate_up")
    down_grad = to_float(down_every, "down_to_float")
    if OPTIONS[7]:
        out_grad = add_float(*sums)
    copies = [
        (0, 0, lambda own: own * query_slab, query_slab),
        (query_slab, 0, lambda own: query_columns + own * pair_slab, pair_slab),
        (
            query_slab + pair_slab,
            0,
            lambda own: query_columns + pair_columns + own * pair_slab,
            pair_slab,
        ),
    ]
    (in_grad,) = arrange_blocks(
        me,
        in_every,
        upward,
        copies,
        (query_columns + 2 * pair_columns,),
        "arrange_in",
    )
    first_gain, second_gain = finish_gains(in_gain, gain_got, gain_in, gain_mid)
    return (
        block_out,
        tokens_grad,
        in_grad,
        out_grad,
        gate_grad,
        up_grad,
        down_grad,
        first_gain.reshape(width),
        second_gain.reshape(width),
    )


def solution(mesh):
    return jax.shard_map(
        body,
        mesh=mesh,
        in_specs=(
            P("fsdp", "seq", None),
            P("fsdp", None),
            P("fsdp", None),
            P("fsdp", None),
            P("fsdp", None),
            P("fsdp", None),
            P(),
            P(),
            P("fsdp", None),
            P("fsdp", "seq", None),
        ),
        out_specs=(
            P("fsdp", "seq", None),
            P("fsdp", "seq", None),
            P("fsdp", None),
            P("fsdp", None),
            P("fsdp", None),
            P("fsdp", None),
            P("fsdp", None),
            P(),
            P(),
        ),
        check_vma=False,
    )
```

```python
import functools
import math

import jax
import jax.numpy as jnp
import numpy as np
from jax import lax
from jax.experimental import pallas as pl
from jax.experimental.pallas import tpu as pltpu
from jax.sharding import PartitionSpec as P

FF = 4096
QUERY_HEAD_COUNT = 16
KEY_VALUE_HEADS = 8
HEAD_DIMENSION = 96
HALF = HEAD_DIMENSION // 2
LANES = 128

epsilon = 1e-05
rope_base = 100000.0
SCALING = 1.0 / math.sqrt(HEAD_DIMENSION)
LOG2E = 1.4426950408889634
BF16 = jnp.bfloat16
F32 = jnp.float32
MIB = 1024 * 1024
VMEM_LIMIT = 64
COST_SCALE = 20
WEIGHTS = {"norm_out_back": 2.5, "feed_out": 2.5}


def dot(a, b, ca, cb):
    return lax.dot_general(a, b, (((ca,), (cb,)), ((), ())), preferred_element_type=F32)


def params(limit):
    return pltpu.CompilerParams(vmem_limit_bytes=limit * MIB)


def cost(flops, moved, trans=0):
    return int(flops), int(moved)


def weighted(estimate, name):
    scale = WEIGHTS.get(name, COST_SCALE)
    return pl.CostEstimate(
        flops=int(estimate[0] * scale), bytes_accessed=int(estimate[1] * scale), transcendentals=0
    )


CHAIN = []


def call(kernel, *, out_shape, in_specs, out_specs, prefetch=0, grid=(1,), scratch=(), cost_estimate=None, name=None, waits=()):
    count = prefetch + len(in_specs)
    waits = (*waits, *CHAIN[-1:])

    def run(*refs):
        kernel(*refs[:count], *refs[count + len(waits) :])

    inner = pl.pallas_call(
        run,
        out_shape=out_shape,
        grid_spec=pltpu.PrefetchScalarGridSpec(
            num_scalar_prefetch=prefetch,
            grid=grid,
            in_specs=[*in_specs, *[pl.BlockSpec(memory_space=pltpu.HBM)] * len(waits)],
            out_specs=out_specs,
            scratch_shapes=list(scratch),
        ),
        compiler_params=params(VMEM_LIMIT),
        cost_estimate=weighted(cost_estimate, name),
        name=name,
    )

    def made(*args):
        out = inner(*args, *waits)
        CHAIN.append(out[-1] if isinstance(out, (list, tuple)) else out)
        return out

    return made


def pin(*values):
    waits = tuple(CHAIN[-1:])
    count = len(values)
    hbm = pl.BlockSpec(memory_space=pltpu.HBM)
    out = pl.pallas_call(
        lambda *refs: None,
        out_shape=[shape(*x.shape, dtype=x.dtype) for x in values],
        in_specs=[hbm] * (count + len(waits)),
        out_specs=[hbm] * count,
        input_output_aliases={at: at for at in range(count)},
        cost_estimate=weighted(cost(0, 0), "pin"),
        name="pin",
    )(*values, *waits)
    CHAIN.append(out[-1])
    return out


def whole(array, **extra):
    return pl.BlockSpec(array.shape, lambda *_: (0,) * len(array.shape), **extra)


def shape(*sizes, dtype=BF16):
    return jax.ShapeDtypeStruct(sizes, dtype)


def pad_matrix(pairs, repeat):
    unit = repeat + 2
    out = np.zeros((pairs * unit * HEAD_DIMENSION, pairs * unit * LANES), np.float32)
    for g in range(pairs):
        for r in range(unit):
            if r < repeat:
                src = (g * repeat + r) * HEAD_DIMENSION
            else:
                src = (pairs * repeat + (r - repeat) * pairs + g) * HEAD_DIMENSION
            dst = (g * unit + r) * LANES
            for j in range(HEAD_DIMENSION):
                lane = j if (r == unit - 1 or j < HALF) else 64 + j - HALF
                out[src + j, dst + lane] = 1.0
    return out


def place_matrix(pairs, repeat):
    out = np.zeros((pairs, repeat * LANES, pairs * repeat * HEAD_DIMENSION), np.float32)
    for g in range(pairs):
        for r in range(repeat):
            for j in range(HEAD_DIMENSION):
                out[g, r * LANES + j, (g * repeat + r) * HEAD_DIMENSION + j] = 1.0
    return out


def order_of(bits):
    owners = [0]
    for bit in bits:
        owners = owners + [at ^ (1 << bit) for at in owners]
    return owners


def swap(value, bit):
    size = lax.axis_size("seq")
    return lax.ppermute(value, "seq", [(i, i ^ (1 << bit)) for i in range(size)])


def exchange(value, other):
    size = lax.axis_size("seq")
    return lax.ppermute(value, "seq", [(i, i ^ other) for i in range(size)])


def shared(heads):
    return [heads[0]] + [exchange(heads[at], at) for at in range(1, len(heads))]


def around(value):
    size = lax.axis_size("fsdp")
    return lax.ppermute(value, "fsdp", [(i, (i + 2) % size) for i in range(size)])


def beside(value):
    size = lax.axis_size("fsdp")
    return lax.ppermute(value, "fsdp", [(i, i ^ 1) for i in range(size)])


def copy_kernel(source_ref, *outs):
    for at, ref in enumerate(outs):
        ref[...] = source_ref[at]


def split_rows(value, waits=()):
    seqs, span, width = value.shape
    out_shape = [shape(span, width)] * seqs
    return call(
        copy_kernel,
        out_shape=out_shape,
        in_specs=[whole(value)],
        out_specs=[whole(x) for x in out_shape],
        cost_estimate=cost(0, 4 * value.size),
        name="split_rows",
        waits=waits,
    )(value)


def stack_kernel(*refs):
    count = len(refs) // 3
    for at in range(count):
        first, second, out = refs[2 * at], refs[2 * at + 1], refs[2 * count + at]
        rows = first.shape[0]
        out[:rows] = first[...]
        out[rows:] = second[...]


def stack_rows(pairs, name, waits=()):
    out_shape = [shape(2 * a.shape[0], a.shape[1]) for a, _ in pairs]
    flat = [x for pair in pairs for x in pair]
    return call(
        stack_kernel,
        out_shape=out_shape,
        in_specs=[whole(x) for x in flat],
        out_specs=[whole(x) for x in out_shape],
        cost_estimate=cost(0, 4 * sum(x.size for x in flat)),
        name=name,
        waits=waits,
    )(*flat)


def gather_start(blocks, orders):
    return [swap(x, bits[0]) for x, bits in zip(blocks, orders)]


def gather_end(blocks, got, orders, name, waits=()):
    held = list(zip(blocks, got))
    for level in range(1, len(orders[0])):
        joined = stack_rows(held, name, waits if level == 1 else ())
        held = [(x, swap(x, bits[level])) for x, bits in zip(joined, orders)]
    return held


def fold_kernel(*refs):
    count = len(refs) // 4
    for at in range(count):
        near, got, keep, send = refs[at], refs[count + at], refs[2 * count + at], refs[3 * count + at]
        total = near[...].astype(F32) + got[...].astype(F32)
        cut = total.shape[0] // 2
        keep[...] = total[:cut]
        send[...] = total[cut:].astype(BF16)


def fold(near, got, waits=()):
    out_shape = [shape(x.shape[0] // 2, x.shape[1], dtype=F32) for x in near]
    out_shape += [shape(x.shape[0] // 2, x.shape[1]) for x in near]
    out = call(
        fold_kernel,
        out_shape=out_shape,
        in_specs=[whole(x) for x in (*near, *got)],
        out_specs=[whole(x) for x in out_shape],
        cost_estimate=cost(0, 5 * sum(x.size for x in near)),
        name="fold",
        waits=waits,
    )(*near, *got)
    return out[: len(near)], out[len(near) :]


def scatter_start(parts, orders):
    return [near for near, _ in parts], [swap(far, bits[-1]) for (_, far), bits in zip(parts, orders)]


def scatter_end(near, got, orders, waits=()):
    for level in range(len(orders[0]) - 2, -1, -1):
        near, sent = fold(near, got, waits)
        got = [swap(x, bits[level]) for x, bits in zip(sent, orders)]
    return list(zip(near, got))


def norm_kernel(tokens_ref, gain_ref, *outs):
    for seq, out in enumerate(outs):
        rows = tokens_ref[seq].astype(F32)
        factor = lax.rsqrt(jnp.mean(rows * rows, axis=-1, keepdims=True) + epsilon)
        out[...] = (rows * factor * gain_ref[...]).astype(BF16)


def norm_rows(tokens, gain):
    seqs, span, width = tokens.shape
    out_shape = [shape(span, width)] * seqs
    return call(
        norm_kernel,
        out_shape=out_shape,
        in_specs=[whole(tokens), whole(gain)],
        out_specs=[whole(x) for x in out_shape],
        cost_estimate=cost(8 * tokens.size, 4 * tokens.size),
        name="norm_rows",
    )(tokens, gain)


def cut_in_kernel(spans, sizes, me_ref, w_ref, out_ref):
    for own in range(spans):

        @pl.when(me_ref[0] == own)
        def _():
            begin, put = 0, 0
            for size in sizes:
                out_ref[:, put : put + size] = w_ref[:, begin + own * size : begin + (own + 1) * size]
                begin, put = begin + spans * size, put + size


def cut_in(me, weight, spans, sizes):
    out_shape = shape(weight.shape[0], sum(sizes))
    return call(
        functools.partial(cut_in_kernel, spans, sizes),
        out_shape=out_shape,
        prefetch=1,
        in_specs=[whole(weight)],
        out_specs=whole(out_shape),
        cost_estimate=cost(0, 4 * weight.size),
        name="cut_in",
    )(me, weight)


def cut_feed_kernel(spans, shards, piece, me_ref, gate_ref, up_ref, down_ref, both_ref, out_ref):
    inner = shards * piece
    for own in range(spans):

        @pl.when(me_ref[0] == own)
        def _():
            for shard in range(shards):
                begin = (shard * spans + own) * piece
                put = shard * piece
                both_ref[:, put : put + piece] = gate_ref[:, begin : begin + piece]
                both_ref[:, inner + put : inner + put + piece] = up_ref[:, begin : begin + piece]
            out_ref[...] = down_ref[own * piece : (own + 1) * piece, :]


def cut_feed(me, gate, up, down, spans, shards, piece, waits):
    out_shape = (shape(gate.shape[0], 2 * shards * piece), shape(piece, down.shape[1]))
    return call(
        functools.partial(cut_feed_kernel, spans, shards, piece),
        out_shape=out_shape,
        prefetch=1,
        in_specs=[whole(x) for x in (gate, up, down)],
        out_specs=[whole(x) for x in out_shape],
        cost_estimate=cost(0, 4 * gate.size),
        name="cut_feed",
        waits=waits,
    )(me, gate, up, down)


def widen_kernel(w_ref, pad_ref, out_ref):
    out_ref[...] = dot(w_ref[...], pad_ref[...], 1, 0).astype(BF16)


def widen(w_slice, pad, waits=()):
    rows, narrow = w_slice.shape
    wide = pad.shape[1]
    out_shape = shape(rows, wide)
    return call(
        widen_kernel,
        out_shape=out_shape,
        in_specs=[whole(w_slice), whole(pad)],
        out_specs=whole(out_shape),
        cost_estimate=cost(2 * rows * narrow * wide, 2 * rows * (narrow + wide)),
        name="widen",
        waits=waits,
    )(w_slice, pad)


class Walk:
    def __init__(self, spans, span, near_first):
        self.cut, self.span, self.near_first = spans // 2, span, near_first

    def first(self, step):
        return jnp.minimum(step, self.cut - 1)

    def second(self, step):
        return jnp.maximum(step - self.cut, 0)

    def near(self, step, *_):
        return (self.first(step) if self.near_first else self.second(step), 0)

    def far(self, step, *_):
        return (self.second(step) if self.near_first else self.first(step), 0)

    def both(self, step, *_):
        return (step if self.near_first else lax.rem(step + self.cut, 2 * self.cut), 0)

    def specs(self, width):
        return [
            pl.BlockSpec((self.span, width), self.near),
            pl.BlockSpec((self.span, width), self.far),
        ]

    def is_near(self):
        early = pl.program_id(0) < self.cut
        return early if self.near_first else jnp.logical_not(early)

    def load(self, near_ref, far_ref):
        return jnp.where(self.is_near(), near_ref[...], far_ref[...])

    def store(self, near_ref, far_ref, value):
        near = self.is_near()

        @pl.when(near)
        def _():
            near_ref[...] = value

        @pl.when(jnp.logical_not(near))
        def _():
            far_ref[...] = value


def owner_at(order, index):
    owner = 0
    for at, value in enumerate(order):
        owner = jnp.where(index == at, value, owner)
    return owner


class Visits:
    def __init__(self, spans, span):
        self.spans, self.span = spans, span
        self.order = sorted(range(spans), key=lambda at: -bin(at).count("1"))

    def index(self, blocks):
        held = [blocks.get(owner) for owner in self.order]
        known = next(x for x in held if x is not None)
        for at, value in enumerate(held):
            known = held[at] = known if value is None else value
        return lambda step, *_: (owner_at(held, step), 0)

    def parts(self, bits):
        order = order_of(bits)
        cut = self.spans // 2
        near = {owner: at for at, owner in enumerate(order[:cut])}
        far = {owner: at for at, owner in enumerate(order[cut:])}
        return near, far

    def specs(self, bits, width):
        return [pl.BlockSpec((self.span, width), self.index(blocks)) for blocks in self.parts(bits)]

    def rows(self, bits, width):
        order = order_of(bits)
        return pl.BlockSpec(
            (self.span, width), self.index({owner: at for at, owner in enumerate(order)})
        )

    def is_near(self, bits):
        near, _ = self.parts(bits)
        flag = jnp.bool_(False)
        for at, owner in enumerate(self.order):
            if owner in near:
                flag = jnp.logical_or(flag, pl.program_id(0) == at)
        return flag

    def load(self, bits, near_ref, far_ref):
        return jnp.where(self.is_near(bits), near_ref[...], far_ref[...])

    def store(self, bits, near_ref, far_ref, value):
        near = self.is_near(bits)

        @pl.when(near)
        def _():
            near_ref[...] = value

        @pl.when(jnp.logical_not(near))
        def _():
            far_ref[...] = value

    def store_halves(self, ways, refs, value):
        columns = value.shape[1] // len(ways)
        for at, bits in enumerate(ways):
            part = value[:, at * columns : (at + 1) * columns]
            self.store(bits, refs[2 * at], refs[2 * at + 1], part)


def in_kernel(walk, unit, me_ref, w_ref, cos_ref, sin_ref, near_ref, far_ref, out_ref):
    rows = dot(walk.load(near_ref, far_ref), w_ref[...], 1, 0)
    cosine, sine = cos_ref[...], sin_ref[...]
    for part in range(rows.shape[1] // LANES):
        lanes = slice(part * LANES, (part + 1) * LANES)
        piece = rows[:, lanes]
        if part % unit != unit - 1:
            piece = piece * cosine + pltpu.roll(piece, 64, 1) * sine
        out_ref[:, lanes] = piece.astype(BF16)


def project_in(me, rows, bits, w_wide, cosine, sine, unit, waits=()):
    width, wide = w_wide.shape
    order = order_of(bits)
    spans = len(order)
    full = cosine.shape[0]
    span = full // spans
    walk = Walk(spans, span, True)

    def ordered(step, me_ref):
        return (jnp.bitwise_xor(me_ref[0], owner_at(order, step)), 0)

    return call(
        functools.partial(in_kernel, walk, unit),
        out_shape=shape(full, wide),
        prefetch=1,
        grid=(spans,),
        in_specs=[
            whole(w_wide, pipeline_mode=pl.Buffered(1)),
            pl.BlockSpec((span, LANES), ordered),
            pl.BlockSpec((span, LANES), ordered),
            *walk.specs(width),
        ],
        out_specs=pl.BlockSpec((span, wide), ordered),
        cost_estimate=cost(2 * full * width * wide, 2 * full * (width + wide) + 2 * width * wide),
        name="project_in",
        waits=waits,
    )(me, w_wide, cosine, sine, *rows)


def mask_of(scores, first_key, first_row, starts, repeat, diagonal):
    keys = lax.broadcasted_iota(jnp.int32, scores.shape, 0) + first_key
    allowed = keys >= starts
    if diagonal:
        step = scores.shape[1] // repeat
        rows = lax.broadcasted_iota(jnp.int32, scores.shape, 1) % step + first_row
        allowed = allowed & (keys <= rows)
    return jnp.where(allowed, scores, -1e30)


def query_of(proj_ref, rows, repeat):
    return jnp.concatenate(
        [proj_ref[rows, r * LANES : (r + 1) * LANES] for r in range(repeat)], axis=0
    )


def forward_kernel(spans, step, repeat, me_ref, proj_ref, start_ref, place_ref, *rest):
    outs, lse_ref, held = rest[:spans], rest[spans], rest[spans + 1]
    full = proj_ref.shape[0]
    span = full // spans
    pair = pl.program_id(0)
    me = me_ref[0]
    value_t = proj_ref[:, (repeat + 1) * LANES :].T
    starts = start_ref[...]

    @pl.when(pair == 0)
    def _():
        held[...] = jnp.zeros_like(held)

    for block in range(full // step):
        begin, end = block * step, (block + 1) * step
        rows = slice(begin, end)
        query = query_of(proj_ref, rows, repeat)
        starts_now = jnp.concatenate([starts[:, rows]] * repeat, axis=1)
        pieces = []
        for key_block in range(block + 1):
            first = key_block * step
            key = proj_ref[first : first + step, repeat * LANES : (repeat + 1) * LANES]
            scores = dot(key, query, 1, 1) * (SCALING * LOG2E)
            pieces.append(mask_of(scores, first, begin, starts_now, repeat, key_block == block))
        top = functools.reduce(jnp.maximum, [jnp.max(p, axis=0, keepdims=True) for p in pieces])
        total = None
        summed = None
        for key_block in range(block + 1):
            first = key_block * step
            raised = jnp.exp2(pieces[key_block] - top)
            part = jnp.sum(raised, axis=0, keepdims=True)
            mixed = dot(value_t[:, first : first + step], raised.astype(BF16), 1, 0)
            total = part if total is None else total + part
            summed = mixed if summed is None else summed + mixed
        mixed_t = (summed * (1.0 / total)).astype(BF16)
        lse_ref[block : block + 1, :] = top + jnp.log2(total)
        wide = None
        for r in range(repeat):
            term = dot(
                mixed_t[:, r * step : (r + 1) * step],
                place_ref[r * LANES : (r + 1) * LANES, :],
                0,
                0,
            )
            wide = term if wide is None else wide + term
        wide = wide.astype(BF16)
        for piece in range(step // span):
            at = jnp.bitwise_xor(me, block * (step // span) + piece)
            held[at] = held[at] + wide[piece * span : (piece + 1) * span]

    @pl.when(pair == pl.num_programs(0) - 1)
    def _():
        for at in range(spans):
            outs[at][...] = held[at]


def attention_forward(me, proj, starts, place, spans, repeat, step, waits=()):
    full, wide = proj.shape
    pairs, _, narrow = place.shape
    group = wide // pairs
    span = full // spans
    work = pairs * repeat * full * full
    out_shape = [jax.ShapeDtypeStruct((span, narrow), BF16)] * spans
    out_shape.append(jax.ShapeDtypeStruct((pairs, full // step, repeat * step), F32))
    *mixed, lse = call(
        functools.partial(forward_kernel, spans, step, repeat),
        out_shape=out_shape,
        prefetch=1,
        grid=(pairs,),
        in_specs=[
            pl.BlockSpec((full, group), lambda j, _: (0, j)),
            pl.BlockSpec((1, full), lambda j, _: (0, 0)),
            pl.BlockSpec((None, repeat * LANES, narrow), lambda j, _: (j, 0, 0)),
        ],
        out_specs=[whole(x) for x in out_shape[:-1]]
        + [pl.BlockSpec((None, full // step, repeat * step), lambda j, _: (j, 0, 0))],
        scratch=[pltpu.VMEM((spans, span, narrow), BF16)],
        cost_estimate=cost(2 * work * 256, 2 * proj.size * 2, work),
        name="attention_forward",
        waits=waits,
    )(me, proj, starts, place)
    return mixed, lse


def backward_kernel(
    order, step, repeat, me_ref, proj_ref, start_ref, place_ref, lse_ref, cos_ref, sin_ref, pad_ref, *rest
):
    spans = len(order)
    grads, (out_ref, key_acc, value_acc, held) = rest[:spans], rest[spans:]
    full = proj_ref.shape[0]
    span = full // spans
    pair = pl.program_id(0)
    me = me_ref[0]
    key_t = proj_ref[:, repeat * LANES : (repeat + 1) * LANES].T
    starts = start_ref[...]
    key_acc[...] = jnp.zeros_like(key_acc)
    value_acc[...] = jnp.zeros_like(value_acc)

    @pl.when(pair == 0)
    def _():
        for at in range(spans):
            held[jnp.bitwise_xor(me, at)] = grads[at][...]
        out_ref[...] = jnp.zeros_like(out_ref)

    def turn_back(grad, rows):
        grad = grad.astype(BF16).astype(F32)
        return (grad * cos_ref[rows, :] - pltpu.roll(grad, 64, 1) * sin_ref[rows, :]).astype(BF16)

    def put(begin, wide):
        for at in range(0, wide.shape[0], span):
            owner = jnp.bitwise_xor(me, (begin + at) // span)
            where = 0
            for index, value in enumerate(order):
                where = jnp.where(owner == value, index, where)
            here = pl.ds(pl.multiple_of(where * span, span), span)
            out_ref[here, :] = out_ref[here, :] + wide[at : at + span]

    for block in range(full // step):
        begin, end = block * step, (block + 1) * step
        rows = slice(begin, end)
        query = query_of(proj_ref, rows, repeat)
        grad_rows = jnp.concatenate(
            [held[at] for at in range(begin // span, end // span)], axis=0
        )
        grad = jnp.concatenate(
            [
                dot(grad_rows, place_ref[r * LANES : (r + 1) * LANES, :], 1, 1).astype(BF16)
                for r in range(repeat)
            ],
            axis=0,
        )
        starts_now = jnp.concatenate([starts[:, rows]] * repeat, axis=1)
        lse = lse_ref[block : block + 1, :]
        kept = []
        mean_dot = None
        for key_block in range(block + 1):
            first = key_block * step
            keys = slice(first, first + step)
            key = proj_ref[keys, repeat * LANES : (repeat + 1) * LANES]
            value = proj_ref[keys, (repeat + 1) * LANES :]
            scores = dot(key, query, 1, 1) * (SCALING * LOG2E)
            scores = mask_of(scores, first, begin, starts_now, repeat, key_block == block)
            shares = jnp.exp2(scores - lse)
            value_acc[keys, :] += dot(shares.astype(BF16), grad, 1, 0)
            product = shares * dot(value, grad, 1, 1)
            part = jnp.sum(product, axis=0, keepdims=True)
            mean_dot = part if mean_dot is None else mean_dot + part
            kept.append((shares, product))
        query_grad_t = None
        for key_block in range(block + 1):
            first = key_block * step
            keys = slice(first, first + step)
            shares, product = kept[key_block]
            score_grad = (SCALING * (product - shares * mean_dot)).astype(BF16)
            key_acc[keys, :] += dot(score_grad, query, 1, 0)
            term = dot(key_t[:, keys], score_grad, 1, 0)
            query_grad_t = term if query_grad_t is None else query_grad_t + term
        query_grad = query_grad_t.T
        wide = None
        for r in range(repeat):
            turned = turn_back(query_grad[r * step : (r + 1) * step], rows)
            term = dot(turned, pad_ref[:, r * LANES : (r + 1) * LANES], 1, 1)
            wide = term if wide is None else wide + term
        put(begin, wide.astype(BF16))
    for block in range(full // step):
        rows = slice(block * step, (block + 1) * step)
        turned = turn_back(key_acc[rows, :], rows)
        wide = dot(turned, pad_ref[:, repeat * LANES : (repeat + 1) * LANES], 1, 1)
        wide += dot(value_acc[rows, :].astype(BF16), pad_ref[:, (repeat + 1) * LANES :], 1, 1)
        put(block * step, wide.astype(BF16))


def attention_backward(
    me, proj, starts, place, grads, bits, lse, cosine, sine, pad, repeat, step, waits=()):
    full, wide = proj.shape
    pairs, _, narrow = place.shape
    group = wide // pairs
    work = pairs * repeat * full * full
    out_shape = shape(full, pad.shape[0])
    return call(
        functools.partial(backward_kernel, order_of(bits), step, repeat),
        out_shape=out_shape,
        prefetch=1,
        grid=(pairs,),
        in_specs=[
            pl.BlockSpec((full, group), lambda j, _: (0, j)),
            pl.BlockSpec((1, full), lambda j, _: (0, 0)),
            pl.BlockSpec((None, repeat * LANES, narrow), lambda j, _: (j, 0, 0)),
            pl.BlockSpec((None, full // step, repeat * step), lambda j, _: (j, 0, 0)),
            whole(cosine),
            whole(sine),
            pl.BlockSpec((pad.shape[0], group), lambda j, _: (0, j)),
            *[whole(x) for x in grads],
        ],
        out_specs=whole(out_shape),
        scratch=[
            pltpu.VMEM((full, LANES), F32),
            pltpu.VMEM((full, LANES), F32),
            pltpu.VMEM((len(grads), full // len(grads), narrow), BF16),
        ],
        cost_estimate=cost(2 * work * 640, 2 * proj.size * 4, work),
        name="attention_backward",
        waits=waits,
    )(me, proj, starts, place, lse, cosine, sine, pad, *grads)


def out_kernel(spans, me_ref, w_ref, tokens_ref, gain_ref, *rest):
    mixed, (resid_ref, *parts) = rest[:spans], rest[spans:]
    summed = tokens_ref[...].astype(F32)
    for at in range(spans):
        summed += dot(mixed[at][...], w_ref[jnp.bitwise_xor(me_ref[0], at)], 1, 0)
    resid_ref[...] = summed
    factor = lax.rsqrt(jnp.mean(summed * summed, axis=-1, keepdims=True) + epsilon)
    normed = (summed * factor * gain_ref[...]).astype(BF16)
    columns = parts[0].shape[1]
    for at, part in enumerate(parts):
        part[...] = normed[:, at * columns : (at + 1) * columns]


def project_out(seq, me, mixed, w_out, tokens, gain, ways, waits=()):
    _, span, width = tokens.shape
    out_shape = [shape(span, width, dtype=F32)] + [shape(span, width // len(ways))] * len(ways)
    return call(
        functools.partial(out_kernel, len(mixed)),
        out_shape=out_shape,
        prefetch=1,
        in_specs=[
            whole(w_out),
            pl.BlockSpec((None, span, width), lambda *_: (seq, 0, 0)),
            whole(gain),
            *[whole(x) for x in mixed],
        ],
        out_specs=[whole(x) for x in out_shape],
        cost_estimate=cost(2 * span * width * width, span * width * 10 + width * width * 2),
        name="project_out",
        waits=waits,
    )(me, w_out, tokens, gain, *mixed)


def assemble(held, core, near_ref, far_ref):
    for chip in range(near_ref.shape[0]):
        held[2 * chip + core] = near_ref[chip]
        held[2 * chip + 1 - core] = far_ref[chip]


def feed_kernel(
    visits, bits, ways, shard_ref, both_ref, near_ref, far_ref, cn_ref, cf_ref, *rest
):
    count = 2 * len(ways)
    rows, (hid_ref, dboth_ref, x_ref, *outs), held = rest[:count], rest[count:-1], rest[-1]
    inner = both_ref.shape[1] // 2

    @pl.when(pl.program_id(0) == 0)
    def _():
        assemble(held, shard_ref[0] % 2, near_ref, far_ref)

    down = held[...].reshape(inner, held.shape[2])
    columns = rows[0].shape[1]
    for at, way in enumerate(ways):
        x_ref[:, at * columns : (at + 1) * columns] = visits.load(way, rows[2 * at], rows[2 * at + 1])
    x = x_ref[...]
    gate = dot(x, both_ref[:, :inner], 1, 0)
    up = dot(x, both_ref[:, inner:], 1, 0)
    sig = jax.nn.sigmoid(gate)
    act = gate * sig
    hid_ref[...] = (act * up).astype(BF16)
    grad_hidden = dot(visits.load(bits, cn_ref, cf_ref), down, 1, 1)
    dboth_ref[:, :inner] = (grad_hidden * up * (sig * (1.0 + gate * (1.0 - sig)))).astype(BF16)
    dboth_ref[:, inner:] = (grad_hidden * act).astype(BF16)
    visits.store_halves(ways, outs, dot(dboth_ref[...], both_ref[...], 1, 1).astype(BF16))


def pairs_of(values):
    return list(zip(values[::2], values[1::2]))


def feed_forward(spans, me_shard, rows, cots, bits, ways, both_w, near, far, waits=()):
    width, inner = both_w.shape[0], both_w.shape[1] // 2
    half = cots[0].shape[0]
    span = 2 * half // spans
    visits = Visits(spans, span)
    one = pl.Buffered(1)
    total = 2 * half
    part = width // len(ways)
    flat = [x for pair in rows for x in pair]
    hidden, grads, x_all, *parts = call(
        functools.partial(feed_kernel, visits, bits, ways),
        out_shape=[shape(total, inner), shape(total, 2 * inner), shape(total, width)]
        + [shape(half, part)] * 2 * len(ways),
        prefetch=1,
        grid=(spans,),
        in_specs=[
            whole(both_w, pipeline_mode=one),
            whole(near, pipeline_mode=one),
            whole(far, pipeline_mode=one),
            *visits.specs(bits, width),
            *[spec for way in ways for spec in visits.specs(way, part)],
        ],
        out_specs=[
            visits.rows(bits, inner),
            visits.rows(bits, 2 * inner),
            visits.rows(bits, width),
            *[spec for way in ways for spec in visits.specs(way, part)],
        ],
        scratch=[pltpu.VMEM((2 * near.shape[0], *near.shape[1:]), BF16)],
        cost_estimate=cost(
            10 * total * width * inner, total * (6 * width + 6 * inner) + 6 * width * inner
        ),
        name="feed_forward",
        waits=waits,
    )(me_shard, both_w, near, far, *cots, *flat)
    return pairs_of(parts), hidden, grads, x_all


def feed_out_kernel(count, walk, shard_ref, near_ref, far_ref, *rest):
    hidden, outs, held = rest[:count], rest[count:-1], rest[-1]

    @pl.when(pl.program_id(0) == 0)
    def _():
        assemble(held, shard_ref[0] % 2, near_ref, far_ref)

    down = held[...].reshape(-1, held.shape[2])
    for at in range(count):
        walk.store(outs[2 * at], outs[2 * at + 1], dot(hidden[at][...], down, 1, 0).astype(BF16))


def feed_out(spans, me_shard, hidden, near, far, waits=()):
    total, inner = hidden[0].shape
    width = near.shape[2]
    walk = Walk(spans, total // spans, False)
    count = len(hidden)
    return pairs_of(
        call(
            functools.partial(feed_out_kernel, count, walk),
            out_shape=[shape(total // 2, width)] * 2 * count,
            prefetch=1,
            grid=(spans,),
            in_specs=[
                whole(near, pipeline_mode=pl.Buffered(1)),
                whole(far, pipeline_mode=pl.Buffered(1)),
                *[pl.BlockSpec((total // spans, inner), walk.both)] * count,
            ],
            out_specs=walk.specs(width) * count,
            scratch=[pltpu.VMEM((2 * near.shape[0], *near.shape[1:]), BF16)],
            cost_estimate=cost(
                2 * count * total * inner * width,
                2 * count * total * (inner + width) + 2 * inner * width,
            ),
            name="feed_out",
            waits=waits,
        )(me_shard, near, far, *hidden)
    )


def terms_of(*refs):
    sums = [a[...].astype(F32) + b[...].astype(F32) for a, b in zip(refs[::2], refs[1::2])]
    return sums[0] if len(sums) == 1 else jnp.concatenate(sums, axis=1)


def back_kernel(count, me_ref, resid_ref, cot_ref, gain_ref, w_ref, *rest):
    terms, (resid_grad_ref, branch_ref, *mixed) = rest[:count], rest[count:]
    rows = resid_ref[...]
    factor = lax.rsqrt(jnp.mean(rows * rows, axis=-1, keepdims=True) + epsilon)
    unit_rows = rows * factor
    scaled = terms_of(*terms) * gain_ref[...]
    mean_dot = jnp.mean(scaled * unit_rows, axis=-1, keepdims=True)
    grad = cot_ref[...].astype(F32) + factor * (scaled - unit_rows * mean_dot)
    resid_grad_ref[...] = grad
    branch = grad.astype(BF16)
    branch_ref[...] = branch
    for at, out in enumerate(mixed):
        out[...] = dot(branch, w_ref[jnp.bitwise_xor(me_ref[0], at)], 1, 1).astype(BF16)


def norm_out_back(seq, me, spans, parts, resid, cot, gain, w_out, waits=()):
    rows, width = resid.shape
    terms = [x for pair in parts for x in pair]
    out_shape = [shape(rows, width, dtype=F32), shape(rows, width)]
    out_shape += [shape(rows, w_out.shape[1])] * spans
    out = call(
        functools.partial(back_kernel, len(terms)),
        out_shape=out_shape,
        prefetch=1,
        in_specs=[whole(resid), pl.BlockSpec((None, rows, width), lambda *_: (seq, 0, 0))]
        + [whole(x) for x in (gain, w_out, *terms)],
        out_specs=[whole(x) for x in out_shape],
        cost_estimate=cost(2 * rows * width * width, rows * width * 16 + width * width * 2),
        name="norm_out_back",
        waits=waits,
    )(me, resid, cot, gain, w_out, *terms)
    return out[0], out[1], out[2:]


def grad_in_kernel(visits, ways, proj_ref, w_ref, *outs):
    visits.store_halves(ways, outs, dot(proj_ref[...], w_ref[...], 1, 1).astype(BF16))


def grad_into_rows(spans, proj_grad, bits, ways, w_in, waits=()):
    full, narrow = proj_grad.shape
    width = w_in.shape[0]
    visits = Visits(spans, full // spans)
    part = width // len(ways)
    parts = call(
        functools.partial(grad_in_kernel, visits, ways),
        out_shape=[shape(full // 2, part)] * 2 * len(ways),
        grid=(spans,),
        in_specs=[visits.rows(bits, narrow), whole(w_in, pipeline_mode=pl.Buffered(1))],
        out_specs=[spec for way in ways for spec in visits.specs(way, part)],
        cost_estimate=cost(2 * full * narrow * width, 2 * full * (narrow + width) + 2 * narrow * width),
        name="grad_into_rows",
        waits=waits,
    )(proj_grad, w_in)
    return pairs_of(parts)


def product_of(lefts, rights):
    total = None
    i = j = a = b = 0
    while i < len(lefts):
        size = min(lefts[i].shape[0] - a, rights[j].shape[0] - b)
        term = dot(lefts[i][a : a + size, :], rights[j][b : b + size, :], 0, 0)
        total = term if total is None else total + term
        a, b = a + size, b + size
        if a == lefts[i].shape[0]:
            i, a = i + 1, 0
        if b == rights[j].shape[0]:
            j, b = j + 1, 0
    return total


def row_sums(product):
    sums = jnp.sum(product, axis=1, keepdims=True)
    return jnp.broadcast_to(sums, (product.shape[0], LANES)).T[:8]


def weight_kernel(left_count, right_count, gain, *refs):
    lefts, rights = refs[:left_count], refs[left_count : left_count + right_count]
    rest = refs[left_count + right_count :]
    total = product_of(lefts, rights)
    if gain:
        w_ref, out_ref, gain_ref = rest
        gain_ref[...] = row_sums(total * w_ref[...].astype(F32))
    else:
        (out_ref,) = rest
    out_ref[...] = total.astype(BF16)


def weight_grad(lefts, rights, weight, name, waits=()):
    rows = lefts[0].shape[1]
    tile = 256
    columns = rights[0].shape[1]
    depth = sum(x.shape[0] for x in lefts)
    out_shape = [shape(rows, columns)]
    out_specs = [pl.BlockSpec((tile, columns), lambda i: (i, 0))]
    weights = () if weight is None else (weight,)
    if weights:
        out_shape.append(shape(8, rows, dtype=F32))
        out_specs.append(pl.BlockSpec((8, tile), lambda i: (0, i)))
    return call(
        functools.partial(weight_kernel, len(lefts), len(rights), bool(weights)),
        out_shape=out_shape,
        grid=(rows // tile,),
        in_specs=[pl.BlockSpec((x.shape[0], tile), lambda i: (0, i)) for x in lefts]
        + [whole(x, pipeline_mode=pl.Buffered(1)) for x in rights]
        + [pl.BlockSpec((tile, x.shape[1]), lambda i: (i, 0)) for x in weights],
        out_specs=out_specs,
        cost_estimate=cost(
            2 * depth * rows * columns, 2 * depth * (rows + columns) + 2 * rows * columns
        ),
        name=name,
        waits=waits,
    )(*lefts, *rights, *weights)


def in_weight_kernel(own, shards, left_count, me_ref, *refs):
    lefts, (*rights, w_ref, other_ref, near_ref, far_ref, gain_ref) = refs[:left_count], refs[left_count:]
    total = product_of(lefts, rights)
    gain = row_sums(total * w_ref[...].astype(F32))
    first = lax.broadcasted_iota(jnp.int32, gain.shape, 0) < 4
    gain_ref[...] = jnp.where(first, gain, other_ref[...])
    total = total.astype(BF16)
    steps = shards.bit_length() - 1
    count = total.shape[0] // own
    for at in range(count):
        apart = jnp.bitwise_xor(me_ref[0], pl.program_id(0) * count + at)
        where = 0
        for bit in range(steps):
            where = where * 2 + (apart >> bit) % 2
        piece = total[at * own : (at + 1) * own]

        @pl.when(where < shards // 2)
        def _():
            near_ref[where] = piece

        @pl.when(where >= shards // 2)
        def _():
            far_ref[where - shards // 2] = piece


def in_weight_grad(me, lefts, rights, weight, other_gain, own, shards, waits=()):
    rows, columns = weight.shape
    tile = math.lcm(own, LANES)
    depth = sum(x.shape[0] for x in lefts)
    half = shape(shards // 2, own, columns)
    out_shape = (half, half, shape(8, rows, dtype=F32))
    return call(
        functools.partial(in_weight_kernel, own, shards, len(lefts)),
        out_shape=out_shape,
        prefetch=1,
        grid=(rows // tile,),
        in_specs=[pl.BlockSpec((x.shape[0], tile), lambda i, _: (0, i)) for x in lefts]
        + [whole(x) for x in rights]
        + [pl.BlockSpec((tile, columns), lambda i, _: (i, 0)), pl.BlockSpec((8, tile), lambda i, _: (0, i))],
        out_specs=[whole(half), whole(half), pl.BlockSpec((8, tile), lambda i, _: (0, i))],
        cost_estimate=cost(
            2 * depth * rows * columns, 2 * depth * (rows + columns) + 2 * rows * columns
        ),
        name="in_weight_grad",
        waits=waits,
    )(me, *lefts, *rights, weight, other_gain)


def add_pairs(left, right):
    return (left.astype(F32) + right.astype(F32)).astype(BF16)


def halve_kernel(near_ref, got_ref, gain_ref, gain_got_ref, *rest):
    outs, gain_out = rest[:-1], rest[-1]
    total = (near_ref[...].astype(F32) + got_ref[...].astype(F32)).astype(BF16)
    cut = total.shape[0] // len(outs)
    for at, out in enumerate(outs):
        out[...] = total[at * cut : (at + 1) * cut]
    gain_out[...] = gain_ref[...] + gain_got_ref[...]


def halve(near, got, gain, gain_got, waits=()):
    parts = 2 if near.shape[0] > 1 else 1
    out_shape = [shape(near.shape[0] // parts, *near.shape[1:])] * parts + [gain]
    return call(
        halve_kernel,
        out_shape=[shape(*x.shape, dtype=x.dtype) for x in out_shape],
        in_specs=[whole(x) for x in (near, got, gain, gain_got)],
        out_specs=[whole(x) for x in out_shape],
        cost_estimate=cost(0, 6 * near.size),
        name="halve",
        waits=waits,
    )(near, got, gain, gain_got)


def across(value, bit):
    size = lax.axis_size("fsdp")
    return lax.ppermute(value, "fsdp", [(i, i ^ bit) for i in range(size)])


def arrange_kernel(copies, every_ref, *outs):
    for own in range(every_ref.shape[0]):
        for source, out, target, size in copies:
            begin = target(own)
            outs[out][:, begin : begin + size] = every_ref[own, :, source : source + size].astype(F32)


def arrange_halves_kernel(order, copies, me_ref, *rest):
    blocks, (out_ref, held) = rest[:-2], rest[-2:]
    for at, owner in enumerate(order):
        held[jnp.bitwise_xor(me_ref[0], owner)] = blocks[at][...]
    arrange_kernel(copies, held, out_ref)


def arrange_halves(me, near, far, bits, copies, width, name):
    order = order_of(bits)
    count = len(order) // 2
    rows, columns = near.shape[0] // count, near.shape[1]
    tile = rows // 2
    out_shape = shape(rows, width, dtype=F32)

    def block(at):
        return pl.BlockSpec((tile, columns), lambda i, _: (2 * at + i, 0))

    return call(
        functools.partial(arrange_halves_kernel, order, copies),
        out_shape=out_shape,
        prefetch=1,
        grid=(2,),
        in_specs=[block(at) for _ in range(2) for at in range(count)],
        out_specs=pl.BlockSpec((tile, width), lambda i, _: (i, 0)),
        scratch=[pltpu.VMEM((len(order), tile, columns), BF16)],
        cost_estimate=cost(0, 6 * rows * width),
        name=name,
    )(me, *[near] * count, *[far] * count)


def arrange_blocks_kernel(order, copies, me_ref, *rest):
    blocks, outs, held = rest[: len(order)], rest[len(order) : -1], rest[-1]
    for at, owner in enumerate(order):
        held[jnp.bitwise_xor(me_ref[0], owner)] = blocks[at][...]
    arrange_kernel(copies, held, *outs)


def arrange_blocks(me, blocks, bits, copies, widths, name):
    rows, columns = blocks[0].shape
    tile = rows // 2
    order = order_of(bits)
    out_shape = [shape(rows, width, dtype=F32) for width in widths]
    return call(
        functools.partial(arrange_blocks_kernel, order, copies),
        out_shape=out_shape,
        prefetch=1,
        grid=(2,),
        in_specs=[pl.BlockSpec((tile, columns), lambda i, _: (i, 0))] * len(blocks),
        out_specs=[pl.BlockSpec((tile, width), lambda i, _: (i, 0)) for width in widths],
        scratch=[pltpu.VMEM((len(blocks), tile, columns), BF16)],
        cost_estimate=cost(0, 6 * rows * sum(widths)),
        name=name,
    )(me, *blocks)


def widen_rows_kernel(every_ref, out_ref):
    out_ref[...] = every_ref[...].astype(F32)


def to_float(value, name, waits=()):
    rows, width = value.shape
    tile = rows // 4 if rows % 64 == 0 else rows
    spec = pl.BlockSpec((tile, width), lambda i: (i, 0))
    return call(
        widen_rows_kernel,
        out_shape=shape(rows, width, dtype=F32),
        grid=(rows // tile,),
        in_specs=[spec],
        out_specs=spec,
        cost_estimate=cost(0, 6 * value.size),
        name=name,
        waits=waits,
    )(value)


def add_kernel(left_ref, right_ref, out_ref):
    out_ref[...] = left_ref[...].astype(F32) + right_ref[...].astype(F32)


def add_float(left, right):
    rows, width = left.shape
    tile = rows // 2
    spec = pl.BlockSpec((tile, width), lambda i: (i, 0))
    return call(
        add_kernel,
        out_shape=shape(rows, width, dtype=F32),
        grid=(2,),
        in_specs=[spec, spec],
        out_specs=spec,
        cost_estimate=cost(0, 8 * left.size),
        name="add_float",
    )(left, right)


def gains_kernel(left_ref, right_ref, first_norm, second_norm, first_ref, second_ref):
    total = left_ref[...] + right_ref[...]
    first_ref[...] = total[0:1] / first_norm[...]
    second_ref[...] = total[4:5] / second_norm[...]


def finish_gains(left, right, first_norm, second_norm):
    out_shape = [shape(1, left.shape[1], dtype=F32)] * 2
    return call(
        gains_kernel,
        out_shape=out_shape,
        in_specs=[whole(x) for x in (left, right, first_norm, second_norm)],
        out_specs=[whole(x) for x in out_shape],
        cost_estimate=cost(0, 8 * left.size),
        name="finish_gains",
    )(left, right, first_norm, second_norm)


def block_out_kernel(count, seqs, *refs):
    out_ref = refs[-1]
    for seq in range(seqs):
        resid_ref, *terms = refs[count * seq : count * (seq + 1)]
        out_ref[seq] = (resid_ref[...] + terms_of(*terms)).astype(BF16)


def finish_block_out(resid, terms, waits=()):
    rows, width = resid[0].shape
    out_shape = shape(len(resid), rows, width)
    flat = [y for q in range(len(resid)) for y in (resid[q], *[x for pair in terms[q] for x in pair])]
    count = len(flat) // len(resid)
    return call(
        functools.partial(block_out_kernel, count, len(resid)),
        out_shape=out_shape,
        in_specs=[whole(x) for x in flat],
        out_specs=whole(out_shape),
        cost_estimate=cost(0, 12 * out_shape.size),
        name="finish_block_out",
        waits=waits,
    )(*flat)


def tokens_grad_kernel(count, seqs, tokens_ref, gain_ref, *refs):
    out_ref = refs[-1]
    for seq in range(seqs):
        resid_ref, *terms = refs[count * seq : count * (seq + 1)]
        rows = tokens_ref[seq].astype(F32)
        factor = lax.rsqrt(jnp.mean(rows * rows, axis=-1, keepdims=True) + epsilon)
        unit_rows = rows * factor
        scaled = terms_of(*terms) * gain_ref[...]
        mean_dot = jnp.mean(scaled * unit_rows, axis=-1, keepdims=True)
        out_ref[seq] = (resid_ref[...] + factor * (scaled - unit_rows * mean_dot)).astype(BF16)


def finish_tokens_grad(tokens, gain, grad_resid, terms, waits=()):
    out_shape = shape(*tokens.shape)
    flat = [
        y for q in range(len(grad_resid)) for y in (grad_resid[q], *[x for pair in terms[q] for x in pair])
    ]
    count = len(flat) // len(grad_resid)
    return call(
        functools.partial(tokens_grad_kernel, count, len(grad_resid)),
        out_shape=out_shape,
        in_specs=[whole(x) for x in (tokens, gain, *flat)],
        out_specs=whole(out_shape),
        cost_estimate=cost(0, 12 * out_shape.size),
        name="finish_tokens_grad",
        waits=waits,
    )(tokens, gain, *flat)


def join_kernel(chips, me_ref, *refs):
    blocks, out_ref = refs[:-1], refs[-1]
    chip = me_ref[0] // 2
    for back in range(chips):
        out_ref[lax.rem(chip - back + chips, chips)] = blocks[back][...]


def join(me, blocks, waits=()):
    rows, width = blocks[0].shape
    out_shape = shape(len(blocks), rows, width)
    return call(
        functools.partial(join_kernel, len(blocks)),
        out_shape=out_shape,
        prefetch=1,
        in_specs=[whole(x) for x in blocks],
        out_specs=whole(out_shape),
        cost_estimate=cost(0, 4 * out_shape.size),
        name="join",
        waits=waits,
    )(me, *blocks)


def out_weight_kernel(spans, seqs, me_ref, *refs):
    mixed, branches, out_ref = refs[: spans * seqs], refs[spans * seqs : -1], refs[-1]
    for at in range(spans):
        total = None
        for seq in range(seqs):
            term = dot(mixed[seq * spans + at][...], branches[seq][...], 0, 0)
            total = term if total is None else total + term
        out_ref[jnp.bitwise_xor(me_ref[0], at)] = total.astype(BF16)


def out_weight_grad(me, mixed, branches, waits=()):
    flat = [x for group in mixed for x in group]
    narrow, width = flat[0].shape[1], branches[0].shape[1]
    out_shape = shape(len(mixed[0]), narrow, width)
    return call(
        functools.partial(out_weight_kernel, len(mixed[0]), len(branches)),
        out_shape=out_shape,
        prefetch=1,
        in_specs=[whole(x) for x in (*flat, *branches)],
        out_specs=whole(out_shape),
        cost_estimate=cost(2 * len(flat) * flat[0].size * width, 2 * len(mixed[0]) * narrow * width),
        name="out_weight_grad",
        waits=waits,
    )(me, *flat, *branches)


def turning_tables(positions):
    frequency = jnp.exp(
        jnp.arange(HALF, dtype=F32) * (-2.0 * math.log(rope_base) / HEAD_DIMENSION)
    )
    angles = positions.astype(F32)[:, :, None] * frequency
    cosine, sine = jnp.cos(angles), jnp.sin(angles)
    empty = jnp.zeros((*positions.shape, 64 - HALF), F32)
    return (
        jnp.concatenate([cosine, empty, cosine, empty], axis=-1),
        jnp.concatenate([-sine, empty, sine, empty], axis=-1),
    )


def body(
    tokens,
    joined_input_weight,
    out_projection,
    gate_weight,
    up_weight,
    down_weight,
    norm_first,
    norm_second,
    positions,
    cotangent,
):
    seqs, span, width = tokens.shape
    spans = lax.axis_size("seq")
    shards = lax.axis_size("fsdp")
    chips = shards // 2
    me = jnp.full((1,), lax.axis_index("seq"), jnp.int32)
    me_shard = jnp.full((1,), lax.axis_index("fsdp"), jnp.int32)
    full = positions.shape[1]
    pairs = KEY_VALUE_HEADS // spans
    repeat = QUERY_HEAD_COUNT // KEY_VALUE_HEADS
    unit = repeat + 2
    query_columns = QUERY_HEAD_COUNT * HEAD_DIMENSION
    pair_columns = KEY_VALUE_HEADS * HEAD_DIMENSION
    query_slab = query_columns // spans
    pair_slab = pair_columns // spans
    own_rows = joined_input_weight.shape[0]
    piece = FF // (shards * spans)
    inner = shards * piece
    step = min(256, full)
    pad = jnp.asarray(pad_matrix(pairs, repeat), BF16)
    place = jnp.asarray(place_matrix(pairs, repeat), BF16)
    gain_in, gain_mid = norm_first[None, :], norm_second[None, :]
    upward = tuple(range(spans.bit_length() - 1))
    orders = [(upward[::-1], upward)[q % 2] for q in range(seqs)]
    both = range(seqs)
    del CHAIN[:]

    def gather(shard):
        return lax.all_gather(shard, "fsdp", axis=0, tiled=True)

    def owned(value):
        return lax.psum_scatter(value, "fsdp", scatter_dimension=0, tiled=True)

    ways = (upward[::-1], upward)

    def flat(pairs):
        return tuple(x for pair in pairs for x in pair)

    def copied(value, bits):
        held = [value]
        for bit in bits:
            held = held + [swap(x, bit) for x in held]
        return held

    in_shard = cut_in(me, joined_input_weight, spans, (query_slab, pair_slab, pair_slab))
    w_in = gather(in_shard)
    w_out = gather(out_projection).reshape(spans, query_slab, width)
    cot_rows = split_rows(cotangent)
    cot_got = gather_start(cot_rows, orders)
    normed = norm_rows(tokens, gain_in)
    x_got = gather_start(normed, orders)
    both_shard, down_shard = cut_feed(
        me, gate_weight, up_weight, down_weight, spans, shards, piece, ()
    )
    w_both = gather(both_shard)
    down_blocks = [down_shard, around(down_shard)]

    def pass_on():
        if len(down_blocks) < chips:
            down_blocks[-1:] = pin(down_blocks[-1])
            down_blocks.append(around(down_blocks[-1]))

    cosine, sine = turning_tables(positions)
    starts = (jnp.arange(full, dtype=jnp.int32)[None, :] - positions)[:, None, :]
    x_in = gather_end(normed, x_got, orders, "stack_in")
    pass_on()
    w_wide = widen(w_in, pad)
    pass_on()

    projected, mixed, lse, resid, x_mid = [], [], [], [], []

    def project_rows(q, waits=()):
        rows, *normed_mid = project_out(q, me, mixed[q], w_out, tokens, gain_mid, ways, waits)
        resid.append(rows)
        return normed_mid, gather_start(normed_mid, ways)

    for q in both:
        projected.append(
            project_in(
                me, x_in[q], orders[q], w_wide, cosine[q], sine[q], unit, x_in[-1] if q == 0 else ()
            )
        )
        if q == 0:
            cots = gather_end(cot_rows, cot_got, orders, "stack_cot")
            pass_on()
        if q == 1:
            started = [project_rows(0)]
        heads, sums = attention_forward(me, projected[q], starts[q], place, spans, repeat, step)
        lse.append(sums)
        mixed.append(shared(heads))
        if q == 0:
            while len(down_blocks) < chips:
                pass_on()
            down_near = join(me_shard, down_blocks)
            down_far = beside(down_near)
    x_mid.append(gather_end(*started[0], ways, "stack_mid"))
    for q in both[1:]:
        started.append(project_rows(q, (down_far, *flat(cots))))
    for q in both[1:]:
        x_mid.append(gather_end(*started[q], ways, "stack_mid"))

    hidden, grad_both, grad_mid, x_all = [], [], [], []
    for q in both:
        parts, kept, grads, rows = feed_forward(
            spans, me_shard, x_mid[q], cots[q], orders[q], ways, w_both, down_near, down_far
        )
        hidden.append(kept)
        grad_both.append(grads)
        x_all.append(rows)
        grad_mid.append(scatter_start(parts, ways))

    grad_resid, branches, head_grads = [], [], []

    def norm_back(q, waits=()):
        rows, branch, heads = norm_out_back(
            q, me, spans, grad_mid[q], resid[q], cotangent, gain_mid, w_out, waits
        )
        grad_resid.append(rows)
        branches.append(branch)
        head_grads.append(shared(heads))

    grad_mid[0] = scatter_end(*grad_mid[0], ways)
    both_part, gain_second = weight_grad(x_all, grad_both, w_both, "gate_up_grad")
    both_own = owned(both_part)
    norm_back(0)
    for q in both[1:]:
        grad_mid[q] = scatter_end(*grad_mid[q], ways)
    outs = scatter_start(
        feed_out(spans, me_shard, hidden, down_near, down_far, tuple(head_grads[0][1:])), orders
    )
    for q in both[1:]:
        norm_back(q)
    (down_part,) = weight_grad(hidden, flat(cots), None, "down_grad")
    down_own = owned(down_part)
    out_part = out_weight_grad(me, mixed, branches).reshape(query_columns, width)
    out_own = owned(out_part)

    proj_grads, grad_in = [], []
    for q in both:
        proj_grads.append(
            attention_backward(
                me,
                projected[q],
                starts[q],
                place,
                head_grads[q],
                orders[q],
                lse[q],
                cosine[q],
                sine[q],
                pad,
                repeat,
                step,
            )
        )
        if q == 0:
            outs = scatter_end(*outs, orders)
            both_every = copied(both_own, ways[0])
        if q == seqs - 1:
            for p in both[:-1]:
                grad_in[p] = scatter_end(*grad_in[p], ways)
            in_near, in_far, in_gain = in_weight_grad(
                me_shard,
                flat(x_in),
                proj_grads,
                w_in,
                gain_second,
                own_rows,
                shards,
                (*flat(outs), both_every[1]),
            )
            in_got, gain_got = across(in_far, 1), across(in_gain, 1)
        waits = tuple(x for group in head_grads[1:] for x in group[1:]) if q == 0 else flat(grad_in[0])
        parts = grad_into_rows(spans, proj_grads[q], orders[q], ways, w_in, waits)
        grad_in.append(scatter_start(parts, ways))
    (down_own,) = pin(down_own)
    down_every = lax.all_gather(down_own, "seq", axis=0, tiled=True)
    in_near, in_sent, in_gain = halve(in_near, in_got, in_gain, gain_got, tuple(both_every))
    in_got, gain_got = across(in_sent, 2), across(in_gain, 2)
    copies = [
        (part * inner + shard * piece, part, lambda own, shard=shard: (shard * spans + own) * piece, piece)
        for part in range(2)
        for shard in range(shards)
    ]
    sums = [out_own]

    def out_start(bit):
        sums[:] = pin(*sums)
        total = sums[0] if len(sums) == 1 else add_pairs(*sums)
        sums[:] = [total, swap(total, bit)]

    out_start(0)
    block_out = finish_block_out(resid, [[pair] for pair in outs])
    grad_in[-1] = scatter_end(*grad_in[-1], ways)
    bit = 4
    while in_near.shape[0] > 1:
        in_near, in_sent, in_gain = halve(in_near, in_got, in_gain, gain_got)
        in_got, gain_got = across(in_sent, bit), across(in_gain, bit)
        bit *= 2
    in_own, in_gain = halve(in_near, in_got, in_gain, gain_got)
    in_every = [in_own[0]]
    out_start(1)
    for bit in upward:
        got = [swap(x, bit) for x in in_every]
        gain_got = swap(in_gain, bit)
        if bit == 0:
            tokens_grad = finish_tokens_grad(tokens, gain_in, grad_resid, grad_in)
        if bit + 1 < len(upward):
            *got, gain_got = pin(*got, gain_got)
        in_every = in_every + got
        if bit + 1 < len(upward):
            in_gain = in_gain + gain_got
    for bit in upward[2:]:
        out_start(bit)
    out_grad = add_float(*sums)
    gate_grad, up_grad = arrange_blocks(me, both_every, ways[0], copies, (FF, FF), "arrange_gate_up")
    down_grad = to_float(down_every, "down_to_float")
    copies = [
        (0, 0, lambda own: own * query_slab, query_slab),
        (query_slab, 0, lambda own: query_columns + own * pair_slab, pair_slab),
        (
            query_slab + pair_slab,
            0,
            lambda own: query_columns + pair_columns + own * pair_slab,
            pair_slab,
        ),
    ]
    (in_grad,) = arrange_blocks(
        me,
        in_every,
        upward,
        copies,
        (query_columns + 2 * pair_columns,),
        "arrange_in",
    )
    first_gain, second_gain = finish_gains(in_gain, gain_got, gain_in, gain_mid)
    return (
        block_out,
        tokens_grad,
        in_grad,
        out_grad,
        gate_grad,
        up_grad,
        down_grad,
        first_gain.reshape(width),
        second_gain.reshape(width),
    )


def solution(mesh):
    return jax.shard_map(
        body,
        mesh=mesh,
        in_specs=(
            P("fsdp", "seq", None),
            P("fsdp", None),
            P("fsdp", None),
            P("fsdp", None),
            P("fsdp", None),
            P("fsdp", None),
            P(),
            P(),
            P("fsdp", None),
            P("fsdp", "seq", None),
        ),
        out_specs=(
            P("fsdp", "seq", None),
            P("fsdp", "seq", None),
            P("fsdp", None),
            P("fsdp", None),
            P("fsdp", None),
            P("fsdp", None),
            P("fsdp", None),
            P(),
            P(),
        ),
        check_vma=False,
    )
```

```python
import functools
import math

import jax
import jax.numpy as jnp
import numpy as np
from jax import lax
from jax.experimental import pallas as pl
from jax.experimental.pallas import tpu as pltpu
from jax.sharding import PartitionSpec as P

FF = 4096
QUERY_HEAD_COUNT = 16
KEY_VALUE_HEADS = 8
HEAD_DIMENSION = 96
HALF = HEAD_DIMENSION // 2
LANES = 128

epsilon = 1e-05
rope_base = 100000.0
SCALING = 1.0 / math.sqrt(HEAD_DIMENSION)
LOG2E = 1.4426950408889634
BF16 = jnp.bfloat16
F32 = jnp.float32
MIB = 1024 * 1024
VMEM_LIMIT = 64
COST_SCALE = 20
WEIGHTS = {"norm_out_back": 2.5, "feed_out": 2.5}


def dot(a, b, ca, cb):
    return lax.dot_general(a, b, (((ca,), (cb,)), ((), ())), preferred_element_type=F32)


def params(limit):
    return pltpu.CompilerParams(vmem_limit_bytes=limit * MIB)


def cost(flops, moved, trans=0):
    return int(flops), int(moved)


def weighted(estimate, name):
    scale = WEIGHTS.get(name, COST_SCALE)
    return pl.CostEstimate(
        flops=int(estimate[0] * scale), bytes_accessed=int(estimate[1] * scale), transcendentals=0
    )


CHAIN = []


def call(kernel, *, out_shape, in_specs, out_specs, prefetch=0, grid=(1,), scratch=(), cost_estimate=None, name=None, waits=()):
    count = prefetch + len(in_specs)
    waits = (*waits, *CHAIN[-1:])

    def run(*refs):
        kernel(*refs[:count], *refs[count + len(waits) :])

    inner = pl.pallas_call(
        run,
        out_shape=out_shape,
        grid_spec=pltpu.PrefetchScalarGridSpec(
            num_scalar_prefetch=prefetch,
            grid=grid,
            in_specs=[*in_specs, *[pl.BlockSpec(memory_space=pltpu.HBM)] * len(waits)],
            out_specs=out_specs,
            scratch_shapes=list(scratch),
        ),
        compiler_params=params(VMEM_LIMIT),
        cost_estimate=weighted(cost_estimate, name),
        name=name,
    )

    def made(*args):
        out = inner(*args, *waits)
        CHAIN.append(out[-1] if isinstance(out, (list, tuple)) else out)
        return out

    return made


def pin(*values):
    waits = tuple(CHAIN[-1:])
    count = len(values)
    hbm = pl.BlockSpec(memory_space=pltpu.HBM)
    out = pl.pallas_call(
        lambda *refs: None,
        out_shape=[shape(*x.shape, dtype=x.dtype) for x in values],
        in_specs=[hbm] * (count + len(waits)),
        out_specs=[hbm] * count,
        input_output_aliases={at: at for at in range(count)},
        cost_estimate=weighted(cost(0, 0), "pin"),
        name="pin",
    )(*values, *waits)
    CHAIN.append(out[-1])
    return out


def whole(array, **extra):
    return pl.BlockSpec(array.shape, lambda *_: (0,) * len(array.shape), **extra)


def shape(*sizes, dtype=BF16):
    return jax.ShapeDtypeStruct(sizes, dtype)


def pad_matrix(pairs, repeat):
    unit = repeat + 2
    out = np.zeros((pairs * unit * HEAD_DIMENSION, pairs * unit * LANES), np.float32)
    for g in range(pairs):
        for r in range(unit):
            if r < repeat:
                src = (g * repeat + r) * HEAD_DIMENSION
            else:
                src = (pairs * repeat + (r - repeat) * pairs + g) * HEAD_DIMENSION
            dst = (g * unit + r) * LANES
            for j in range(HEAD_DIMENSION):
                lane = j if (r == unit - 1 or j < HALF) else 64 + j - HALF
                out[src + j, dst + lane] = 1.0
    return out


def place_matrix(pairs, repeat):
    out = np.zeros((pairs, repeat * LANES, pairs * repeat * HEAD_DIMENSION), np.float32)
    for g in range(pairs):
        for r in range(repeat):
            for j in range(HEAD_DIMENSION):
                out[g, r * LANES + j, (g * repeat + r) * HEAD_DIMENSION + j] = 1.0
    return out


def order_of(bits):
    owners = [0]
    for bit in bits:
        owners = owners + [at ^ (1 << bit) for at in owners]
    return owners


def swap(value, bit):
    size = lax.axis_size("seq")
    return lax.ppermute(value, "seq", [(i, i ^ (1 << bit)) for i in range(size)])


def exchange(value, other):
    size = lax.axis_size("seq")
    return lax.ppermute(value, "seq", [(i, i ^ other) for i in range(size)])


def shared(heads):
    return [heads[0]] + [exchange(heads[at], at) for at in range(1, len(heads))]


def around(value):
    size = lax.axis_size("fsdp")
    return lax.ppermute(value, "fsdp", [(i, (i + 2) % size) for i in range(size)])


def beside(value):
    size = lax.axis_size("fsdp")
    return lax.ppermute(value, "fsdp", [(i, i ^ 1) for i in range(size)])


def copy_kernel(source_ref, *outs):
    for at, ref in enumerate(outs):
        ref[...] = source_ref[at]


def split_rows(value, waits=()):
    seqs, span, width = value.shape
    out_shape = [shape(span, width)] * seqs
    return call(
        copy_kernel,
        out_shape=out_shape,
        in_specs=[whole(value)],
        out_specs=[whole(x) for x in out_shape],
        cost_estimate=cost(0, 4 * value.size),
        name="split_rows",
        waits=waits,
    )(value)


def stack_kernel(*refs):
    count = len(refs) // 3
    for at in range(count):
        first, second, out = refs[2 * at], refs[2 * at + 1], refs[2 * count + at]
        rows = first.shape[0]
        out[:rows] = first[...]
        out[rows:] = second[...]


def stack_rows(pairs, name, waits=()):
    out_shape = [shape(2 * a.shape[0], a.shape[1]) for a, _ in pairs]
    flat = [x for pair in pairs for x in pair]
    return call(
        stack_kernel,
        out_shape=out_shape,
        in_specs=[whole(x) for x in flat],
        out_specs=[whole(x) for x in out_shape],
        cost_estimate=cost(0, 4 * sum(x.size for x in flat)),
        name=name,
        waits=waits,
    )(*flat)


def gather_start(blocks, orders):
    return [swap(x, bits[0]) for x, bits in zip(blocks, orders)]


def gather_end(blocks, got, orders, name, waits=()):
    held = list(zip(blocks, got))
    for level in range(1, len(orders[0])):
        joined = stack_rows(held, name, waits if level == 1 else ())
        held = [(x, swap(x, bits[level])) for x, bits in zip(joined, orders)]
    return held


def fold_kernel(*refs):
    count = len(refs) // 4
    for at in range(count):
        near, got, keep, send = refs[at], refs[count + at], refs[2 * count + at], refs[3 * count + at]
        total = near[...].astype(F32) + got[...].astype(F32)
        cut = total.shape[0] // 2
        keep[...] = total[:cut]
        send[...] = total[cut:].astype(BF16)


def fold(near, got, waits=()):
    out_shape = [shape(x.shape[0] // 2, x.shape[1], dtype=F32) for x in near]
    out_shape += [shape(x.shape[0] // 2, x.shape[1]) for x in near]
    out = call(
        fold_kernel,
        out_shape=out_shape,
        in_specs=[whole(x) for x in (*near, *got)],
        out_specs=[whole(x) for x in out_shape],
        cost_estimate=cost(0, 5 * sum(x.size for x in near)),
        name="fold",
        waits=waits,
    )(*near, *got)
    return out[: len(near)], out[len(near) :]


def scatter_start(parts, orders):
    return [near for near, _ in parts], [swap(far, bits[-1]) for (_, far), bits in zip(parts, orders)]


def scatter_end(near, got, orders, waits=()):
    for level in range(len(orders[0]) - 2, -1, -1):
        near, sent = fold(near, got, waits)
        got = [swap(x, bits[level]) for x, bits in zip(sent, orders)]
    return list(zip(near, got))


def norm_kernel(tokens_ref, gain_ref, *outs):
    for seq, out in enumerate(outs):
        rows = tokens_ref[seq].astype(F32)
        factor = lax.rsqrt(jnp.mean(rows * rows, axis=-1, keepdims=True) + epsilon)
        out[...] = (rows * factor * gain_ref[...]).astype(BF16)


def norm_rows(tokens, gain):
    seqs, span, width = tokens.shape
    out_shape = [shape(span, width)] * seqs
    return call(
        norm_kernel,
        out_shape=out_shape,
        in_specs=[whole(tokens), whole(gain)],
        out_specs=[whole(x) for x in out_shape],
        cost_estimate=cost(8 * tokens.size, 4 * tokens.size),
        name="norm_rows",
    )(tokens, gain)


def cut_in_kernel(spans, sizes, me_ref, w_ref, out_ref):
    for own in range(spans):

        @pl.when(me_ref[0] == own)
        def _():
            begin, put = 0, 0
            for size in sizes:
                out_ref[:, put : put + size] = w_ref[:, begin + own * size : begin + (own + 1) * size]
                begin, put = begin + spans * size, put + size


def cut_in(me, weight, spans, sizes):
    out_shape = shape(weight.shape[0], sum(sizes))
    return call(
        functools.partial(cut_in_kernel, spans, sizes),
        out_shape=out_shape,
        prefetch=1,
        in_specs=[whole(weight)],
        out_specs=whole(out_shape),
        cost_estimate=cost(0, 4 * weight.size),
        name="cut_in",
    )(me, weight)


def cut_feed_kernel(spans, shards, piece, me_ref, gate_ref, up_ref, down_ref, both_ref, out_ref):
    inner = shards * piece
    for own in range(spans):

        @pl.when(me_ref[0] == own)
        def _():
            for shard in range(shards):
                begin = (shard * spans + own) * piece
                put = shard * piece
                both_ref[:, put : put + piece] = gate_ref[:, begin : begin + piece]
                both_ref[:, inner + put : inner + put + piece] = up_ref[:, begin : begin + piece]
            out_ref[...] = down_ref[own * piece : (own + 1) * piece, :]


def cut_feed(me, gate, up, down, spans, shards, piece, waits):
    out_shape = (shape(gate.shape[0], 2 * shards * piece), shape(piece, down.shape[1]))
    return call(
        functools.partial(cut_feed_kernel, spans, shards, piece),
        out_shape=out_shape,
        prefetch=1,
        in_specs=[whole(x) for x in (gate, up, down)],
        out_specs=[whole(x) for x in out_shape],
        cost_estimate=cost(0, 4 * gate.size),
        name="cut_feed",
        waits=waits,
    )(me, gate, up, down)


def widen_kernel(w_ref, pad_ref, out_ref):
    out_ref[...] = dot(w_ref[...], pad_ref[...], 1, 0).astype(BF16)


def widen(w_slice, pad, waits=()):
    rows, narrow = w_slice.shape
    wide = pad.shape[1]
    out_shape = shape(rows, wide)
    return call(
        widen_kernel,
        out_shape=out_shape,
        in_specs=[whole(w_slice), whole(pad)],
        out_specs=whole(out_shape),
        cost_estimate=cost(2 * rows * narrow * wide, 2 * rows * (narrow + wide)),
        name="widen",
        waits=waits,
    )(w_slice, pad)


class Walk:
    def __init__(self, spans, span, near_first):
        self.cut, self.span, self.near_first = spans // 2, span, near_first

    def first(self, step):
        return jnp.minimum(step, self.cut - 1)

    def second(self, step):
        return jnp.maximum(step - self.cut, 0)

    def near(self, step, *_):
        return (self.first(step) if self.near_first else self.second(step), 0)

    def far(self, step, *_):
        return (self.second(step) if self.near_first else self.first(step), 0)

    def both(self, step, *_):
        return (step if self.near_first else lax.rem(step + self.cut, 2 * self.cut), 0)

    def specs(self, width):
        return [
            pl.BlockSpec((self.span, width), self.near),
            pl.BlockSpec((self.span, width), self.far),
        ]

    def is_near(self):
        early = pl.program_id(0) < self.cut
        return early if self.near_first else jnp.logical_not(early)

    def load(self, near_ref, far_ref):
        return jnp.where(self.is_near(), near_ref[...], far_ref[...])

    def store(self, near_ref, far_ref, value):
        near = self.is_near()

        @pl.when(near)
        def _():
            near_ref[...] = value

        @pl.when(jnp.logical_not(near))
        def _():
            far_ref[...] = value


def owner_at(order, index):
    owner = 0
    for at, value in enumerate(order):
        owner = jnp.where(index == at, value, owner)
    return owner


class Visits:
    def __init__(self, spans, span):
        self.spans, self.span = spans, span
        self.order = sorted(range(spans), key=lambda at: -bin(at).count("1"))

    def index(self, blocks):
        held = [blocks.get(owner) for owner in self.order]
        known = next(x for x in held if x is not None)
        for at, value in enumerate(held):
            known = held[at] = known if value is None else value
        return lambda step, *_: (owner_at(held, step), 0)

    def parts(self, bits):
        order = order_of(bits)
        cut = self.spans // 2
        near = {owner: at for at, owner in enumerate(order[:cut])}
        far = {owner: at for at, owner in enumerate(order[cut:])}
        return near, far

    def specs(self, bits, width):
        return [pl.BlockSpec((self.span, width), self.index(blocks)) for blocks in self.parts(bits)]

    def rows(self, bits, width):
        order = order_of(bits)
        return pl.BlockSpec(
            (self.span, width), self.index({owner: at for at, owner in enumerate(order)})
        )

    def is_near(self, bits):
        near, _ = self.parts(bits)
        flag = jnp.bool_(False)
        for at, owner in enumerate(self.order):
            if owner in near:
                flag = jnp.logical_or(flag, pl.program_id(0) == at)
        return flag

    def load(self, bits, near_ref, far_ref):
        return jnp.where(self.is_near(bits), near_ref[...], far_ref[...])

    def store(self, bits, near_ref, far_ref, value):
        near = self.is_near(bits)

        @pl.when(near)
        def _():
            near_ref[...] = value

        @pl.when(jnp.logical_not(near))
        def _():
            far_ref[...] = value

    def store_halves(self, ways, refs, value):
        columns = value.shape[1] // len(ways)
        for at, bits in enumerate(ways):
            part = value[:, at * columns : (at + 1) * columns]
            self.store(bits, refs[2 * at], refs[2 * at + 1], part)


def in_kernel(walk, unit, me_ref, w_ref, cos_ref, sin_ref, near_ref, far_ref, out_ref):
    rows = dot(walk.load(near_ref, far_ref), w_ref[...], 1, 0)
    cosine, sine = cos_ref[...], sin_ref[...]
    for part in range(rows.shape[1] // LANES):
        lanes = slice(part * LANES, (part + 1) * LANES)
        piece = rows[:, lanes]
        if part % unit != unit - 1:
            piece = piece * cosine + pltpu.roll(piece, 64, 1) * sine
        out_ref[:, lanes] = piece.astype(BF16)


def project_in(me, rows, bits, w_wide, cosine, sine, unit, waits=()):
    width, wide = w_wide.shape
    order = order_of(bits)
    spans = len(order)
    full = cosine.shape[0]
    span = full // spans
    walk = Walk(spans, span, True)

    def ordered(step, me_ref):
        return (jnp.bitwise_xor(me_ref[0], owner_at(order, step)), 0)

    return call(
        functools.partial(in_kernel, walk, unit),
        out_shape=shape(full, wide),
        prefetch=1,
        grid=(spans,),
        in_specs=[
            whole(w_wide, pipeline_mode=pl.Buffered(1)),
            pl.BlockSpec((span, LANES), ordered),
            pl.BlockSpec((span, LANES), ordered),
            *walk.specs(width),
        ],
        out_specs=pl.BlockSpec((span, wide), ordered),
        cost_estimate=cost(2 * full * width * wide, 2 * full * (width + wide) + 2 * width * wide),
        name="project_in",
        waits=waits,
    )(me, w_wide, cosine, sine, *rows)


def mask_of(scores, first_key, first_row, starts, repeat, diagonal):
    keys = lax.broadcasted_iota(jnp.int32, scores.shape, 0) + first_key
    allowed = keys >= starts
    if diagonal:
        step = scores.shape[1] // repeat
        rows = lax.broadcasted_iota(jnp.int32, scores.shape, 1) % step + first_row
        allowed = allowed & (keys <= rows)
    return jnp.where(allowed, scores, -1e30)


def query_of(proj_ref, rows, repeat):
    return jnp.concatenate(
        [proj_ref[rows, r * LANES : (r + 1) * LANES] for r in range(repeat)], axis=0
    )


def forward_kernel(spans, step, repeat, me_ref, proj_ref, start_ref, place_ref, *rest):
    outs, lse_ref, held = rest[:spans], rest[spans], rest[spans + 1]
    full = proj_ref.shape[0]
    span = full // spans
    pair = pl.program_id(0)
    me = me_ref[0]
    value_t = proj_ref[:, (repeat + 1) * LANES :].T
    starts = start_ref[...]

    @pl.when(pair == 0)
    def _():
        held[...] = jnp.zeros_like(held)

    for block in range(full // step):
        begin, end = block * step, (block + 1) * step
        rows = slice(begin, end)
        query = query_of(proj_ref, rows, repeat)
        starts_now = jnp.concatenate([starts[:, rows]] * repeat, axis=1)
        pieces = []
        for key_block in range(block + 1):
            first = key_block * step
            key = proj_ref[first : first + step, repeat * LANES : (repeat + 1) * LANES]
            scores = dot(key, query, 1, 1) * (SCALING * LOG2E)
            pieces.append(mask_of(scores, first, begin, starts_now, repeat, key_block == block))
        top = functools.reduce(jnp.maximum, [jnp.max(p, axis=0, keepdims=True) for p in pieces])
        total = None
        summed = None
        for key_block in range(block + 1):
            first = key_block * step
            raised = jnp.exp2(pieces[key_block] - top)
            part = jnp.sum(raised, axis=0, keepdims=True)
            mixed = dot(value_t[:, first : first + step], raised.astype(BF16), 1, 0)
            total = part if total is None else total + part
            summed = mixed if summed is None else summed + mixed
        mixed_t = (summed * (1.0 / total)).astype(BF16)
        lse_ref[block : block + 1, :] = top + jnp.log2(total)
        wide = None
        for r in range(repeat):
            term = dot(
                mixed_t[:, r * step : (r + 1) * step],
                place_ref[r * LANES : (r + 1) * LANES, :],
                0,
                0,
            )
            wide = term if wide is None else wide + term
        wide = wide.astype(BF16)
        for piece in range(step // span):
            at = jnp.bitwise_xor(me, block * (step // span) + piece)
            held[at] = held[at] + wide[piece * span : (piece + 1) * span]

    @pl.when(pair == pl.num_programs(0) - 1)
    def _():
        for at in range(spans):
            outs[at][...] = held[at]


def attention_forward(me, proj, starts, place, spans, repeat, step, waits=()):
    full, wide = proj.shape
    pairs, _, narrow = place.shape
    group = wide // pairs
    span = full // spans
    work = pairs * repeat * full * full
    out_shape = [jax.ShapeDtypeStruct((span, narrow), BF16)] * spans
    out_shape.append(jax.ShapeDtypeStruct((pairs, full // step, repeat * step), F32))
    *mixed, lse = call(
        functools.partial(forward_kernel, spans, step, repeat),
        out_shape=out_shape,
        prefetch=1,
        grid=(pairs,),
        in_specs=[
            pl.BlockSpec((full, group), lambda j, _: (0, j)),
            pl.BlockSpec((1, full), lambda j, _: (0, 0)),
            pl.BlockSpec((None, repeat * LANES, narrow), lambda j, _: (j, 0, 0)),
        ],
        out_specs=[whole(x) for x in out_shape[:-1]]
        + [pl.BlockSpec((None, full // step, repeat * step), lambda j, _: (j, 0, 0))],
        scratch=[pltpu.VMEM((spans, span, narrow), BF16)],
        cost_estimate=cost(2 * work * 256, 2 * proj.size * 2, work),
        name="attention_forward",
        waits=waits,
    )(me, proj, starts, place)
    return mixed, lse


def backward_kernel(
    order, step, repeat, me_ref, proj_ref, start_ref, place_ref, lse_ref, cos_ref, sin_ref, pad_ref, *rest
):
    spans = len(order)
    grads, (out_ref, key_acc, value_acc, held) = rest[:spans], rest[spans:]
    full = proj_ref.shape[0]
    span = full // spans
    pair = pl.program_id(0)
    me = me_ref[0]
    key_t = proj_ref[:, repeat * LANES : (repeat + 1) * LANES].T
    starts = start_ref[...]
    key_acc[...] = jnp.zeros_like(key_acc)
    value_acc[...] = jnp.zeros_like(value_acc)

    @pl.when(pair == 0)
    def _():
        for at in range(spans):
            held[jnp.bitwise_xor(me, at)] = grads[at][...]
        out_ref[...] = jnp.zeros_like(out_ref)

    def turn_back(grad, rows):
        grad = grad.astype(BF16).astype(F32)
        return (grad * cos_ref[rows, :] - pltpu.roll(grad, 64, 1) * sin_ref[rows, :]).astype(BF16)

    def put(begin, wide):
        for at in range(0, wide.shape[0], span):
            owner = jnp.bitwise_xor(me, (begin + at) // span)
            where = 0
            for index, value in enumerate(order):
                where = jnp.where(owner == value, index, where)
            here = pl.ds(pl.multiple_of(where * span, span), span)
            out_ref[here, :] = out_ref[here, :] + wide[at : at + span]

    for block in range(full // step):
        begin, end = block * step, (block + 1) * step
        rows = slice(begin, end)
        query = query_of(proj_ref, rows, repeat)
        grad_rows = jnp.concatenate(
            [held[at] for at in range(begin // span, end // span)], axis=0
        )
        grad = jnp.concatenate(
            [
                dot(grad_rows, place_ref[r * LANES : (r + 1) * LANES, :], 1, 1).astype(BF16)
                for r in range(repeat)
            ],
            axis=0,
        )
        starts_now = jnp.concatenate([starts[:, rows]] * repeat, axis=1)
        lse = lse_ref[block : block + 1, :]
        kept = []
        mean_dot = None
        for key_block in range(block + 1):
            first = key_block * step
            keys = slice(first, first + step)
            key = proj_ref[keys, repeat * LANES : (repeat + 1) * LANES]
            value = proj_ref[keys, (repeat + 1) * LANES :]
            scores = dot(key, query, 1, 1) * (SCALING * LOG2E)
            scores = mask_of(scores, first, begin, starts_now, repeat, key_block == block)
            shares = jnp.exp2(scores - lse)
            value_acc[keys, :] += dot(shares.astype(BF16), grad, 1, 0)
            product = shares * dot(value, grad, 1, 1)
            part = jnp.sum(product, axis=0, keepdims=True)
            mean_dot = part if mean_dot is None else mean_dot + part
            kept.append((shares, product))
        query_grad_t = None
        for key_block in range(block + 1):
            first = key_block * step
            keys = slice(first, first + step)
            shares, product = kept[key_block]
            score_grad = (SCALING * (product - shares * mean_dot)).astype(BF16)
            key_acc[keys, :] += dot(score_grad, query, 1, 0)
            term = dot(key_t[:, keys], score_grad, 1, 0)
            query_grad_t = term if query_grad_t is None else query_grad_t + term
        query_grad = query_grad_t.T
        wide = None
        for r in range(repeat):
            turned = turn_back(query_grad[r * step : (r + 1) * step], rows)
            term = dot(turned, pad_ref[:, r * LANES : (r + 1) * LANES], 1, 1)
            wide = term if wide is None else wide + term
        put(begin, wide.astype(BF16))
    for block in range(full // step):
        rows = slice(block * step, (block + 1) * step)
        turned = turn_back(key_acc[rows, :], rows)
        wide = dot(turned, pad_ref[:, repeat * LANES : (repeat + 1) * LANES], 1, 1)
        wide += dot(value_acc[rows, :].astype(BF16), pad_ref[:, (repeat + 1) * LANES :], 1, 1)
        put(block * step, wide.astype(BF16))


def attention_backward(
    me, proj, starts, place, grads, bits, lse, cosine, sine, pad, repeat, step, waits=()):
    full, wide = proj.shape
    pairs, _, narrow = place.shape
    group = wide // pairs
    work = pairs * repeat * full * full
    out_shape = shape(full, pad.shape[0])
    return call(
        functools.partial(backward_kernel, order_of(bits), step, repeat),
        out_shape=out_shape,
        prefetch=1,
        grid=(pairs,),
        in_specs=[
            pl.BlockSpec((full, group), lambda j, _: (0, j)),
            pl.BlockSpec((1, full), lambda j, _: (0, 0)),
            pl.BlockSpec((None, repeat * LANES, narrow), lambda j, _: (j, 0, 0)),
            pl.BlockSpec((None, full // step, repeat * step), lambda j, _: (j, 0, 0)),
            whole(cosine),
            whole(sine),
            pl.BlockSpec((pad.shape[0], group), lambda j, _: (0, j)),
            *[whole(x) for x in grads],
        ],
        out_specs=whole(out_shape),
        scratch=[
            pltpu.VMEM((full, LANES), F32),
            pltpu.VMEM((full, LANES), F32),
            pltpu.VMEM((len(grads), full // len(grads), narrow), BF16),
        ],
        cost_estimate=cost(2 * work * 640, 2 * proj.size * 4, work),
        name="attention_backward",
        waits=waits,
    )(me, proj, starts, place, lse, cosine, sine, pad, *grads)


def out_kernel(spans, me_ref, w_ref, tokens_ref, gain_ref, *rest):
    mixed, (resid_ref, *parts) = rest[:spans], rest[spans:]
    summed = tokens_ref[...].astype(F32)
    for at in range(spans):
        summed += dot(mixed[at][...], w_ref[jnp.bitwise_xor(me_ref[0], at)], 1, 0)
    resid_ref[...] = summed
    factor = lax.rsqrt(jnp.mean(summed * summed, axis=-1, keepdims=True) + epsilon)
    normed = (summed * factor * gain_ref[...]).astype(BF16)
    columns = parts[0].shape[1]
    for at, part in enumerate(parts):
        part[...] = normed[:, at * columns : (at + 1) * columns]


def project_out(seq, me, mixed, w_out, tokens, gain, ways, waits=()):
    _, span, width = tokens.shape
    out_shape = [shape(span, width, dtype=F32)] + [shape(span, width // len(ways))] * len(ways)
    return call(
        functools.partial(out_kernel, len(mixed)),
        out_shape=out_shape,
        prefetch=1,
        in_specs=[
            whole(w_out),
            pl.BlockSpec((None, span, width), lambda *_: (seq, 0, 0)),
            whole(gain),
            *[whole(x) for x in mixed],
        ],
        out_specs=[whole(x) for x in out_shape],
        cost_estimate=cost(2 * span * width * width, span * width * 10 + width * width * 2),
        name="project_out",
        waits=waits,
    )(me, w_out, tokens, gain, *mixed)


def assemble(held, core, near_ref, far_ref):
    for chip in range(near_ref.shape[0]):
        held[2 * chip + core] = near_ref[chip]
        held[2 * chip + 1 - core] = far_ref[chip]


def feed_kernel(
    visits, bits, ways, shard_ref, both_ref, near_ref, far_ref, cn_ref, cf_ref, *rest
):
    count = 2 * len(ways)
    rows, (hid_ref, dboth_ref, x_ref, *outs), held = rest[:count], rest[count:-1], rest[-1]
    inner = both_ref.shape[1] // 2

    @pl.when(pl.program_id(0) == 0)
    def _():
        assemble(held, shard_ref[0] % 2, near_ref, far_ref)

    down = held[...].reshape(inner, held.shape[2])
    columns = rows[0].shape[1]
    for at, way in enumerate(ways):
        x_ref[:, at * columns : (at + 1) * columns] = visits.load(way, rows[2 * at], rows[2 * at + 1])
    x = x_ref[...]
    gate = dot(x, both_ref[:, :inner], 1, 0)
    up = dot(x, both_ref[:, inner:], 1, 0)
    sig = jax.nn.sigmoid(gate)
    act = gate * sig
    hid_ref[...] = (act * up).astype(BF16)
    grad_hidden = dot(visits.load(bits, cn_ref, cf_ref), down, 1, 1)
    dboth_ref[:, :inner] = (grad_hidden * up * (sig * (1.0 + gate * (1.0 - sig)))).astype(BF16)
    dboth_ref[:, inner:] = (grad_hidden * act).astype(BF16)
    visits.store_halves(ways, outs, dot(dboth_ref[...], both_ref[...], 1, 1).astype(BF16))


def pairs_of(values):
    return list(zip(values[::2], values[1::2]))


def feed_forward(spans, me_shard, rows, cots, bits, ways, both_w, near, far, waits=()):
    width, inner = both_w.shape[0], both_w.shape[1] // 2
    half = cots[0].shape[0]
    span = 2 * half // spans
    visits = Visits(spans, span)
    one = pl.Buffered(1)
    total = 2 * half
    part = width // len(ways)
    flat = [x for pair in rows for x in pair]
    hidden, grads, x_all, *parts = call(
        functools.partial(feed_kernel, visits, bits, ways),
        out_shape=[shape(total, inner), shape(total, 2 * inner), shape(total, width)]
        + [shape(half, part)] * 2 * len(ways),
        prefetch=1,
        grid=(spans,),
        in_specs=[
            whole(both_w, pipeline_mode=one),
            whole(near, pipeline_mode=one),
            whole(far, pipeline_mode=one),
            *visits.specs(bits, width),
            *[spec for way in ways for spec in visits.specs(way, part)],
        ],
        out_specs=[
            visits.rows(bits, inner),
            visits.rows(bits, 2 * inner),
            visits.rows(bits, width),
            *[spec for way in ways for spec in visits.specs(way, part)],
        ],
        scratch=[pltpu.VMEM((2 * near.shape[0], *near.shape[1:]), BF16)],
        cost_estimate=cost(
            10 * total * width * inner, total * (6 * width + 6 * inner) + 6 * width * inner
        ),
        name="feed_forward",
        waits=waits,
    )(me_shard, both_w, near, far, *cots, *flat)
    return pairs_of(parts), hidden, grads, x_all


def feed_out_kernel(count, walk, shard_ref, near_ref, far_ref, *rest):
    hidden, outs, held = rest[:count], rest[count:-1], rest[-1]

    @pl.when(pl.program_id(0) == 0)
    def _():
        assemble(held, shard_ref[0] % 2, near_ref, far_ref)

    down = held[...].reshape(-1, held.shape[2])
    for at in range(count):
        walk.store(outs[2 * at], outs[2 * at + 1], dot(hidden[at][...], down, 1, 0).astype(BF16))


def feed_out(spans, me_shard, hidden, near, far, waits=()):
    total, inner = hidden[0].shape
    width = near.shape[2]
    walk = Walk(spans, total // spans, False)
    count = len(hidden)
    return pairs_of(
        call(
            functools.partial(feed_out_kernel, count, walk),
            out_shape=[shape(total // 2, width)] * 2 * count,
            prefetch=1,
            grid=(spans,),
            in_specs=[
                whole(near, pipeline_mode=pl.Buffered(1)),
                whole(far, pipeline_mode=pl.Buffered(1)),
                *[pl.BlockSpec((total // spans, inner), walk.both)] * count,
            ],
            out_specs=walk.specs(width) * count,
            scratch=[pltpu.VMEM((2 * near.shape[0], *near.shape[1:]), BF16)],
            cost_estimate=cost(
                2 * count * total * inner * width,
                2 * count * total * (inner + width) + 2 * inner * width,
            ),
            name="feed_out",
            waits=waits,
        )(me_shard, near, far, *hidden)
    )


def terms_of(*refs):
    sums = [a[...].astype(F32) + b[...].astype(F32) for a, b in zip(refs[::2], refs[1::2])]
    return sums[0] if len(sums) == 1 else jnp.concatenate(sums, axis=1)


def back_kernel(count, me_ref, resid_ref, cot_ref, gain_ref, w_ref, *rest):
    terms, (resid_grad_ref, branch_ref, *mixed) = rest[:count], rest[count:]
    rows = resid_ref[...]
    factor = lax.rsqrt(jnp.mean(rows * rows, axis=-1, keepdims=True) + epsilon)
    unit_rows = rows * factor
    scaled = terms_of(*terms) * gain_ref[...]
    mean_dot = jnp.mean(scaled * unit_rows, axis=-1, keepdims=True)
    grad = cot_ref[...].astype(F32) + factor * (scaled - unit_rows * mean_dot)
    resid_grad_ref[...] = grad
    branch = grad.astype(BF16)
    branch_ref[...] = branch
    for at, out in enumerate(mixed):
        out[...] = dot(branch, w_ref[jnp.bitwise_xor(me_ref[0], at)], 1, 1).astype(BF16)


def norm_out_back(seq, me, spans, parts, resid, cot, gain, w_out, waits=()):
    rows, width = resid.shape
    terms = [x for pair in parts for x in pair]
    out_shape = [shape(rows, width, dtype=F32), shape(rows, width)]
    out_shape += [shape(rows, w_out.shape[1])] * spans
    out = call(
        functools.partial(back_kernel, len(terms)),
        out_shape=out_shape,
        prefetch=1,
        in_specs=[whole(resid), pl.BlockSpec((None, rows, width), lambda *_: (seq, 0, 0))]
        + [whole(x) for x in (gain, w_out, *terms)],
        out_specs=[whole(x) for x in out_shape],
        cost_estimate=cost(2 * rows * width * width, rows * width * 16 + width * width * 2),
        name="norm_out_back",
        waits=waits,
    )(me, resid, cot, gain, w_out, *terms)
    return out[0], out[1], out[2:]


def grad_in_kernel(visits, ways, proj_ref, w_ref, *outs):
    visits.store_halves(ways, outs, dot(proj_ref[...], w_ref[...], 1, 1).astype(BF16))


def grad_into_rows(spans, proj_grad, bits, ways, w_in, waits=()):
    full, narrow = proj_grad.shape
    width = w_in.shape[0]
    visits = Visits(spans, full // spans)
    part = width // len(ways)
    parts = call(
        functools.partial(grad_in_kernel, visits, ways),
        out_shape=[shape(full // 2, part)] * 2 * len(ways),
        grid=(spans,),
        in_specs=[visits.rows(bits, narrow), whole(w_in, pipeline_mode=pl.Buffered(1))],
        out_specs=[spec for way in ways for spec in visits.specs(way, part)],
        cost_estimate=cost(2 * full * narrow * width, 2 * full * (narrow + width) + 2 * narrow * width),
        name="grad_into_rows",
        waits=waits,
    )(proj_grad, w_in)
    return pairs_of(parts)


def product_of(lefts, rights):
    total = None
    i = j = a = b = 0
    while i < len(lefts):
        size = min(lefts[i].shape[0] - a, rights[j].shape[0] - b)
        term = dot(lefts[i][a : a + size, :], rights[j][b : b + size, :], 0, 0)
        total = term if total is None else total + term
        a, b = a + size, b + size
        if a == lefts[i].shape[0]:
            i, a = i + 1, 0
        if b == rights[j].shape[0]:
            j, b = j + 1, 0
    return total


def row_sums(product):
    sums = jnp.sum(product, axis=1, keepdims=True)
    return jnp.broadcast_to(sums, (product.shape[0], LANES)).T[:8]


def weight_kernel(left_count, right_count, gain, *refs):
    lefts, rights = refs[:left_count], refs[left_count : left_count + right_count]
    rest = refs[left_count + right_count :]
    total = product_of(lefts, rights)
    if gain:
        w_ref, out_ref, gain_ref = rest
        gain_ref[...] = row_sums(total * w_ref[...].astype(F32))
    else:
        (out_ref,) = rest
    out_ref[...] = total.astype(BF16)


def weight_grad(lefts, rights, weight, name, waits=()):
    rows = lefts[0].shape[1]
    tile = 256
    columns = rights[0].shape[1]
    depth = sum(x.shape[0] for x in lefts)
    out_shape = [shape(rows, columns)]
    out_specs = [pl.BlockSpec((tile, columns), lambda i: (i, 0))]
    weights = () if weight is None else (weight,)
    if weights:
        out_shape.append(shape(8, rows, dtype=F32))
        out_specs.append(pl.BlockSpec((8, tile), lambda i: (0, i)))
    return call(
        functools.partial(weight_kernel, len(lefts), len(rights), bool(weights)),
        out_shape=out_shape,
        grid=(rows // tile,),
        in_specs=[pl.BlockSpec((x.shape[0], tile), lambda i: (0, i)) for x in lefts]
        + [whole(x, pipeline_mode=pl.Buffered(1)) for x in rights]
        + [pl.BlockSpec((tile, x.shape[1]), lambda i: (i, 0)) for x in weights],
        out_specs=out_specs,
        cost_estimate=cost(
            2 * depth * rows * columns, 2 * depth * (rows + columns) + 2 * rows * columns
        ),
        name=name,
        waits=waits,
    )(*lefts, *rights, *weights)


def in_weight_kernel(own, shards, left_count, me_ref, *refs):
    lefts, (*rights, w_ref, other_ref, near_ref, far_ref, gain_ref) = refs[:left_count], refs[left_count:]
    total = product_of(lefts, rights)
    gain = row_sums(total * w_ref[...].astype(F32))
    first = lax.broadcasted_iota(jnp.int32, gain.shape, 0) < 4
    gain_ref[...] = jnp.where(first, gain, other_ref[...])
    total = total.astype(BF16)
    steps = shards.bit_length() - 1
    count = total.shape[0] // own
    for at in range(count):
        apart = jnp.bitwise_xor(me_ref[0], pl.program_id(0) * count + at)
        where = 0
        for bit in range(steps):
            where = where * 2 + (apart >> bit) % 2
        piece = total[at * own : (at + 1) * own]

        @pl.when(where < shards // 2)
        def _():
            near_ref[where] = piece

        @pl.when(where >= shards // 2)
        def _():
            far_ref[where - shards // 2] = piece


def in_weight_grad(me, lefts, rights, weight, other_gain, own, shards, waits=()):
    rows, columns = weight.shape
    tile = math.lcm(own, LANES)
    depth = sum(x.shape[0] for x in lefts)
    half = shape(shards // 2, own, columns)
    out_shape = (half, half, shape(8, rows, dtype=F32))
    return call(
        functools.partial(in_weight_kernel, own, shards, len(lefts)),
        out_shape=out_shape,
        prefetch=1,
        grid=(rows // tile,),
        in_specs=[pl.BlockSpec((x.shape[0], tile), lambda i, _: (0, i)) for x in lefts]
        + [whole(x) for x in rights]
        + [pl.BlockSpec((tile, columns), lambda i, _: (i, 0)), pl.BlockSpec((8, tile), lambda i, _: (0, i))],
        out_specs=[whole(half), whole(half), pl.BlockSpec((8, tile), lambda i, _: (0, i))],
        cost_estimate=cost(
            2 * depth * rows * columns, 2 * depth * (rows + columns) + 2 * rows * columns
        ),
        name="in_weight_grad",
        waits=waits,
    )(me, *lefts, *rights, weight, other_gain)


def add_pairs(left, right):
    return (left.astype(F32) + right.astype(F32)).astype(BF16)


def halve_kernel(near_ref, got_ref, gain_ref, gain_got_ref, *rest):
    outs, gain_out = rest[:-1], rest[-1]
    total = (near_ref[...].astype(F32) + got_ref[...].astype(F32)).astype(BF16)
    cut = total.shape[0] // len(outs)
    for at, out in enumerate(outs):
        out[...] = total[at * cut : (at + 1) * cut]
    gain_out[...] = gain_ref[...] + gain_got_ref[...]


def halve(near, got, gain, gain_got, waits=()):
    parts = 2 if near.shape[0] > 1 else 1
    out_shape = [shape(near.shape[0] // parts, *near.shape[1:])] * parts + [gain]
    return call(
        halve_kernel,
        out_shape=[shape(*x.shape, dtype=x.dtype) for x in out_shape],
        in_specs=[whole(x) for x in (near, got, gain, gain_got)],
        out_specs=[whole(x) for x in out_shape],
        cost_estimate=cost(0, 6 * near.size),
        name="halve",
        waits=waits,
    )(near, got, gain, gain_got)


def across(value, bit):
    size = lax.axis_size("fsdp")
    return lax.ppermute(value, "fsdp", [(i, i ^ bit) for i in range(size)])


def arrange_kernel(copies, every_ref, *outs):
    for own in range(every_ref.shape[0]):
        for source, out, target, size in copies:
            begin = target(own)
            outs[out][:, begin : begin + size] = every_ref[own, :, source : source + size].astype(F32)


def arrange_halves_kernel(order, copies, me_ref, *rest):
    blocks, (out_ref, held) = rest[:-2], rest[-2:]
    for at, owner in enumerate(order):
        held[jnp.bitwise_xor(me_ref[0], owner)] = blocks[at][...]
    arrange_kernel(copies, held, out_ref)


def arrange_halves(me, near, far, bits, copies, width, name):
    order = order_of(bits)
    count = len(order) // 2
    rows, columns = near.shape[0] // count, near.shape[1]
    tile = rows // 2
    out_shape = shape(rows, width, dtype=F32)

    def block(at):
        return pl.BlockSpec((tile, columns), lambda i, _: (2 * at + i, 0))

    return call(
        functools.partial(arrange_halves_kernel, order, copies),
        out_shape=out_shape,
        prefetch=1,
        grid=(2,),
        in_specs=[block(at) for _ in range(2) for at in range(count)],
        out_specs=pl.BlockSpec((tile, width), lambda i, _: (i, 0)),
        scratch=[pltpu.VMEM((len(order), tile, columns), BF16)],
        cost_estimate=cost(0, 6 * rows * width),
        name=name,
    )(me, *[near] * count, *[far] * count)


def arrange_blocks_kernel(order, copies, me_ref, *rest):
    blocks, outs, held = rest[: len(order)], rest[len(order) : -1], rest[-1]
    for at, owner in enumerate(order):
        held[jnp.bitwise_xor(me_ref[0], owner)] = blocks[at][...]
    arrange_kernel(copies, held, *outs)


def arrange_blocks(me, blocks, bits, copies, widths, name):
    rows, columns = blocks[0].shape
    tile = rows // 2
    order = order_of(bits)
    out_shape = [shape(rows, width, dtype=F32) for width in widths]
    return call(
        functools.partial(arrange_blocks_kernel, order, copies),
        out_shape=out_shape,
        prefetch=1,
        grid=(2,),
        in_specs=[pl.BlockSpec((tile, columns), lambda i, _: (i, 0))] * len(blocks),
        out_specs=[pl.BlockSpec((tile, width), lambda i, _: (i, 0)) for width in widths],
        scratch=[pltpu.VMEM((len(blocks), tile, columns), BF16)],
        cost_estimate=cost(0, 6 * rows * sum(widths)),
        name=name,
    )(me, *blocks)


def widen_rows_kernel(every_ref, out_ref):
    out_ref[...] = every_ref[...].astype(F32)


def to_float(value, name, waits=()):
    rows, width = value.shape
    tile = rows // 4 if rows % 64 == 0 else rows
    spec = pl.BlockSpec((tile, width), lambda i: (i, 0))
    return call(
        widen_rows_kernel,
        out_shape=shape(rows, width, dtype=F32),
        grid=(rows // tile,),
        in_specs=[spec],
        out_specs=spec,
        cost_estimate=cost(0, 6 * value.size),
        name=name,
        waits=waits,
    )(value)


def add_kernel(left_ref, right_ref, out_ref):
    out_ref[...] = left_ref[...].astype(F32) + right_ref[...].astype(F32)


def add_float(left, right):
    rows, width = left.shape
    tile = rows // 2
    spec = pl.BlockSpec((tile, width), lambda i: (i, 0))
    return call(
        add_kernel,
        out_shape=shape(rows, width, dtype=F32),
        grid=(2,),
        in_specs=[spec, spec],
        out_specs=spec,
        cost_estimate=cost(0, 8 * left.size),
        name="add_float",
    )(left, right)


def gains_kernel(left_ref, right_ref, first_norm, second_norm, first_ref, second_ref):
    total = left_ref[...] + right_ref[...]
    first_ref[...] = (total[0:1] / first_norm[...])[0]
    second_ref[...] = (total[4:5] / second_norm[...])[0]


def finish_gains(left, right, first_norm, second_norm):
    out_shape = [shape(left.shape[1], dtype=F32)] * 2
    return call(
        gains_kernel,
        out_shape=out_shape,
        in_specs=[whole(x) for x in (left, right, first_norm, second_norm)],
        out_specs=[whole(x) for x in out_shape],
        cost_estimate=cost(0, 8 * left.size),
        name="finish_gains",
    )(left, right, first_norm, second_norm)


def block_out_kernel(count, seqs, *refs):
    out_ref = refs[-1]
    for seq in range(seqs):
        resid_ref, *terms = refs[count * seq : count * (seq + 1)]
        out_ref[seq] = (resid_ref[...] + terms_of(*terms)).astype(BF16)


def finish_block_out(resid, terms, waits=()):
    rows, width = resid[0].shape
    out_shape = shape(len(resid), rows, width)
    flat = [y for q in range(len(resid)) for y in (resid[q], *[x for pair in terms[q] for x in pair])]
    count = len(flat) // len(resid)
    return call(
        functools.partial(block_out_kernel, count, len(resid)),
        out_shape=out_shape,
        in_specs=[whole(x) for x in flat],
        out_specs=whole(out_shape),
        cost_estimate=cost(0, 12 * out_shape.size),
        name="finish_block_out",
        waits=waits,
    )(*flat)


def tokens_grad_kernel(count, seqs, tokens_ref, gain_ref, *refs):
    out_ref = refs[-1]
    for seq in range(seqs):
        resid_ref, *terms = refs[count * seq : count * (seq + 1)]
        rows = tokens_ref[seq].astype(F32)
        factor = lax.rsqrt(jnp.mean(rows * rows, axis=-1, keepdims=True) + epsilon)
        unit_rows = rows * factor
        scaled = terms_of(*terms) * gain_ref[...]
        mean_dot = jnp.mean(scaled * unit_rows, axis=-1, keepdims=True)
        out_ref[seq] = (resid_ref[...] + factor * (scaled - unit_rows * mean_dot)).astype(BF16)


def finish_tokens_grad(tokens, gain, grad_resid, terms, waits=()):
    out_shape = shape(*tokens.shape)
    flat = [
        y for q in range(len(grad_resid)) for y in (grad_resid[q], *[x for pair in terms[q] for x in pair])
    ]
    count = len(flat) // len(grad_resid)
    return call(
        functools.partial(tokens_grad_kernel, count, len(grad_resid)),
        out_shape=out_shape,
        in_specs=[whole(x) for x in (tokens, gain, *flat)],
        out_specs=whole(out_shape),
        cost_estimate=cost(0, 12 * out_shape.size),
        name="finish_tokens_grad",
        waits=waits,
    )(tokens, gain, *flat)


def join_kernel(chips, me_ref, *refs):
    blocks, out_ref = refs[:-1], refs[-1]
    chip = me_ref[0] // 2
    for back in range(chips):
        out_ref[lax.rem(chip - back + chips, chips)] = blocks[back][...]


def join(me, blocks, waits=()):
    rows, width = blocks[0].shape
    out_shape = shape(len(blocks), rows, width)
    return call(
        functools.partial(join_kernel, len(blocks)),
        out_shape=out_shape,
        prefetch=1,
        in_specs=[whole(x) for x in blocks],
        out_specs=whole(out_shape),
        cost_estimate=cost(0, 4 * out_shape.size),
        name="join",
        waits=waits,
    )(me, *blocks)


def out_weight_kernel(spans, seqs, me_ref, *refs):
    mixed, branches, out_ref = refs[: spans * seqs], refs[spans * seqs : -1], refs[-1]
    for at in range(spans):
        total = None
        for seq in range(seqs):
            term = dot(mixed[seq * spans + at][...], branches[seq][...], 0, 0)
            total = term if total is None else total + term
        out_ref[jnp.bitwise_xor(me_ref[0], at)] = total.astype(BF16)


def out_weight_grad(me, mixed, branches, waits=()):
    flat = [x for group in mixed for x in group]
    narrow, width = flat[0].shape[1], branches[0].shape[1]
    out_shape = shape(len(mixed[0]), narrow, width)
    return call(
        functools.partial(out_weight_kernel, len(mixed[0]), len(branches)),
        out_shape=out_shape,
        prefetch=1,
        in_specs=[whole(x) for x in (*flat, *branches)],
        out_specs=whole(out_shape),
        cost_estimate=cost(2 * len(flat) * flat[0].size * width, 2 * len(mixed[0]) * narrow * width),
        name="out_weight_grad",
        waits=waits,
    )(me, *flat, *branches)


def turning_tables(positions):
    frequency = jnp.exp(
        jnp.arange(HALF, dtype=F32) * (-2.0 * math.log(rope_base) / HEAD_DIMENSION)
    )
    angles = positions.astype(F32)[:, :, None] * frequency
    cosine, sine = jnp.cos(angles), jnp.sin(angles)
    empty = jnp.zeros((*positions.shape, 64 - HALF), F32)
    return (
        jnp.concatenate([cosine, empty, cosine, empty], axis=-1),
        jnp.concatenate([-sine, empty, sine, empty], axis=-1),
    )


def body(
    tokens,
    joined_input_weight,
    out_projection,
    gate_weight,
    up_weight,
    down_weight,
    norm_first,
    norm_second,
    positions,
    cotangent,
):
    seqs, span, width = tokens.shape
    spans = lax.axis_size("seq")
    shards = lax.axis_size("fsdp")
    chips = shards // 2
    me = jnp.full((1,), lax.axis_index("seq"), jnp.int32)
    me_shard = jnp.full((1,), lax.axis_index("fsdp"), jnp.int32)
    full = positions.shape[1]
    pairs = KEY_VALUE_HEADS // spans
    repeat = QUERY_HEAD_COUNT // KEY_VALUE_HEADS
    unit = repeat + 2
    query_columns = QUERY_HEAD_COUNT * HEAD_DIMENSION
    pair_columns = KEY_VALUE_HEADS * HEAD_DIMENSION
    query_slab = query_columns // spans
    pair_slab = pair_columns // spans
    own_rows = joined_input_weight.shape[0]
    piece = FF // (shards * spans)
    inner = shards * piece
    step = min(256, full)
    pad = jnp.asarray(pad_matrix(pairs, repeat), BF16)
    place = jnp.asarray(place_matrix(pairs, repeat), BF16)
    gain_in, gain_mid = norm_first[None, :], norm_second[None, :]
    upward = tuple(range(spans.bit_length() - 1))
    orders = [(upward[::-1], upward)[q % 2] for q in range(seqs)]
    both = range(seqs)
    del CHAIN[:]

    def gather(shard):
        return lax.all_gather(shard, "fsdp", axis=0, tiled=True)

    def owned(value):
        return lax.psum_scatter(value, "fsdp", scatter_dimension=0, tiled=True)

    ways = (upward[::-1], upward)

    def flat(pairs):
        return tuple(x for pair in pairs for x in pair)

    def copied(value, bits):
        held = [value]
        for bit in bits:
            held = held + [swap(x, bit) for x in held]
        return held

    in_shard = cut_in(me, joined_input_weight, spans, (query_slab, pair_slab, pair_slab))
    w_in = gather(in_shard)
    w_out = gather(out_projection).reshape(spans, query_slab, width)
    cot_rows = split_rows(cotangent)
    cot_got = gather_start(cot_rows, orders)
    normed = norm_rows(tokens, gain_in)
    x_got = gather_start(normed, orders)
    both_shard, down_shard = cut_feed(
        me, gate_weight, up_weight, down_weight, spans, shards, piece, ()
    )
    w_both = gather(both_shard)
    down_blocks = [down_shard, around(down_shard)]

    def pass_on():
        if len(down_blocks) < chips:
            down_blocks[-1:] = pin(down_blocks[-1])
            down_blocks.append(around(down_blocks[-1]))

    cosine, sine = turning_tables(positions)
    starts = (jnp.arange(full, dtype=jnp.int32)[None, :] - positions)[:, None, :]
    x_in = gather_end(normed, x_got, orders, "stack_in")
    pass_on()
    w_wide = widen(w_in, pad)
    pass_on()

    projected, mixed, lse, resid, x_mid = [], [], [], [], []

    def project_rows(q, waits=()):
        rows, *normed_mid = project_out(q, me, mixed[q], w_out, tokens, gain_mid, ways, waits)
        resid.append(rows)
        return normed_mid, gather_start(normed_mid, ways)

    for q in both:
        projected.append(
            project_in(
                me, x_in[q], orders[q], w_wide, cosine[q], sine[q], unit, x_in[-1] if q == 0 else ()
            )
        )
        if q == 0:
            cots = gather_end(cot_rows, cot_got, orders, "stack_cot")
            pass_on()
        if q == 1:
            started = [project_rows(0)]
        heads, sums = attention_forward(me, projected[q], starts[q], place, spans, repeat, step)
        lse.append(sums)
        mixed.append(shared(heads))
        if q == 0:
            while len(down_blocks) < chips:
                pass_on()
            down_near = join(me_shard, down_blocks)
            down_far = beside(down_near)
    x_mid.append(gather_end(*started[0], ways, "stack_mid"))
    for q in both[1:]:
        started.append(project_rows(q, (down_far, *flat(cots))))
    for q in both[1:]:
        x_mid.append(gather_end(*started[q], ways, "stack_mid"))

    hidden, grad_both, grad_mid, x_all = [], [], [], []
    for q in both:
        parts, kept, grads, rows = feed_forward(
            spans, me_shard, x_mid[q], cots[q], orders[q], ways, w_both, down_near, down_far
        )
        hidden.append(kept)
        grad_both.append(grads)
        x_all.append(rows)
        grad_mid.append(scatter_start(parts, ways))

    grad_resid, branches, head_grads = [], [], []

    def norm_back(q, waits=()):
        rows, branch, heads = norm_out_back(
            q, me, spans, grad_mid[q], resid[q], cotangent, gain_mid, w_out, waits
        )
        grad_resid.append(rows)
        branches.append(branch)
        head_grads.append(shared(heads))

    grad_mid[0] = scatter_end(*grad_mid[0], ways)
    both_part, gain_second = weight_grad(x_all, grad_both, w_both, "gate_up_grad")
    both_own = owned(both_part)
    norm_back(0)
    for q in both[1:]:
        grad_mid[q] = scatter_end(*grad_mid[q], ways)
    outs = scatter_start(
        feed_out(spans, me_shard, hidden, down_near, down_far, tuple(head_grads[0][1:])), orders
    )
    for q in both[1:]:
        norm_back(q)
    (down_part,) = weight_grad(hidden, flat(cots), None, "down_grad")
    down_own = owned(down_part)
    out_part = out_weight_grad(me, mixed, branches).reshape(query_columns, width)
    out_own = owned(out_part)

    proj_grads, grad_in = [], []
    for q in both:
        proj_grads.append(
            attention_backward(
                me,
                projected[q],
                starts[q],
                place,
                head_grads[q],
                orders[q],
                lse[q],
                cosine[q],
                sine[q],
                pad,
                repeat,
                step,
            )
        )
        if q == 0:
            outs = scatter_end(*outs, orders)
            both_every = copied(both_own, ways[0])
        if q == seqs - 1:
            for p in both[:-1]:
                grad_in[p] = scatter_end(*grad_in[p], ways)
            in_near, in_far, in_gain = in_weight_grad(
                me_shard,
                flat(x_in),
                proj_grads,
                w_in,
                gain_second,
                own_rows,
                shards,
                (*flat(outs), both_every[1]),
            )
            in_got, gain_got = across(in_far, 1), across(in_gain, 1)
        waits = tuple(x for group in head_grads[1:] for x in group[1:]) if q == 0 else flat(grad_in[0])
        parts = grad_into_rows(spans, proj_grads[q], orders[q], ways, w_in, waits)
        grad_in.append(scatter_start(parts, ways))
    (down_own,) = pin(down_own)
    down_every = lax.all_gather(down_own, "seq", axis=0, tiled=True)
    in_near, in_sent, in_gain = halve(in_near, in_got, in_gain, gain_got, tuple(both_every))
    in_got, gain_got = across(in_sent, 2), across(in_gain, 2)
    copies = [
        (part * inner + shard * piece, part, lambda own, shard=shard: (shard * spans + own) * piece, piece)
        for part in range(2)
        for shard in range(shards)
    ]
    sums = [out_own]

    def out_start(bit):
        sums[:] = pin(*sums)
        total = sums[0] if len(sums) == 1 else add_pairs(*sums)
        sums[:] = [total, swap(total, bit)]

    out_start(0)
    block_out = finish_block_out(resid, [[pair] for pair in outs])
    grad_in[-1] = scatter_end(*grad_in[-1], ways)
    bit = 4
    while in_near.shape[0] > 1:
        in_near, in_sent, in_gain = halve(in_near, in_got, in_gain, gain_got)
        in_got, gain_got = across(in_sent, bit), across(in_gain, bit)
        bit *= 2
    in_own, in_gain = halve(in_near, in_got, in_gain, gain_got)
    in_every = [in_own[0]]
    out_start(1)
    for bit in upward:
        got = [swap(x, bit) for x in in_every]
        gain_got = swap(in_gain, bit)
        if bit == 0:
            tokens_grad = finish_tokens_grad(tokens, gain_in, grad_resid, grad_in)
        if bit + 1 < len(upward):
            *got, gain_got = pin(*got, gain_got)
        in_every = in_every + got
        if bit + 1 < len(upward):
            in_gain = in_gain + gain_got
    for bit in upward[2:]:
        out_start(bit)
    out_grad = add_float(*sums)
    gate_grad, up_grad = arrange_blocks(me, both_every, ways[0], copies, (FF, FF), "arrange_gate_up")
    down_grad = to_float(down_every, "down_to_float")
    copies = [
        (0, 0, lambda own: own * query_slab, query_slab),
        (query_slab, 0, lambda own: query_columns + own * pair_slab, pair_slab),
        (
            query_slab + pair_slab,
            0,
            lambda own: query_columns + pair_columns + own * pair_slab,
            pair_slab,
        ),
    ]
    (in_grad,) = arrange_blocks(
        me,
        in_every,
        upward,
        copies,
        (query_columns + 2 * pair_columns,),
        "arrange_in",
    )
    first_gain, second_gain = finish_gains(in_gain, gain_got, gain_in, gain_mid)
    return (
        block_out,
        tokens_grad,
        in_grad,
        out_grad,
        gate_grad,
        up_grad,
        down_grad,
        first_gain,
        second_gain,
    )


def solution(mesh):
    return jax.shard_map(
        body,
        mesh=mesh,
        in_specs=(
            P("fsdp", "seq", None),
            P("fsdp", None),
            P("fsdp", None),
            P("fsdp", None),
            P("fsdp", None),
            P("fsdp", None),
            P(),
            P(),
            P("fsdp", None),
            P("fsdp", "seq", None),
        ),
        out_specs=(
            P("fsdp", "seq", None),
            P("fsdp", "seq", None),
            P("fsdp", None),
            P("fsdp", None),
            P("fsdp", None),
            P("fsdp", None),
            P("fsdp", None),
            P(),
            P(),
        ),
        check_vma=False,
    )
```
